512 devices in a mesh: dp: 256 (over z, y, x), ctx: 2 (over core).
Axes of the slice: x: 4, y: 8, z: 8, core: 2. Of those that a mesh axis runs over, the one named last changes fastest.
Arguments:
- head_inputs: float32 [512, 131072], P('ctx', 'dp'), may hold values from -30 to 30
- gate_inputs: float32 [512, 131072], P('ctx', 'dp'), may hold values from -6 to 6
- step_raw: float32 [2048, 512], P('dp', 'ctx'), may hold values from -4 to 4
- b_rows: float32 [16384, 512], P('dp', 'ctx'), may hold values from -6 to 6
- c_rows: float32 [16384, 512], P('dp', 'ctx'), may hold values from -0.125 to 0.125
- decay_log: float32 [2048], P('dp'), may hold values from -12 to -2
- step_bias: float32 [2048], P('dp'), may hold values from -1 to 1
- skip_gain: float32 [2048], P('dp'), may hold values from 0.5 to 1.5
- norm_gain: float32 [131072], P('dp'), may hold values from 0.1 to 1.9
- out_grad: float32 [512, 131072], P('ctx', 'dp'), may hold values from -16 to 16
Outputs:
- output: float32 [512, 131072], P('ctx', 'dp')
- head_grad: float32 [512, 131072], P('ctx', 'dp')
- gate_grad: float32 [512, 131072], P('ctx', 'dp')
- step_grad: float32 [2048, 512], P('dp', 'ctx')
- b_grad: float32 [16384, 512], P('dp', 'ctx')
- c_grad: float32 [16384, 512], P('dp', 'ctx')
- decay_grad: float32 [2048], P('dp')
- bias_grad: float32 [2048], P('dp')
- skip_grad: float32 [2048], P('dp')
- gain_grad: float32 [131072], P('dp')
The draws below stay inside these ranges and needn't reach their ends.
All inputs are finite; a program needn't handle non-finite values.
Results may differ from the reference program's by a relative error of at most 0.0003.
Values sent between devices are 32-bit elements; how exact they have to be, the bound alone decides.
A program may use at most 64 MiB of HBM per device.

```python
import math
import jax
import jax.numpy as jnp
from jax import lax

P_SIZE = 64
N = 256
HEAD_DEV = 8
GROUP_DEVS = 4
Q = 128
HEADS = 2048
GROUPS = 64
SEQ = 512


def draw_head_inputs(key, part):
    key = jax.random.fold_in(key, 11)
    key_base, key_head = jax.random.split(key, 2)
    per_group = HEAD_DEV * GROUP_DEVS
    position = (jnp.arange(HEADS) % per_group).astype(jnp.float32) / max(per_group - 1, 1)
    head_scale = jnp.exp(math.log(3.0) * position) * jnp.exp(jax.random.uniform(key_head, (HEADS,), jnp.float32, -0.35, 0.35))
    base = jnp.clip(jax.random.normal(key_base, (SEQ, HEADS, P_SIZE), jnp.float32), -5.0, 5.0)
    return (base * head_scale[None, :, None]).reshape(SEQ, HEADS * P_SIZE)


def draw_decay_log(key, part):
    key = jax.random.fold_in(key, 12)
    key_pick, key_slow, key_fast = jax.random.split(key, 3)
    share = 0.5
    slow = jax.random.uniform(key_pick, (HEADS,), jnp.float32) < share
    slow_rate = jnp.exp(jax.random.uniform(key_slow, (HEADS,), jnp.float32, math.log(0.3), 0.0)) / SEQ
    fast_rate = jnp.exp(jax.random.uniform(key_fast, (HEADS,), jnp.float32, math.log(0.03), math.log(0.06)))
    return jnp.log(jnp.where(slow, slow_rate, fast_rate))


def draw_step_raw(key, part):
    key = jax.random.fold_in(key, 13)
    key_noise, key_offset = jax.random.split(key, 2)
    noise = jnp.clip(0.5 * jax.random.normal(key_noise, (HEADS, SEQ), jnp.float32), -2.5, 2.5)
    offsets = jax.random.uniform(key_offset, (HEADS, SEQ // Q), jnp.float32, -1.0, 1.0)
    return noise + jnp.repeat(offsets, Q, axis=1)


def draw_out_grad(key, part):
    key = jax.random.fold_in(key, 14)
    key_base = jax.random.fold_in(key, 0)
    ramp = jnp.exp(math.log(3.0) * jnp.arange(SEQ).astype(jnp.float32) / max(SEQ - 1, 1))
    base = jnp.clip(jax.random.normal(key_base, (SEQ, HEADS * P_SIZE), jnp.float32), -5.0, 5.0)
    return base * ramp[:, None]


def levels(rng, shape, cuts, smallest, high):
    factor_of, own = 1.0, jax.random.fold_in(rng, 6)
    for dim, parts in cuts:
        steps = jnp.exp(jax.random.uniform(jax.random.fold_in(own, dim), (parts,), jnp.float32, smallest / len(cuts), high / len(cuts)))
        factor_of = factor_of * jnp.repeat(steps, shape[dim] // parts).reshape([-1 if axis == dim else 1 for axis in range(len(shape))])
    return factor_of


def scatter_about(own_key, shape, width, bound, shards=(), held_as=jnp.bfloat16):
    values = jax.random.normal(own_key, shape, jnp.float32) * width
    if len(shards) > 0:
        values = levels(own_key, shape, shards, -0.22, 0.18) * values
    return jnp.clip(values, min=-bound, max=bound).astype(held_as)


def setup_inputs(seed: int = 0) -> dict:
    streams_of = jax.random.split(jax.random.key(seed), 11)
    return {
        "head_inputs": draw_head_inputs(jax.random.fold_in(streams_of[10], 71), 0),
        "gate_inputs": scatter_about(streams_of[1], (SEQ, HEADS * P_SIZE), 1.0, 6.0, ((0, 2), (1, 256)), jnp.float32),
        "step_raw": draw_step_raw(jax.random.fold_in(streams_of[10], 71), 0),
        "b_rows": scatter_about(streams_of[3], (GROUPS * N, SEQ), 1.0, 6.0, ((0, 256), (1, 2)), jnp.float32),
        "c_rows": scatter_about(streams_of[4], (GROUPS * N, SEQ), (N * SEQ // 64) ** -0.5, 0.125, ((0, 256), (1, 2)), jnp.float32),
        "decay_log": draw_decay_log(jax.random.fold_in(streams_of[10], 71), 0),
        "step_bias": jnp.clip(jax.random.uniform(streams_of[6], (HEADS,), jnp.float32, -1.0, 1.0) * levels(streams_of[6], (HEADS,), ((0, 256),), -0.4, 0.0), -1.0, 1.0),
        "skip_gain": jnp.clip(0.5 + 1.0 * jax.random.uniform(streams_of[7], (HEADS,), jnp.float32) ** levels(streams_of[7], (HEADS,), ((0, 256),), -0.2, 0.2), 0.5, 1.5),
        "norm_gain": jnp.clip(1.0 + 0.18 * jax.random.normal(streams_of[8], (HEADS * P_SIZE,), jnp.float32), 0.1, 1.9),
        "out_grad": draw_out_grad(jax.random.fold_in(streams_of[10], 71), 0),
    }


HIGH = lax.Precision.HIGHEST
EPSILON = 1e-05

def stretch_scan(head_x, step_size, log_rate, b_group, c_group, state_init):
    length = head_x.shape[0]
    group_count = head_x.shape[1]
    per_group = head_x.shape[2]
    head_size = head_x.shape[3]
    blocks = length // Q
    x_blocks = head_x.reshape(blocks, Q, group_count, per_group, head_size)

    def to_blocks(array):
        return jnp.moveaxis(array.reshape(array.shape[:-1] + (blocks, Q)), -2, 0)
    positions = jnp.arange(Q)
    lower = positions[:, None] >= positions[None, :]

    def advance(state, block):
        x_part, step_part, rate_part, b_part, c_part = block
        running = jnp.cumsum(rate_part, axis=-1)
        gaps = running[..., :, None] - running[..., None, :]
        decay_mat = jnp.where(lower, jnp.exp(jnp.minimum(gaps, 0.0)), 0.0)
        scores = jnp.einsum('gni,gnj->gij', c_part, b_part, precision=HIGH)
        mixing = decay_mat * scores[:, None]
        scaled_x = x_part * jnp.transpose(step_part, (2, 0, 1))[..., None]
        inner = jnp.einsum('ghij,jghp->ighp', mixing, scaled_x, precision=HIGH)
        carried = jnp.einsum('gni,ghpn->ighp', c_part, state, precision=HIGH)
        carried = carried * jnp.transpose(jnp.exp(running), (2, 0, 1))[..., None]
        tail_decay = jnp.exp(running[..., -1:] - running)
        weighted_x = scaled_x * jnp.transpose(tail_decay, (2, 0, 1))[..., None]
        state_next = jnp.exp(running[..., -1])[..., None, None] * state
        state_next = state_next + jnp.einsum('gnj,jghp->ghpn', b_part, weighted_x, precision=HIGH)
        return (state_next, inner + carried)
    state_end, outputs = lax.scan(advance, state_init, (x_blocks, to_blocks(step_size), to_blocks(log_rate), to_blocks(b_group), to_blocks(c_group)))
    return (outputs.reshape(length, group_count, per_group, head_size), state_end)

def layer(head_inputs, gate_inputs, step_raw, b_rows, c_rows, decay_log, step_bias, skip_gain, norm_gain):
    seq_len = head_inputs.shape[0]
    head_count = decay_log.shape[0]
    group_count = b_rows.shape[0] // N
    per_group = head_count // group_count
    step_size = jax.nn.softplus(step_raw + step_bias[:, None])
    log_rate = -jnp.exp(decay_log)[:, None] * step_size
    head_x = head_inputs.reshape(seq_len, group_count, per_group, P_SIZE)
    state_init = jnp.zeros((group_count, per_group, P_SIZE, N), jnp.float32)
    mixed, state_end = stretch_scan(head_x, step_size.reshape(group_count, per_group, seq_len), log_rate.reshape(group_count, per_group, seq_len), b_rows.reshape(group_count, N, seq_len), c_rows.reshape(group_count, N, seq_len), state_init)
    mixed = mixed + skip_gain.reshape(group_count, per_group, 1) * head_x
    gated = mixed.reshape(seq_len, head_count * P_SIZE) * jax.nn.silu(gate_inputs)
    grouped = gated.reshape(seq_len, group_count, per_group * P_SIZE)
    inverse = lax.rsqrt(lax.optimization_barrier(jnp.mean(grouped * grouped, axis=-1, keepdims=True)) + EPSILON)
    return (grouped * inverse).reshape(seq_len, head_count * P_SIZE) * norm_gain

def reference(head_inputs, gate_inputs, step_raw, b_rows, c_rows, decay_log, step_bias, skip_gain, norm_gain, out_grad):
    output, pullback = jax.vjp(layer, head_inputs, gate_inputs, step_raw, b_rows, c_rows, decay_log, step_bias, skip_gain, norm_gain)
    grads = pullback(out_grad)
    return (output, grads[0], grads[1], grads[2], grads[3], grads[4], grads[5], grads[6], grads[7], grads[8])
```

```python
import jax
import jax.numpy as jnp
from jax import lax
from jax.experimental import pallas as pl
from jax.experimental.pallas import tpu as pltpu
from jax.sharding import PartitionSpec as P

MESH = pl.DeviceIdType.MESH
F32 = jnp.float32
BF = jnp.bfloat16
T = 256
Q = 128
N = 256
D = 512
H = 8
W = 64
ROWS = 16
TILES = T // ROWS
GROUP_WIDTH = 2048
EPSILON = 1e-05

NN = (((1,), (0,)), ((), ()))
NT = (((1,), (1,)), ((), ()))


def halves(v):
    hi = v.astype(BF)
    return hi, (v - hi.astype(F32)).astype(BF)


def dot(a, b, dims=NN):
    return lax.dot_general(a, b, dims, preferred_element_type=F32)


def dot3(a, b, dims=NN):
    return dot(a[0], b[0], dims) + (dot(a[0], b[1], dims) + dot(a[1], b[0], dims))


def thirds(v):
    hi = v.astype(BF).astype(F32)
    mid = (v - hi).astype(BF).astype(F32)
    return jnp.concatenate([hi, mid, v - hi - mid, jnp.zeros_like(v)], axis=0)


def sum_thirds(v):
    return v[0:8] + (v[8:16] + v[16:24])


def lanes(v):
    return (v[:, 0:128] + v[:, 128:256]) + (v[:, 256:384] + v[:, 384:512])


def fold(v):
    return v[0:8] + v[8:16]


def tiles(step, count=TILES, init=None):
    def run(i, carry):
        return step(pl.ds(pl.multiple_of(i * ROWS, ROWS), ROWS), carry)

    return lax.fori_loop(0, count, run, 0 if init is None else init)


def iota(shape, dim):
    return lax.broadcasted_iota(jnp.int32, shape, dim)


def body(
    x_in, z_in, raw_in, b_in, c_in, decay_s, bias_s, skip_s, gain_in, og_in,
    out_o, hg_o, zg_o, sg_o, bg_o, cg_o, decay_o, bias_o, skip_o, gain_o,
    xv, zv, ogv, rawv, gainv, bv, cv,
    a1, a2, a5, gate, dgate, ogg, vh, vl, kh, kl, ph, pld,
    bh, bl, ch, cl, cth, ctl, bth, btl, gh, gl, gth, gtl,
    state, other, yi, yv, gated, qh, ql, norm, cols, dy, uh, ul, sh, sl, rh, rl,
    dv, dx, first, second, recv_a, recv_b, small, outv, hgv, zgv, sgv,
    local_sem, send_sem, recv_sem,
):
    dp = lax.axis_index("dp")
    ctx = lax.axis_index("ctx")
    place = lax.rem(dp, 4)
    base = dp - place
    right = base + lax.rem(place + 1, 4)
    left = base + lax.rem(place + 3, 4)
    across = base + lax.rem(place + 2, 4)
    early = ctx == 0
    late = ctx == 1

    used = []

    def local(src, dst):
        copy = pltpu.make_async_copy(src, dst, local_sem.at[len(used)])
        used.append(copy)
        return copy

    sent = []

    def remote(src, dst, device):
        k = len(sent)
        sent.append(k)
        return pltpu.make_async_remote_copy(
            src_ref=src, dst_ref=dst, send_sem=send_sem.at[k], recv_sem=recv_sem.at[k],
            device_id=device, device_id_type=MESH,
        )

    to_right, to_left, to_across, to_core = (right, ctx), (left, ctx), (across, ctx), (dp, 1 - ctx)

    barrier = pltpu.get_barrier_semaphore()
    for device in (to_right, to_left, to_across, to_core):
        pl.semaphore_signal(barrier, inc=1, device_id=device, device_id_type=MESH)

    get_raw = local(raw_in, rawv)
    get_gain = local(gain_in, gainv.at[0])
    get_x = local(x_in, xv)
    get_z = local(z_in, zv)
    get_og = local(og_in, ogv)
    get_b = local(b_in, bv.at[pl.ds(0, W)])
    get_c = local(c_in, cv.at[pl.ds(0, W)])
    for copy in used:
        copy.start()
    pl.semaphore_wait(barrier, 4)

    b_right = remote(b_in, bv.at[pl.ds(W, W)], to_right)
    b_left = remote(b_in, bv.at[pl.ds(2 * W, W)], to_left)
    c_right = remote(c_in, cv.at[pl.ds(W, W)], to_right)
    c_left = remote(c_in, cv.at[pl.ds(2 * W, W)], to_left)
    half = W // 2
    b_on_right = remote(bv.at[pl.ds(W, half)], bv.at[pl.ds(3 * W, half)], to_right)
    b_on_left = remote(bv.at[pl.ds(2 * W + half, half)], bv.at[pl.ds(3 * W + half, half)], to_left)
    c_on_right = remote(cv.at[pl.ds(W, half)], cv.at[pl.ds(3 * W, half)], to_right)
    c_on_left = remote(cv.at[pl.ds(2 * W + half, half)], cv.at[pl.ds(3 * W + half, half)], to_left)
    for copy in (b_right, b_left, c_right, c_left):
        copy.start()

    def per_head(ref, width):
        row = iota((H, width), 0)
        value = jnp.full((H, width), ref[0], F32)
        for h in range(1, H):
            value = jnp.where(row == h, ref[h], value)
        return value

    get_raw.wait()
    speed = jnp.exp(per_head(decay_s, T))
    pre = rawv[...] + per_head(bias_s, T)
    step = jnp.maximum(pre, 0.0) + jnp.log1p(jnp.exp(-jnp.abs(pre)))
    rate = -speed * step
    src, dst = iota((T, T), 0), iota((T, T), 1)
    upto = jnp.where((src <= dst) & (src // Q == dst // Q), 1.0, 0.0).astype(BF)
    run = sum_thirds(dot(thirds(rate).astype(BF), upto))
    total0 = run[:, Q - 1:Q]
    total1 = run[:, T - 1:T]
    position = iota((H, T), 1)
    block1 = position >= Q
    centre = 0.5 * jnp.where(block1, total1, total0)
    scale1 = jnp.exp(run - centre)
    scale2 = step * jnp.exp(centre - run)
    since_start = jnp.where(block1, run + total0, run)
    to_end = jnp.where(block1, total1 - run, total0 - run + total1)
    scale5 = jnp.where(early, step, 1.0) * jnp.exp(jnp.where(early, to_end, since_start))
    stacked = jnp.concatenate(
        [thirds(scale1), thirds(scale2), thirds(scale5), jnp.zeros((32, T), F32)], axis=0
    ).T.astype(BF)
    row, col = iota((128, D), 0), iota((128, D), 1)
    same = (row % 8 == col // W) & (row % 32 < 24)
    for k, ref in enumerate((a1, a2, a5)):
        spread = jnp.where(same & (row // 32 == k), 1.0, 0.0).astype(BF)
        ref[...] = dot(stacked, spread)
    own = iota((H, D), 0) == iota((H, D), 1) // W
    kappa = jnp.sum(
        jnp.where(own, jnp.exp(0.5 * (total0 + total1)), 0.0), axis=0, keepdims=True
    )
    skip_row = jnp.sum(jnp.where(own, per_head(skip_s, D), 0.0), axis=0, keepdims=True)

    get_gain.wait()
    get_x.wait()
    get_z.wait()
    get_og.wait()

    def prepare(r, carry):
        z = zv[r]
        sig = 1.0 / (1.0 + jnp.exp(-z))
        gate[r] = z * sig
        dgate[r] = sig * (1.0 + z * (1.0 - sig))
        ogg[r] = ogv[r] * gainv[...]
        x = xv[r]
        vh[r], vl[r] = halves(a2[r] * x)
        ph[r], pld[r] = halves(a5[r] * x)
        return carry

    tiles(prepare)

    def prepare0(r, carry):
        kh[r], kl[r] = halves((a2[r] * xv[r]) * kappa)
        return carry

    tiles(prepare0, TILES // 2)

    b_right.wait_recv()
    b_on_right.start()
    b_left.wait_recv()
    b_on_left.start()
    c_right.wait_recv()
    c_on_right.start()
    c_left.wait_recv()
    c_on_left.start()
    get_b.wait()
    get_c.wait()
    b_on_right.wait_recv()
    b_on_left.wait_recv()
    bh[...], bl[...] = halves(bv[...])

    state_out = [remote(state.at[k], other.at[k], to_core) for k in range(2)]

    @pl.when(early)
    def _():
        for k in range(2):
            part = pl.ds(k * 256, 256)
            state[k] = dot3((bh[...], bl[...]), (ph[:, part], pld[:, part]))
            state_out[k].start()

    c_on_right.wait_recv()
    c_on_left.wait_recv()
    cth[...], ctl[...] = halves(cv[...].T)
    ch[...], cl[...] = halves(cv[...])

    low = src >= dst
    g0 = dot3((cth[0:Q], ctl[0:Q]), (bh[:, 0:Q], bl[:, 0:Q]))
    g1 = dot3((cth[Q:T], ctl[Q:T]), (bh[...], bl[...]))
    g0 = jnp.where(low[0:Q, 0:Q], g0, 0.0)
    g1 = jnp.where(low[Q:T], g1, 0.0)
    gh[0:Q, 0:Q], gl[0:Q, 0:Q] = halves(g0)
    gh[Q:T], gl[Q:T] = halves(g1)
    gth[0:Q, 0:Q], gtl[0:Q, 0:Q] = halves(g0.T)
    gth[:, Q:T], gtl[:, Q:T] = halves(g1.T)
    for k in range(2):
        part = pl.ds(k * 256, 256)
        yi[0:Q, part] = dot3((gh[0:Q, 0:Q], gl[0:Q, 0:Q]), (vh[0:Q, part], vl[0:Q, part]))
        yi[Q:T, part] = dot3(
            (gh[Q:T], gl[Q:T]),
            (
                jnp.concatenate([kh[:, part], vh[Q:T, part]], axis=0),
                jnp.concatenate([kl[:, part], vl[Q:T, part]], axis=0),
            ),
        )

    def mix(r, y):
        yv[r] = y
        mixed = y + skip_row * xv[r]
        g = mixed * gate[r]
        gated[r] = g
        qh[r, 0:128], ql[r, 0:128] = halves(lanes(g * g))
        qh[r, 128:256], ql[r, 128:256] = halves(lanes(g * ogg[r]))

    @pl.when(early)
    def _():
        def go(r, carry):
            mix(r, a1[r] * yi[r])
            return carry

        tiles(go)
        bth[...], btl[...] = halves(bv[...].T)

    @pl.when(late)
    def _():
        for k in range(2):
            state_out[k].wait_recv()
            sh[k], sl[k] = halves(other[k])
            dx[:, pl.ds(k * 256, 256)] = dot3((cth[...], ctl[...]), (sh[k], sl[k]))

        def go(r, carry):
            mix(r, a1[r] * yi[r] + a5[r] * dx[r])
            return carry

        tiles(go)

    pick = jnp.where(iota((H, 256), 0) == iota((H, 256), 1) // 128, 1.0, 0.0).astype(BF)
    norm[0] = dot(pick, qh[:, 0:256], NT) + dot(pick, ql[:, 0:256], NT)
    norm_out = [
        remote(norm.at[0], norm.at[1 + k], device)
        for k, device in enumerate((to_right, to_left, to_across))
    ]
    for copy in norm_out:
        copy.start()
    for copy in norm_out:
        copy.wait_recv()
    sums = (norm[0] + norm[1]) + (norm[2] + norm[3])
    inverse = lax.rsqrt(sums[0:1] * (1.0 / GROUP_WIDTH) + EPSILON)
    slope = inverse * inverse * inverse * sums[1:2] * (1.0 / GROUP_WIDTH)
    lead = iota((128, T), 0)
    cols[...] = jnp.where(lead == 0, inverse, jnp.where(lead == 1, slope, 0.0)).T

    def finish(r, carry):
        gain_sum, skip_sum = carry
        inv = cols[r, 0:1]
        k = cols[r, 1:2]
        g = gated[r]
        x = xv[r]
        y = yv[r]
        normed = g * inv
        outv[r] = normed * gainv[...]
        grad = ogg[r] * inv - g * k
        zgv[r] = grad * (y + skip_row * x) * dgate[r]
        d = grad * gate[r]
        dy[r] = d
        uh[r], ul[r] = halves(a1[r] * d)
        qh[r], ql[r] = halves(d * y)
        return gain_sum + fold(ogv[r] * normed), skip_sum + fold(d * x)

    zero = jnp.zeros((8, D), F32)
    gain_sum, skip_sum = tiles(finish, init=(zero, zero))
    put_out = local(outv, out_o)
    put_zg = local(zgv, zg_o)
    put_out.start()
    put_zg.start()

    start_out = [remote(state.at[k], other.at[k], to_core) for k in range(2)]

    @pl.when(late)
    def _():
        def go(r, carry):
            ph[r], pld[r] = halves(a5[r] * dy[r])
            return carry

        tiles(go)
        for k in range(2):
            part = pl.ds(k * 256, 256)
            state[k] = dot3((ch[...], cl[...]), (ph[:, part], pld[:, part]))
            start_out[k].start()

    d0 = dot3((uh[0:Q], ul[0:Q]), (vh[0:Q], vl[0:Q]), NT)
    d10 = dot3((uh[Q:T], ul[Q:T]), (kh[...], kl[...]), NT)
    d11 = dot3((uh[Q:T], ul[Q:T]), (vh[Q:T], vl[Q:T]), NT)
    diagonal = low[0:Q, 0:Q]
    gh[0:Q, 0:Q], gl[0:Q, 0:Q] = halves(jnp.where(diagonal, d0, 0.0))
    gh[0:Q, Q:T] = jnp.zeros((Q, Q), BF)
    gl[0:Q, Q:T] = jnp.zeros((Q, Q), BF)
    gh[Q:T, 0:Q], gl[Q:T, 0:Q] = halves(d10)
    gh[Q:T, Q:T], gl[Q:T, Q:T] = halves(jnp.where(diagonal, d11, 0.0))

    def c_part():
        return dot3((bh[...], bl[...]), (gh[...], gl[...]), NT)

    def b_part():
        return dot3((ch[...], cl[...]), (gh[...], gl[...]))

    def scatter(full, landing):
        far_right = remote(full.at[pl.ds(3 * W, half)], landing.at[pl.ds(0, half)], to_right)
        far_left = remote(full.at[pl.ds(3 * W + half, half)], landing.at[pl.ds(half, half)], to_left)
        near_right = remote(full.at[pl.ds(2 * W + half, half)], landing.at[pl.ds(W + half, half)], to_right)
        near_left = remote(full.at[pl.ds(W, half)], landing.at[pl.ds(2 * W, half)], to_left)
        sum_right = remote(full.at[pl.ds(2 * W, half)], landing.at[pl.ds(W, half)], to_right)
        sum_left = remote(full.at[pl.ds(W + half, half)], landing.at[pl.ds(2 * W + half, half)], to_left)

        def start():
            for copy in (far_right, far_left, near_right, near_left):
                copy.start()

        def relay():
            far_right.wait_recv()
            full[pl.ds(2 * W, half)] += landing[pl.ds(0, half)]
            sum_right.start()
            far_left.wait_recv()
            full[pl.ds(W + half, half)] += landing[pl.ds(half, half)]
            sum_left.start()

        def end():
            for copy in (near_right, near_left, sum_right, sum_left):
                copy.wait_recv()
            full[0:W] += landing[W:2 * W] + landing[2 * W:3 * W]
            for copy in (far_right, far_left, near_right, near_left, sum_right, sum_left):
                copy.wait_send()

        return start, relay, end

    first_start, first_relay, first_end = scatter(first, recv_a)
    second_start, second_relay, second_end = scatter(second, recv_b)

    @pl.when(early)
    def _():
        first[...] = c_part()
        first_start()
        second[...] = b_part()

    @pl.when(late)
    def _():
        first[...] = b_part()
        first_start()
        second[...] = c_part() + (
            dot3((sh[0], sl[0]), (ph[:, 0:256], pld[:, 0:256]), NT)
            + dot3((sh[1], sl[1]), (ph[:, 256:512], pld[:, 256:512]), NT)
        )
        second_start()

    for k in range(2):
        part = pl.ds(k * 256, 256)
        dv[0:Q, part] = dot3((gth[0:Q, 0:Q], gtl[0:Q, 0:Q]), (uh[0:Q, part], ul[0:Q, part])) + kappa[
            :, k * 256:(k + 1) * 256
        ] * dot3((gth[0:Q, Q:T], gtl[0:Q, Q:T]), (uh[Q:T, part], ul[Q:T, part]))
        dv[Q:T, part] = dot3((gth[Q:T, Q:T], gtl[Q:T, Q:T]), (uh[Q:T, part], ul[Q:T, part]))

    first_relay()

    @pl.when(early)
    def _():
        for k in range(2):
            start_out[k].wait_recv()
            rh[k], rl[k] = halves(other[k])
        second[...] += dot3((rh[0], rl[0]), (ph[:, 0:256], pld[:, 0:256]), NT) + dot3(
            (rh[1], rl[1]), (ph[:, 256:512], pld[:, 256:512]), NT
        )
        second_start()
        for k in range(2):
            dx[:, pl.ds(k * 256, 256)] = dot3((bth[...], btl[...]), (rh[k], rl[k]))

    def gather_x(r, f):
        hgv[r] = f + skip_row * dy[r]
        sxh, sxl = halves(f * xv[r])
        uh[r] = sxh
        ul[r] = sxl

    small[0:16] = jnp.zeros((16, D), F32)

    @pl.when(early)
    def _():
        def go(r, carry):
            gather_x(r, a2[r] * dv[r] + a5[r] * dx[r])
            return carry

        tiles(go)
        sums = []
        for k in range(2):
            sums.append(tiles(
                lambda r, acc, k=k: acc + fold(state[k, r] * other[k, r]),
                init=jnp.zeros((8, 256), F32),
            ))
        small[8:16] = jnp.concatenate(sums, axis=1)

    @pl.when(late)
    def _():
        def go(r, carry):
            gather_x(r, a2[r] * dv[r])
            return carry

        tiles(go)

    put_hg = local(hgv, hg_o)
    put_hg.start()
    second_relay()

    heads = jnp.where(own, 1.0, 0.0).astype(BF)
    y_sum = dot(heads, qh[...], NT) + dot(heads, ql[...], NT)
    x_sum = dot(heads, uh[...], NT) + dot(heads, ul[...], NT)
    from_end = jnp.sum(
        jnp.where(own, jnp.sum(small[8:16], axis=0, keepdims=True), 0.0), axis=1, keepdims=True
    )
    onward = jnp.where(low, 1.0, 0.0).astype(BF)
    rate_grad = sum_thirds(dot(thirds(y_sum - x_sum).astype(BF), onward)) + from_end
    step_grad = (x_sum / step - speed * rate_grad) * (1.0 / (1.0 + jnp.exp(-pre)))
    sgv[...] = step_grad
    put_sg = local(sgv, sg_o)
    put_sg.start()

    def as_row(column):
        hit = iota((H, D), 0) == iota((H, D), 1)
        return jnp.sum(jnp.where(hit, column, 0.0), axis=0, keepdims=True)

    skip_column = jnp.sum(
        jnp.where(own, jnp.sum(skip_sum, axis=0, keepdims=True), 0.0), axis=1, keepdims=True
    )
    small[0:1] = jnp.sum(gain_sum, axis=0, keepdims=True)
    small[1:2] = as_row(jnp.sum(rate_grad * rate, axis=1, keepdims=True))
    small[2:3] = as_row(jnp.sum(step_grad, axis=1, keepdims=True))
    small[3:4] = as_row(skip_column)
    small_out = remote(small.at[pl.ds(0, 8)], small.at[pl.ds(16, 8)], to_core)
    small_out.start()
    first_end()

    put_first = [local(first.at[pl.ds(0, W)], o) for o in (cg_o, bg_o)]
    put_second = [local(second.at[pl.ds(0, W)], o) for o in (bg_o, cg_o)]

    @pl.when(early)
    def _():
        put_first[0].start()

    @pl.when(late)
    def _():
        put_first[1].start()

    small_out.wait()
    small[24:32] = small[0:8] + small[16:24]
    put_small = [local(small.at[24, pl.ds(0, D)], gain_o)]
    for k, ref in enumerate((decay_o, bias_o, skip_o)):
        ref[...] = small[25 + k, 0:H]
    for copy in put_small:
        copy.start()
    second_end()

    @pl.when(early)
    def _():
        put_second[0].start()
        put_first[0].wait()
        put_second[0].wait()
        for k in range(2):
            state_out[k].wait_send()

    @pl.when(late)
    def _():
        put_second[1].start()
        put_first[1].wait()
        put_second[1].wait()
        for k in range(2):
            start_out[k].wait_send()

    for copy in [put_out, put_zg, put_hg, put_sg] + put_small:
        copy.wait()
    for copy in [b_right, b_left, c_right, c_left, b_on_right, b_on_left, c_on_right, c_on_left] + norm_out:
        copy.wait_send()


def shards(*args):
    def f32(*shape):
        return jax.ShapeDtypeStruct(shape, F32)

    def vm(*shape):
        return pltpu.VMEM(shape, F32)

    def vb(*shape):
        return pltpu.VMEM(shape, BF)

    anywhere = pl.BlockSpec(memory_space=pl.ANY)
    scalars = pl.BlockSpec(memory_space=pltpu.SMEM)
    scratch = [
        vm(T, D), vm(T, D), vm(T, D), vm(H, T), vm(1, D), vm(N, T), vm(N, T),
        vm(T, D), vm(T, D), vm(T, D), vm(T, D), vm(T, D), vm(T, D),
        vb(T, D), vb(T, D), vb(Q, D), vb(Q, D), vb(T, D), vb(T, D),
        vb(N, T), vb(N, T), vb(N, T), vb(N, T), vb(T, N), vb(T, N), vb(T, N), vb(T, N),
        vb(T, T), vb(T, T), vb(T, T), vb(T, T),
        vm(2, N, 256), vm(2, N, 256), vm(T, D), vm(T, D), vm(T, D), vb(T, D), vb(T, D),
        vm(4, 8, T), vm(T, 128), vm(T, D), vb(T, D), vb(T, D),
        vb(2, N, 256), vb(2, N, 256), vb(2, N, 256), vb(2, N, 256),
        vm(T, D), vm(T, D), vm(N, T), vm(N, T), vm(3 * W, T), vm(3 * W, T), vm(32, D),
        vm(T, D), vm(T, D), vm(T, D), vm(H, T),
        pltpu.SemaphoreType.DMA((24,)),
        pltpu.SemaphoreType.DMA((28,)),
        pltpu.SemaphoreType.DMA((28,)),
    ]
    return pl.pallas_call(
        body,
        out_shape=[
            f32(T, D), f32(T, D), f32(T, D), f32(H, T), f32(W, T), f32(W, T),
            f32(H), f32(H), f32(H), f32(D),
        ],
        in_specs=[anywhere] * 5 + [scalars] * 3 + [anywhere] * 2,
        out_specs=[anywhere] * 6 + [pl.BlockSpec(memory_space=pltpu.VMEM)] * 3 + [anywhere],
        scratch_shapes=scratch,
        compiler_params=pltpu.CompilerParams(
            collective_id=0, has_side_effects=True, vmem_limit_bytes=48 * 1024 * 1024
        ),
        name="layer",
    )(*args)


def solution(mesh):
    rows, cols = P("ctx", "dp"), P("dp", "ctx")
    heads = P("dp")
    return jax.shard_map(
        shards,
        mesh=mesh,
        in_specs=(rows, rows, cols, cols, cols, heads, heads, heads, heads, rows),
        out_specs=(rows, rows, rows, cols, cols, cols, heads, heads, heads, heads),
        check_vma=False,
    )
```

```python
import jax
import jax.numpy as jnp
from jax import lax
from jax.experimental import pallas as pl
from jax.experimental.pallas import tpu as pltpu
from jax.sharding import PartitionSpec as P

MESH = pl.DeviceIdType.MESH
F32 = jnp.float32
BF = jnp.bfloat16
T = 256
Q = 128
N = 256
D = 512
H = 8
W = 64
ROWS = 16
TILES = T // ROWS
GROUP_WIDTH = 2048
EPSILON = 1e-05

NN = (((1,), (0,)), ((), ()))
NT = (((1,), (1,)), ((), ()))


def halves(v):
    hi = v.astype(BF)
    return hi, (v - hi.astype(F32)).astype(BF)


def dot(a, b, dims=NN):
    return lax.dot_general(a, b, dims, preferred_element_type=F32)


def dot3(a, b, dims=NN):
    return dot(a[0], b[0], dims) + (dot(a[0], b[1], dims) + dot(a[1], b[0], dims))


def thirds(v):
    hi = v.astype(BF).astype(F32)
    mid = (v - hi).astype(BF).astype(F32)
    return jnp.concatenate([hi, mid, v - hi - mid, jnp.zeros_like(v)], axis=0)


def sum_thirds(v):
    return v[0:8] + (v[8:16] + v[16:24])


def lanes(v):
    return (v[:, 0:128] + v[:, 128:256]) + (v[:, 256:384] + v[:, 384:512])


def fold(v):
    return v[0:8] + v[8:16]


def tiles(step, count=TILES, init=None):
    def run(i, carry):
        return step(pl.ds(pl.multiple_of(i * ROWS, ROWS), ROWS), carry)

    return lax.fori_loop(0, count, run, 0 if init is None else init)


def iota(shape, dim):
    return lax.broadcasted_iota(jnp.int32, shape, dim)


def body(
    x_in, z_in, raw_in, b_in, c_in, decay_in, bias_in, skip_in, gain_in, og_in,
    out_o, hg_o, zg_o, sg_o, bg_o, cg_o, params_o,
    xv, zv, ogv, rawv, gainv, decay_s, bias_s, skip_s, bv, cv,
    a1, a2, a5, gate, dgate, ogg, vh, vl, kh, kl, ph, pld,
    bh, bl, ch, cl, cth, ctl, bth, btl, gh, gl, gth, gtl,
    state, other, yi, yv, gated, qh, ql, norm, cols, dy, uh, ul, sh, sl, rh, rl,
    dv, dx, first, second, recv_a, recv_b, small, outv, hgv, zgv, sgv,
    local_sem, send_sem, recv_sem,
):
    dp = lax.axis_index("dp")
    ctx = lax.axis_index("ctx")
    place = lax.rem(dp, 4)
    base = dp - place
    right = base + lax.rem(place + 1, 4)
    left = base + lax.rem(place + 3, 4)
    across = base + lax.rem(place + 2, 4)
    early = ctx == 0
    late = ctx == 1

    used = []

    def local(src, dst):
        copy = pltpu.make_async_copy(src, dst, local_sem.at[len(used)])
        used.append(copy)
        return copy

    sent = []

    def remote(src, dst, device):
        k = len(sent)
        sent.append(k)
        return pltpu.make_async_remote_copy(
            src_ref=src, dst_ref=dst, send_sem=send_sem.at[k], recv_sem=recv_sem.at[k],
            device_id=device, device_id_type=MESH,
        )

    to_right, to_left, to_across, to_core = (right, ctx), (left, ctx), (across, ctx), (dp, 1 - ctx)

    barrier = pltpu.get_barrier_semaphore()
    for device in (to_right, to_left, to_across, to_core):
        pl.semaphore_signal(barrier, inc=1, device_id=device, device_id_type=MESH)

    get_heads = [
        local(ref, row)
        for ref, row in ((decay_in, decay_s), (bias_in, bias_s), (skip_in, skip_s))
    ]
    get_raw = local(raw_in, rawv)
    get_gain = local(gain_in, gainv.at[0])
    get_x = local(x_in, xv)
    get_z = local(z_in, zv)
    get_og = local(og_in, ogv)
    get_b = local(b_in, bv.at[pl.ds(0, W)])
    get_c = local(c_in, cv.at[pl.ds(0, W)])
    for copy in used:
        copy.start()
    pl.semaphore_wait(barrier, 4)

    b_right = remote(b_in, bv.at[pl.ds(W, W)], to_right)
    b_left = remote(b_in, bv.at[pl.ds(2 * W, W)], to_left)
    c_right = remote(c_in, cv.at[pl.ds(W, W)], to_right)
    c_left = remote(c_in, cv.at[pl.ds(2 * W, W)], to_left)
    half = W // 2
    b_on_right = remote(bv.at[pl.ds(W, half)], bv.at[pl.ds(3 * W, half)], to_right)
    b_on_left = remote(bv.at[pl.ds(2 * W + half, half)], bv.at[pl.ds(3 * W + half, half)], to_left)
    c_on_right = remote(cv.at[pl.ds(W, half)], cv.at[pl.ds(3 * W, half)], to_right)
    c_on_left = remote(cv.at[pl.ds(2 * W + half, half)], cv.at[pl.ds(3 * W + half, half)], to_left)
    for copy in (b_right, b_left, c_right, c_left):
        copy.start()

    def per_head(ref, width):
        row = iota((H, width), 0)
        value = jnp.full((H, width), ref[0], F32)
        for h in range(1, H):
            value = jnp.where(row == h, ref[h], value)
        return value

    get_raw.wait()
    for copy in get_heads:
        copy.wait()
    speed = jnp.exp(per_head(decay_s, T))
    pre = rawv[...] + per_head(bias_s, T)
    step = jnp.maximum(pre, 0.0) + jnp.log1p(jnp.exp(-jnp.abs(pre)))
    rate = -speed * step
    src, dst = iota((T, T), 0), iota((T, T), 1)
    upto = jnp.where((src <= dst) & (src // Q == dst // Q), 1.0, 0.0).astype(BF)
    run = sum_thirds(dot(thirds(rate).astype(BF), upto))
    total0 = run[:, Q - 1:Q]
    total1 = run[:, T - 1:T]
    position = iota((H, T), 1)
    block1 = position >= Q
    centre = 0.5 * jnp.where(block1, total1, total0)
    scale1 = jnp.exp(run - centre)
    scale2 = step * jnp.exp(centre - run)
    since_start = jnp.where(block1, run + total0, run)
    to_end = jnp.where(block1, total1 - run, total0 - run + total1)
    scale5 = jnp.where(early, step, 1.0) * jnp.exp(jnp.where(early, to_end, since_start))
    stacked = jnp.concatenate(
        [thirds(scale1), thirds(scale2), thirds(scale5), jnp.zeros((32, T), F32)], axis=0
    ).T.astype(BF)
    row, col = iota((128, D), 0), iota((128, D), 1)
    same = (row % 8 == col // W) & (row % 32 < 24)
    for k, ref in enumerate((a1, a2, a5)):
        spread = jnp.where(same & (row // 32 == k), 1.0, 0.0).astype(BF)
        ref[...] = dot(stacked, spread)
    own = iota((H, D), 0) == iota((H, D), 1) // W
    kappa = jnp.sum(
        jnp.where(own, jnp.exp(0.5 * (total0 + total1)), 0.0), axis=0, keepdims=True
    )
    skip_row = jnp.sum(jnp.where(own, per_head(skip_s, D), 0.0), axis=0, keepdims=True)

    get_gain.wait()
    get_x.wait()
    get_z.wait()
    get_og.wait()

    def prepare(r, carry):
        z = zv[r]
        sig = 1.0 / (1.0 + jnp.exp(-z))
        gate[r] = z * sig
        dgate[r] = sig * (1.0 + z * (1.0 - sig))
        ogg[r] = ogv[r] * gainv[...]
        x = xv[r]
        vh[r], vl[r] = halves(a2[r] * x)
        ph[r], pld[r] = halves(a5[r] * x)
        return carry

    tiles(prepare)

    def prepare0(r, carry):
        kh[r], kl[r] = halves((a2[r] * xv[r]) * kappa)
        return carry

    tiles(prepare0, TILES // 2)

    b_right.wait_recv()
    b_on_right.start()
    b_left.wait_recv()
    b_on_left.start()
    c_right.wait_recv()
    c_on_right.start()
    c_left.wait_recv()
    c_on_left.start()
    get_b.wait()
    get_c.wait()
    b_on_right.wait_recv()
    b_on_left.wait_recv()
    bh[...], bl[...] = halves(bv[...])

    state_out = [remote(state.at[k], other.at[k], to_core) for k in range(2)]

    @pl.when(early)
    def _():
        for k in range(2):
            part = pl.ds(k * 256, 256)
            state[k] = dot3((bh[...], bl[...]), (ph[:, part], pld[:, part]))
            state_out[k].start()

    c_on_right.wait_recv()
    c_on_left.wait_recv()
    cth[...], ctl[...] = halves(cv[...].T)
    ch[...], cl[...] = halves(cv[...])

    low = src >= dst
    g0 = dot3((cth[0:Q], ctl[0:Q]), (bh[:, 0:Q], bl[:, 0:Q]))
    g1 = dot3((cth[Q:T], ctl[Q:T]), (bh[...], bl[...]))
    g0 = jnp.where(low[0:Q, 0:Q], g0, 0.0)
    g1 = jnp.where(low[Q:T], g1, 0.0)
    gh[0:Q, 0:Q], gl[0:Q, 0:Q] = halves(g0)
    gh[Q:T], gl[Q:T] = halves(g1)
    gth[0:Q, 0:Q], gtl[0:Q, 0:Q] = halves(g0.T)
    gth[:, Q:T], gtl[:, Q:T] = halves(g1.T)
    for k in range(2):
        part = pl.ds(k * 256, 256)
        yi[0:Q, part] = dot3((gh[0:Q, 0:Q], gl[0:Q, 0:Q]), (vh[0:Q, part], vl[0:Q, part]))
        yi[Q:T, part] = dot3(
            (gh[Q:T], gl[Q:T]),
            (
                jnp.concatenate([kh[:, part], vh[Q:T, part]], axis=0),
                jnp.concatenate([kl[:, part], vl[Q:T, part]], axis=0),
            ),
        )

    def mix(r, y):
        yv[r] = y
        mixed = y + skip_row * xv[r]
        g = mixed * gate[r]
        gated[r] = g
        qh[r, 0:128], ql[r, 0:128] = halves(lanes(g * g))
        qh[r, 128:256], ql[r, 128:256] = halves(lanes(g * ogg[r]))

    @pl.when(early)
    def _():
        def go(r, carry):
            mix(r, a1[r] * yi[r])
            return carry

        tiles(go)
        bth[...], btl[...] = halves(bv[...].T)

    @pl.when(late)
    def _():
        for k in range(2):
            state_out[k].wait_recv()
            sh[k], sl[k] = halves(other[k])
            dx[:, pl.ds(k * 256, 256)] = dot3((cth[...], ctl[...]), (sh[k], sl[k]))

        def go(r, carry):
            mix(r, a1[r] * yi[r] + a5[r] * dx[r])
            return carry

        tiles(go)

    pick = jnp.where(iota((H, 256), 0) == iota((H, 256), 1) // 128, 1.0, 0.0).astype(BF)
    norm[0] = dot(pick, qh[:, 0:256], NT) + dot(pick, ql[:, 0:256], NT)
    norm_out = [
        remote(norm.at[0], norm.at[1 + k], device)
        for k, device in enumerate((to_right, to_left, to_across))
    ]
    for copy in norm_out:
        copy.start()
    for copy in norm_out:
        copy.wait_recv()
    sums = (norm[0] + norm[1]) + (norm[2] + norm[3])
    inverse = lax.rsqrt(sums[0:1] * (1.0 / GROUP_WIDTH) + EPSILON)
    slope = inverse * inverse * inverse * sums[1:2] * (1.0 / GROUP_WIDTH)
    lead = iota((128, T), 0)
    cols[...] = jnp.where(lead == 0, inverse, jnp.where(lead == 1, slope, 0.0)).T

    def finish(r, carry):
        gain_sum, skip_sum = carry
        inv = cols[r, 0:1]
        k = cols[r, 1:2]
        g = gated[r]
        x = xv[r]
        y = yv[r]
        normed = g * inv
        outv[r] = normed * gainv[...]
        grad = ogg[r] * inv - g * k
        zgv[r] = grad * (y + skip_row * x) * dgate[r]
        d = grad * gate[r]
        dy[r] = d
        uh[r], ul[r] = halves(a1[r] * d)
        qh[r], ql[r] = halves(d * y)
        return gain_sum + fold(ogv[r] * normed), skip_sum + fold(d * x)

    zero = jnp.zeros((8, D), F32)
    gain_sum, skip_sum = tiles(finish, init=(zero, zero))

    put_out = local(outv, out_o)
    put_zg = local(zgv, zg_o)
    put_out.start()
    put_zg.start()

    start_out = [remote(state.at[k], other.at[k], to_core) for k in range(2)]

    @pl.when(late)
    def _():
        def go(r, carry):
            ph[r], pld[r] = halves(a5[r] * dy[r])
            return carry

        tiles(go)
        for k in range(2):
            part = pl.ds(k * 256, 256)
            state[k] = dot3((ch[...], cl[...]), (ph[:, part], pld[:, part]))
            start_out[k].start()

    d0 = dot3((uh[0:Q], ul[0:Q]), (vh[0:Q], vl[0:Q]), NT)
    d10 = dot3((uh[Q:T], ul[Q:T]), (kh[...], kl[...]), NT)
    d11 = dot3((uh[Q:T], ul[Q:T]), (vh[Q:T], vl[Q:T]), NT)
    diagonal = low[0:Q, 0:Q]
    gh[0:Q, 0:Q], gl[0:Q, 0:Q] = halves(jnp.where(diagonal, d0, 0.0))
    gh[0:Q, Q:T] = jnp.zeros((Q, Q), BF)
    gl[0:Q, Q:T] = jnp.zeros((Q, Q), BF)
    gh[Q:T, 0:Q], gl[Q:T, 0:Q] = halves(d10)
    gh[Q:T, Q:T], gl[Q:T, Q:T] = halves(jnp.where(diagonal, d11, 0.0))

    def c_part():
        return dot3((bh[...], bl[...]), (gh[...], gl[...]), NT)

    def b_part():
        return dot3((ch[...], cl[...]), (gh[...], gl[...]))

    def scatter(full, landing):
        far_right = remote(full.at[pl.ds(3 * W, half)], landing.at[pl.ds(0, half)], to_right)
        far_left = remote(full.at[pl.ds(3 * W + half, half)], landing.at[pl.ds(half, half)], to_left)
        near_right = remote(full.at[pl.ds(2 * W + half, half)], landing.at[pl.ds(W + half, half)], to_right)
        near_left = remote(full.at[pl.ds(W, half)], landing.at[pl.ds(2 * W, half)], to_left)
        sum_right = remote(full.at[pl.ds(2 * W, half)], landing.at[pl.ds(W, half)], to_right)
        sum_left = remote(full.at[pl.ds(W + half, half)], landing.at[pl.ds(2 * W + half, half)], to_left)

        def start():
            for copy in (far_right, far_left, near_right, near_left):
                copy.start()

        def relay():
            far_right.wait_recv()
            full[pl.ds(2 * W, half)] += landing[pl.ds(0, half)]
            sum_right.start()
            far_left.wait_recv()
            full[pl.ds(W + half, half)] += landing[pl.ds(half, half)]
            sum_left.start()

        def end():
            for copy in (near_right, near_left, sum_right, sum_left):
                copy.wait_recv()
            full[0:W] += landing[W:2 * W] + landing[2 * W:3 * W]
            for copy in (far_right, far_left, near_right, near_left, sum_right, sum_left):
                copy.wait_send()

        return start, relay, end

    first_start, first_relay, first_end = scatter(first, recv_a)
    second_start, second_relay, second_end = scatter(second, recv_b)

    @pl.when(early)
    def _():
        first[...] = c_part()
        first_start()
        second[...] = b_part()

    @pl.when(late)
    def _():
        first[...] = b_part()
        first_start()
        second[...] = c_part() + (
            dot3((sh[0], sl[0]), (ph[:, 0:256], pld[:, 0:256]), NT)
            + dot3((sh[1], sl[1]), (ph[:, 256:512], pld[:, 256:512]), NT)
        )
        second_start()

    for k in range(2):
        part = pl.ds(k * 256, 256)
        dv[0:Q, part] = dot3((gth[0:Q, 0:Q], gtl[0:Q, 0:Q]), (uh[0:Q, part], ul[0:Q, part])) + kappa[
            :, k * 256:(k + 1) * 256
        ] * dot3((gth[0:Q, Q:T], gtl[0:Q, Q:T]), (uh[Q:T, part], ul[Q:T, part]))
        dv[Q:T, part] = dot3((gth[Q:T, Q:T], gtl[Q:T, Q:T]), (uh[Q:T, part], ul[Q:T, part]))

    first_relay()

    @pl.when(early)
    def _():
        for k in range(2):
            start_out[k].wait_recv()
            rh[k], rl[k] = halves(other[k])
        second[...] += dot3((rh[0], rl[0]), (ph[:, 0:256], pld[:, 0:256]), NT) + dot3(
            (rh[1], rl[1]), (ph[:, 256:512], pld[:, 256:512]), NT
        )
        second_start()
        for k in range(2):
            dx[:, pl.ds(k * 256, 256)] = dot3((bth[...], btl[...]), (rh[k], rl[k]))

    def gather_x(r, f):
        hgv[r] = f + skip_row * dy[r]
        sxh, sxl = halves(f * xv[r])
        uh[r] = sxh
        ul[r] = sxl

    small[0:16] = jnp.zeros((16, D), F32)

    @pl.when(early)
    def _():
        def go(r, carry):
            gather_x(r, a2[r] * dv[r] + a5[r] * dx[r])
            return carry

        tiles(go)
        sums = []
        for k in range(2):
            sums.append(tiles(
                lambda r, acc, k=k: acc + fold(state[k, r] * other[k, r]),
                init=jnp.zeros((8, 256), F32),
            ))
        small[8:16] = jnp.concatenate(sums, axis=1)

    @pl.when(late)
    def _():
        def go(r, carry):
            gather_x(r, a2[r] * dv[r])
            return carry

        tiles(go)

    put_hg = local(hgv, hg_o)
    put_hg.start()
    second_relay()

    heads = jnp.where(own, 1.0, 0.0).astype(BF)
    y_sum = dot(heads, qh[...], NT) + dot(heads, ql[...], NT)
    x_sum = dot(heads, uh[...], NT) + dot(heads, ul[...], NT)
    from_end = jnp.sum(
        jnp.where(own, jnp.sum(small[8:16], axis=0, keepdims=True), 0.0), axis=1, keepdims=True
    )
    onward = jnp.where(low, 1.0, 0.0).astype(BF)
    rate_grad = sum_thirds(dot(thirds(y_sum - x_sum).astype(BF), onward)) + from_end
    step_grad = (x_sum / step - speed * rate_grad) * (1.0 / (1.0 + jnp.exp(-pre)))
    sgv[...] = step_grad
    put_sg = local(sgv, sg_o)
    put_sg.start()

    def as_row(column):
        hit = iota((H, D), 0) == iota((H, D), 1)
        return jnp.sum(jnp.where(hit, column, 0.0), axis=0, keepdims=True)

    skip_column = jnp.sum(
        jnp.where(own, jnp.sum(skip_sum, axis=0, keepdims=True), 0.0), axis=1, keepdims=True
    )
    small[0:1] = jnp.sum(gain_sum, axis=0, keepdims=True)
    small[1:2] = as_row(jnp.sum(rate_grad * rate, axis=1, keepdims=True))
    small[2:3] = as_row(jnp.sum(step_grad, axis=1, keepdims=True))
    small[3:4] = as_row(skip_column)
    small_out = remote(small.at[pl.ds(0, 8)], small.at[pl.ds(16, 8)], to_core)
    small_out.start()
    first_end()

    put_first = [local(first.at[pl.ds(0, W)], o) for o in (cg_o, bg_o)]
    put_second = [local(second.at[pl.ds(0, W)], o) for o in (bg_o, cg_o)]

    @pl.when(early)
    def _():
        put_first[0].start()

    @pl.when(late)
    def _():
        put_first[1].start()

    small_out.wait()
    small[24:32] = small[0:8] + small[16:24]
    put_params = local(small.at[pl.ds(24, 8)], params_o)
    put_params.start()
    second_end()

    @pl.when(early)
    def _():
        put_second[0].start()
        put_first[0].wait()
        put_second[0].wait()
        for k in range(2):
            state_out[k].wait_send()

    @pl.when(late)
    def _():
        put_second[1].start()
        put_first[1].wait()
        put_second[1].wait()
        for k in range(2):
            start_out[k].wait_send()

    for copy in (put_out, put_zg, put_hg, put_sg, put_params):
        copy.wait()
    for copy in [b_right, b_left, c_right, c_left, b_on_right, b_on_left, c_on_right, c_on_left] + norm_out:
        copy.wait_send()


def place_results(*refs):
    results, outputs, held, (get_sem, put_sem) = refs[:7], refs[7:17], refs[17:24], refs[24:]
    out_o, hg_o, zg_o, sg_o, bg_o, cg_o, decay_o, bias_o, skip_o, gain_o = outputs
    gets = [pltpu.make_async_copy(src, dst, get_sem.at[k]) for k, (src, dst) in enumerate(zip(results, held))]
    for copy in gets:
        copy.start()
    puts = []
    rows = held[6]
    for k, ref in enumerate((out_o, hg_o, zg_o, sg_o, bg_o, cg_o, gain_o)):
        gets[k].wait()
        copy = pltpu.make_async_copy(rows.at[0] if ref is gain_o else held[k], ref, put_sem.at[k])
        copy.start()
        puts.append(copy)
    for k, ref in enumerate((decay_o, bias_o, skip_o)):
        ref[...] = rows[1 + k, 0:H]
    for copy in puts:
        copy.wait()


def shards(*args):
    def f32(*shape):
        return jax.ShapeDtypeStruct(shape, F32)

    def vm(*shape):
        return pltpu.VMEM(shape, F32)

    def vb(*shape):
        return pltpu.VMEM(shape, BF)

    in_hbm = pl.BlockSpec(memory_space=pltpu.HBM)
    in_vmem = pl.BlockSpec(memory_space=pltpu.VMEM)
    scalars = pltpu.SMEM((H,), F32)
    scratch = [
        vm(T, D), vm(T, D), vm(T, D), vm(H, T), vm(1, D), scalars, scalars, scalars, vm(N, T), vm(N, T),
        vm(T, D), vm(T, D), vm(T, D), vm(T, D), vm(T, D), vm(T, D),
        vb(T, D), vb(T, D), vb(Q, D), vb(Q, D), vb(T, D), vb(T, D),
        vb(N, T), vb(N, T), vb(N, T), vb(N, T), vb(T, N), vb(T, N), vb(T, N), vb(T, N),
        vb(T, T), vb(T, T), vb(T, T), vb(T, T),
        vm(2, N, 256), vm(2, N, 256), vm(T, D), vm(T, D), vm(T, D), vb(T, D), vb(T, D),
        vm(4, 8, T), vm(T, 128), vm(T, D), vb(T, D), vb(T, D),
        vb(2, N, 256), vb(2, N, 256), vb(2, N, 256), vb(2, N, 256),
        vm(T, D), vm(T, D), vm(N, T), vm(N, T), vm(3 * W, T), vm(3 * W, T), vm(32, D),
        vm(T, D), vm(T, D), vm(T, D), vm(H, T),
        pltpu.SemaphoreType.DMA((19,)),
        pltpu.SemaphoreType.DMA((28,)),
        pltpu.SemaphoreType.DMA((28,)),
    ]
    results = pl.pallas_call(
        body,
        out_shape=[f32(T, D), f32(T, D), f32(T, D), f32(H, T), f32(W, T), f32(W, T), f32(8, D)],
        in_specs=[in_hbm] * 10,
        out_specs=[in_hbm] * 7,
        scratch_shapes=scratch,
        compiler_params=pltpu.CompilerParams(
            collective_id=0, has_side_effects=True, vmem_limit_bytes=64 * 1024 * 1024
        ),
        name="layer",
    )(*args)
    return pl.pallas_call(
        place_results,
        out_shape=[
            f32(T, D), f32(T, D), f32(T, D), f32(H, T), f32(W, T), f32(W, T),
            f32(H), f32(H), f32(H), f32(D),
        ],
        in_specs=[in_hbm] * 7,
        out_specs=[in_hbm] * 6 + [in_vmem] * 3 + [in_hbm],
        scratch_shapes=[
            vm(T, D), vm(T, D), vm(T, D), vm(H, T), vm(W, T), vm(W, T), vm(8, D),
            pltpu.SemaphoreType.DMA((7,)), pltpu.SemaphoreType.DMA((7,)),
        ],
        compiler_params=pltpu.CompilerParams(vmem_limit_bytes=64 * 1024 * 1024),
        name="place_results",
    )(*results)


def solution(mesh):
    rows, cols = P("ctx", "dp"), P("dp", "ctx")
    heads = P("dp")
    return jax.shard_map(
        shards,
        mesh=mesh,
        in_specs=(rows, rows, cols, cols, cols, heads, heads, heads, heads, rows),
        out_specs=(rows, rows, rows, cols, cols, cols, heads, heads, heads, heads),
        check_vma=False,
    )
```

```python
import jax
import jax.numpy as jnp
from jax import lax
from jax.experimental import pallas as pl
from jax.experimental.pallas import tpu as pltpu
from jax.sharding import PartitionSpec as P

MESH = pl.DeviceIdType.MESH
F32 = jnp.float32
BF = jnp.bfloat16
T = 256
Q = 128
N = 256
D = 512
H = 8
W = 64
ROWS = 16
TILES = T // ROWS
GROUP_WIDTH = 2048
EPSILON = 1e-05

NN = (((1,), (0,)), ((), ()))
NT = (((1,), (1,)), ((), ()))


def halves(v):
    hi = v.astype(BF)
    return hi, (v - hi.astype(F32)).astype(BF)


def dot(a, b, dims=NN):
    return lax.dot_general(a, b, dims, preferred_element_type=F32)


def dot3(a, b, dims=NN):
    return dot(a[0], b[0], dims) + (dot(a[0], b[1], dims) + dot(a[1], b[0], dims))


def thirds(v):
    hi = v.astype(BF).astype(F32)
    mid = (v - hi).astype(BF).astype(F32)
    return jnp.concatenate([hi, mid, v - hi - mid, jnp.zeros_like(v)], axis=0)


def sum_thirds(v):
    return v[0:8] + (v[8:16] + v[16:24])


def lanes(v):
    return (v[:, 0:128] + v[:, 128:256]) + (v[:, 256:384] + v[:, 384:512])


def fold(v):
    return v[0:8] + v[8:16]


def tiles(step, count=TILES, init=None):
    def run(i, carry):
        return step(pl.ds(pl.multiple_of(i * ROWS, ROWS), ROWS), carry)

    return lax.fori_loop(0, count, run, 0 if init is None else init)


def iota(shape, dim):
    return lax.broadcasted_iota(jnp.int32, shape, dim)


def body(
    x_in, z_in, raw_in, b_in, c_in, decay_in, bias_in, skip_in, gain_in, og_in,
    out_o, hg_o, zg_o, sg_o, bg_o, cg_o, params_o,
    xv, zv, ogv, rawv, gainv, decay_s, bias_s, skip_s, bv, cv, c1v,
    a1, a2, a5, gate, dgate, ogg,
    vh, vl, kh, kl, wh, wl, ph, pld, qh, ql, eh, el, uh, ul,
    bh, bl, ch, cl, cth, ctl, bth, btl, c1h, c1l, gh, gl, gth, gtl, oh, ol, th, tl, fh, fl,
    state, other, sh, sl, ap, ap_in, aq, aq_in, rows, rows_in,
    yi, yv, gated, carry_v, sumh, suml, norm, cols, cols1, d1, d2, k1, k2, dy, yqh, yql,
    dv, dx, first, second, recv_a, recv_b, small, outv, hgv, zgv, sgv,
    local_sem, send_sem, recv_sem,
):
    dp = lax.axis_index("dp")
    ctx = lax.axis_index("ctx")
    place = lax.rem(dp, 4)
    base = dp - place
    right = base + lax.rem(place + 1, 4)
    left = base + lax.rem(place + 3, 4)
    across = base + lax.rem(place + 2, 4)
    early = ctx == 0
    late = ctx == 1

    used = []

    def local(src, dst):
        copy = pltpu.make_async_copy(src, dst, local_sem.at[len(used)])
        used.append(copy)
        return copy

    sent = []

    def remote(src, dst, device):
        k = len(sent)
        sent.append(k)
        return pltpu.make_async_remote_copy(
            src_ref=src, dst_ref=dst, send_sem=send_sem.at[k], recv_sem=recv_sem.at[k],
            device_id=device, device_id_type=MESH,
        )

    to_right, to_left, to_across, to_core = (right, ctx), (left, ctx), (across, ctx), (dp, 1 - ctx)

    barrier = pltpu.get_barrier_semaphore()
    for device in (to_right, to_left, to_across, to_core):
        pl.semaphore_signal(barrier, inc=1, device_id=device, device_id_type=MESH)

    get_heads = [
        local(ref, row)
        for ref, row in ((decay_in, decay_s), (bias_in, bias_s), (skip_in, skip_s))
    ]
    get_raw = local(raw_in, rawv)
    get_gain = local(gain_in, gainv.at[0])
    get_x = local(x_in, xv)
    get_z = local(z_in, zv)
    get_og = local(og_in, ogv)
    get_b = local(b_in, bv.at[pl.ds(0, W)])
    get_c = local(c_in, cv.at[pl.ds(0, W)])
    for copy in used:
        copy.start()
    pl.semaphore_wait(barrier, 4)

    half = W // 2

    def gather(mine, group):
        ahead = [
            remote(mine.at[pl.ds(0, half)], group.at[pl.ds(W, half)], to_right),
            remote(mine.at[pl.ds(half, half)], group.at[pl.ds(2 * W + half, half)], to_left),
        ]
        after = [
            remote(mine.at[pl.ds(half, half)], group.at[pl.ds(W + half, half)], to_right),
            remote(mine.at[pl.ds(0, half)], group.at[pl.ds(2 * W, half)], to_left),
        ]
        onward = [
            remote(group.at[pl.ds(W, half)], group.at[pl.ds(3 * W, half)], to_right),
            remote(group.at[pl.ds(2 * W + half, half)], group.at[pl.ds(3 * W + half, half)], to_left),
        ]
        return ahead, after, onward

    b_ahead, b_after, b_onward = gather(b_in, bv)
    c_ahead, c_after, c_onward = gather(c_in, cv)
    for copy in b_ahead + b_after + c_ahead + c_after:
        copy.start()

    def per_head(ref, width):
        row = iota((H, width), 0)
        value = jnp.full((H, width), ref[0], F32)
        for h in range(1, H):
            value = jnp.where(row == h, ref[h], value)
        return value

    get_raw.wait()
    for copy in get_heads:
        copy.wait()
    speed = jnp.exp(per_head(decay_s, T))
    pre = rawv[...] + per_head(bias_s, T)
    step = jnp.maximum(pre, 0.0) + jnp.log1p(jnp.exp(-jnp.abs(pre)))
    rate = -speed * step
    src, dst = iota((T, T), 0), iota((T, T), 1)
    upto = jnp.where((src <= dst) & (src // Q == dst // Q), 1.0, 0.0).astype(BF)
    run = sum_thirds(dot(thirds(rate).astype(BF), upto))
    total0 = run[:, Q - 1:Q]
    total1 = run[:, T - 1:T]
    position = iota((H, T), 1)
    block1 = position >= Q
    centre = 0.5 * jnp.where(block1, total1, total0)
    scale1 = jnp.exp(run - centre)
    scale2 = step * jnp.exp(centre - run)
    since_start = jnp.where(block1, run + total0, run)
    to_end = jnp.where(block1, total1 - run, total0 - run + total1)
    scale5 = jnp.where(early, step, 1.0) * jnp.exp(jnp.where(early, to_end, since_start))
    stacked = jnp.concatenate(
        [thirds(scale1), thirds(scale2), thirds(scale5), jnp.zeros((32, T), F32)], axis=0
    ).T.astype(BF)
    row, col = iota((128, D), 0), iota((128, D), 1)
    same = (row % 8 == col // W) & (row % 32 < 24)
    for k, ref in enumerate((a1, a2, a5)):
        spread = jnp.where(same & (row // 32 == k), 1.0, 0.0).astype(BF)
        ref[...] = dot(stacked, spread)
    own = iota((H, D), 0) == iota((H, D), 1) // W
    kappa = jnp.sum(
        jnp.where(own, jnp.exp(0.5 * (total0 + total1)), 0.0), axis=0, keepdims=True
    )
    skip_row = jnp.sum(jnp.where(own, per_head(skip_s, D), 0.0), axis=0, keepdims=True)

    for ahead, onward in ((b_ahead, b_onward), (c_ahead, c_onward)):
        for came, goes in zip(ahead, onward):
            came.wait_recv()
            goes.start()

    get_gain.wait()
    get_x.wait()
    get_z.wait()
    get_og.wait()

    def prepare(r, carry):
        z = zv[r]
        sig = 1.0 / (1.0 + jnp.exp(-z))
        g = z * sig
        gate[r] = g
        dgate[r] = sig * (1.0 + z * (1.0 - sig))
        scaled = ogv[r] * gainv[...]
        ogg[r] = scaled
        x = xv[r]
        p = scaled * g
        vh[r], vl[r] = halves(a2[r] * x)
        ph[r], pld[r] = halves(a1[r] * p)
        w = a5[r] * jnp.where(early, x, p)
        ap[r] = w
        wh[r], wl[r] = halves(w)
        return carry

    tiles(prepare)

    ap_out = remote(ap, ap_in, to_core)

    @pl.when(late)
    def _():
        ap_out.start()

    def prepare0(r, carry):
        kh[r], kl[r] = halves((a2[r] * xv[r]) * kappa)
        return carry

    tiles(prepare0, TILES // 2)

    state_out = [remote(state.at[k], other.at[k], to_core) for k in range(4)]

    def end_state(k):
        part = slice(k * W, (k + 1) * W)
        state[k] = dot3((bh[part], bl[part]), (wh[...], wl[...]))
        state_out[k].start()

    get_b.wait()
    for copy in b_ahead:
        copy.wait_send()
    bh[0:W], bl[0:W] = halves(bv[0:W])

    @pl.when(early)
    def _():
        end_state(0)

    def score_grad(out, far, near):
        out[0:Q, 0:Q] = dot3((vh[0:Q], vl[0:Q]), (far[0:Q], near[0:Q]), NT)
        out[0:Q, Q:T] = dot3((kh[...], kl[...]), (far[Q:T], near[Q:T]), NT)
        out[Q:T, Q:T] = dot3((vh[Q:T], vl[Q:T]), (far[Q:T], near[Q:T]), NT)
        out[Q:T, 0:Q] = jnp.zeros((Q, Q), F32)

    score_grad(d1, ph, pld)
    for copy in b_after:
        copy.wait_recv()
    bh[W:3 * W], bl[W:3 * W] = halves(bv[W:3 * W])

    @pl.when(early)
    def _():
        end_state(1)
        end_state(2)

    for copy in b_onward:
        copy.wait_recv()
    bh[3 * W:N], bl[3 * W:N] = halves(bv[3 * W:N])

    @pl.when(early)
    def _():
        end_state(3)

    get_c.wait()
    for copy in c_after:
        copy.wait_recv()
    cth[:, 0:128], ctl[:, 0:128] = halves(cv[0:128].T)
    for copy in c_onward:
        copy.wait_recv()
    cth[:, 128:256], ctl[:, 128:256] = halves(cv[128:256].T)
    c_out = remote(cv, c1v, to_core)

    @pl.when(late)
    def _():
        c_out.start()

    low = src >= dst
    high = src <= dst
    g0 = dot3((cth[0:Q], ctl[0:Q]), (bh[:, 0:Q], bl[:, 0:Q]))
    g1 = dot3((cth[Q:T], ctl[Q:T]), (bh[...], bl[...]))
    gh[0:Q, 0:Q], gl[0:Q, 0:Q] = halves(jnp.where(low[0:Q, 0:Q], g0, 0.0))
    gh[Q:T], gl[Q:T] = halves(jnp.where(low[Q:T], g1, 0.0))
    for k in range(2):
        part = pl.ds(k * 256, 256)
        yi[0:Q, part] = dot3((gh[0:Q, 0:Q], gl[0:Q, 0:Q]), (vh[0:Q, part], vl[0:Q, part]))
        yi[Q:T, part] = dot3(
            (gh[Q:T], gl[Q:T]),
            (
                jnp.concatenate([kh[:, part], vh[Q:T, part]], axis=0),
                jnp.concatenate([kl[:, part], vl[Q:T, part]], axis=0),
            ),
        )

    def mix(r, y):
        yv[r] = y
        mixed = y + skip_row * xv[r]
        g = mixed * gate[r]
        gated[r] = g
        sumh[r, 0:128], suml[r, 0:128] = halves(lanes(g * g))
        sumh[r, 128:256], suml[r, 128:256] = halves(lanes(g * ogg[r]))
        q = g * gate[r]
        qh[r], ql[r] = halves(a1[r] * q)
        return q

    aq_out = remote(aq, aq_in, to_core)

    @pl.when(early)
    def _():
        def go(r, carry):
            mix(r, a1[r] * yi[r])
            return carry

        tiles(go)

    @pl.when(late)
    def _():
        for k in range(4):
            state_out[k].wait_recv()
            sh[k * W:(k + 1) * W], sl[k * W:(k + 1) * W] = halves(other[k])
        for k in range(2):
            part = pl.ds(k * 256, 256)
            carry_v[:, part] = dot3((cth[...], ctl[...]), (sh[:, part], sl[:, part]))

        def go(r, carry):
            w = a5[r] * mix(r, a1[r] * yi[r] + a5[r] * carry_v[r])
            aq[r] = w
            eh[r], el[r] = halves(w)
            return carry

        tiles(go)
        aq_out.start()

    pick = jnp.where(iota((H, 256), 0) == iota((H, 256), 1) // 128, 1.0, 0.0).astype(BF)
    norm[0] = dot(pick, sumh[...], NT) + dot(pick, suml[...], NT)
    norm_out = [
        remote(norm.at[0], norm.at[1 + k], device)
        for k, device in enumerate((to_across, to_right, to_left))
    ]
    for copy in norm_out:
        copy.start()

    score_grad(d2, qh, ql)
    ch[...], cl[...] = halves(cv[...])

    @pl.when(early)
    def _():
        ap_out.wait_recv()
        fh[...], fl[...] = halves(ap_in[...])
        k1[...] = dot3((wh[...], wl[...]), (fh[...], fl[...]), NT)
        bth[...], btl[...] = halves(bv[...].T)
        c_out.wait_recv()
        c1h[...], c1l[...] = halves(c1v[...])

    @pl.when(late)
    def _():
        k1[...] = dot3((sh[...], sl[...]), (wh[...], wl[...]), NT)
        k2[...] = dot3((sh[...], sl[...]), (eh[...], el[...]), NT)

    for copy in norm_out:
        copy.wait_recv()
    sums = (norm[0] + norm[1]) + (norm[2] + norm[3])
    inverse = lax.rsqrt(sums[0:1] * (1.0 / GROUP_WIDTH) + EPSILON)
    slope = inverse * inverse * inverse * sums[1:2] * (1.0 / GROUP_WIDTH)
    rows[...] = jnp.where(iota((8, T), 0) == 0, inverse, slope)
    rows_out = remote(rows, rows_in, to_core)

    @pl.when(late)
    def _():
        rows_out.start()

    full = jnp.where(high, inverse * d1[...] - slope * d2[...], 0.0)
    th[...], tl[...] = halves(full)

    def c_part():
        return dot3((bh[...], bl[...]), (th[...], tl[...]))

    def b_part():
        return dot3((ch[...], cl[...]), (th[...], tl[...]), NT)

    def scatter(parts, landing):
        return [
            remote(parts.at[pl.ds(k * W, W)], landing.at[pl.ds(j * W, W)], device)
            for j, (k, device) in enumerate(((3, to_across), (2, to_right), (1, to_left)))
        ]

    first_out = scatter(first, recv_a)
    second_out = scatter(second, recv_b)

    @pl.when(early)
    def _():
        first[...] = c_part()
        for copy in first_out:
            copy.start()
        second[...] = b_part()
        aq_out.wait_recv()
        oh[...], ol[...] = halves(aq_in[...])
        k2[...] = dot3((wh[...], wl[...]), (oh[...], ol[...]), NT)
        rows_out.wait_recv()
        gth[...], gtl[...] = halves(rows_in[0:1] * k1[...] - rows_in[1:2] * k2[...])
        second[...] += dot3((c1h[...], c1l[...]), (gth[...], gtl[...]), NT)
        for copy in second_out:
            copy.start()

    @pl.when(late)
    def _():
        first[...] = b_part()
        for copy in first_out:
            copy.start()
        second[...] = c_part() + (inverse * k1[...] - slope * k2[...])
        for copy in second_out:
            copy.start()

    lead = iota((128, T), 0)
    cols[...] = jnp.where(lead == 0, inverse, jnp.where(lead == 1, slope, 0.0)).T

    def finish(r, carry):
        gain_sum, skip_sum = carry
        inv = cols[r, 0:1]
        k = cols[r, 1:2]
        g = gated[r]
        x = xv[r]
        y = yv[r]
        normed = g * inv
        outv[r] = normed * gainv[...]
        grad = ogg[r] * inv - g * k
        zgv[r] = grad * (y + skip_row * x) * dgate[r]
        d = grad * gate[r]
        dy[r] = d
        uh[r], ul[r] = halves(a1[r] * d)
        yqh[r], yql[r] = halves(d * y)
        return gain_sum + fold(ogv[r] * normed), skip_sum + fold(d * x)

    zero = jnp.zeros((8, D), F32)
    gain_sum, skip_sum = tiles(finish, init=(zero, zero))
    put_out = local(outv, out_o)
    put_zg = local(zgv, zg_o)
    put_out.start()
    put_zg.start()

    def turned(top, bottom):
        return (gh[top, bottom].astype(F32).T.astype(BF), gl[top, bottom].astype(F32).T.astype(BF))

    lo, hi = slice(0, Q), slice(Q, T)
    g00, g10, g11 = turned(lo, lo), turned(hi, lo), turned(hi, hi)
    for k in range(2):
        part = pl.ds(k * 256, 256)
        dv[0:Q, part] = dot3(g00, (uh[0:Q, part], ul[0:Q, part])) + kappa[
            :, k * 256:(k + 1) * 256
        ] * dot3(g10, (uh[Q:T, part], ul[Q:T, part]))
        dv[Q:T, part] = dot3(g11, (uh[Q:T, part], ul[Q:T, part]))

    small[0:16] = jnp.zeros((16, D), F32)

    def x_grad(r, f):
        hgv[r] = f + skip_row * dy[r]
        uh[r], ul[r] = halves(f * xv[r])

    @pl.when(early)
    def _():
        cols1[...] = jnp.where(lead == 0, rows_in[0:1], jnp.where(lead == 1, rows_in[1:2], 0.0)).T

        def later(r, carry):
            eh[r], el[r] = halves(cols1[r, 0:1] * ap_in[r] - cols1[r, 1:2] * aq_in[r])
            return carry

        tiles(later)
        cross = halves(dot3((bth[...], btl[...]), (c1h[...], c1l[...])))
        for k in range(2):
            part = pl.ds(k * 256, 256)
            dx[:, part] = dot3(cross, (eh[:, part], el[:, part]))

        def go(r, carry):
            tail = a5[r] * dx[r]
            x_grad(r, a2[r] * dv[r] + tail)
            return carry + fold(tail * xv[r])

        small[8:16] = tiles(go, init=zero)

    @pl.when(late)
    def _():
        def go(r, carry):
            x_grad(r, a2[r] * dv[r])
            return carry

        tiles(go)

    put_hg = local(hgv, hg_o)
    put_hg.start()

    heads = jnp.where(own, 1.0, 0.0).astype(BF)
    y_sum = dot(heads, yqh[...], NT) + dot(heads, yql[...], NT)
    x_sum = dot(heads, uh[...], NT) + dot(heads, ul[...], NT)
    from_end = jnp.sum(
        jnp.where(own, jnp.sum(small[8:16], axis=0, keepdims=True), 0.0), axis=1, keepdims=True
    )
    onward = jnp.where(low, 1.0, 0.0).astype(BF)
    rate_grad = sum_thirds(dot(thirds(y_sum - x_sum).astype(BF), onward)) + from_end
    step_grad = (x_sum / step - speed * rate_grad) * (1.0 / (1.0 + jnp.exp(-pre)))
    sgv[...] = step_grad
    put_sg = local(sgv, sg_o)
    put_sg.start()

    def as_row(column):
        hit = iota((H, D), 0) == iota((H, D), 1)
        return jnp.sum(jnp.where(hit, column, 0.0), axis=0, keepdims=True)

    skip_column = jnp.sum(
        jnp.where(own, jnp.sum(skip_sum, axis=0, keepdims=True), 0.0), axis=1, keepdims=True
    )
    small[0:1] = jnp.sum(gain_sum, axis=0, keepdims=True)
    small[1:2] = as_row(jnp.sum(rate_grad * rate, axis=1, keepdims=True))
    small[2:3] = as_row(jnp.sum(step_grad, axis=1, keepdims=True))
    small[3:4] = as_row(skip_column)
    small_out = remote(small.at[pl.ds(0, 8)], small.at[pl.ds(16, 8)], to_core)
    small_out.start()

    def total(parts, landing, copies):
        for copy in copies:
            copy.wait()
        parts[0:W] += landing[0:W] + (landing[W:2 * W] + landing[2 * W:3 * W])

    total(first, recv_a, first_out)
    put_first = [local(first.at[pl.ds(0, W)], o) for o in (cg_o, bg_o)]
    put_second = [local(second.at[pl.ds(0, W)], o) for o in (bg_o, cg_o)]

    @pl.when(early)
    def _():
        put_first[0].start()

    @pl.when(late)
    def _():
        put_first[1].start()

    small_out.wait()
    small[24:32] = small[0:8] + small[16:24]
    put_params = local(small.at[pl.ds(24, 8)], params_o)
    put_params.start()
    total(second, recv_b, second_out)

    @pl.when(early)
    def _():
        put_second[0].start()
        put_first[0].wait()
        put_second[0].wait()
        for copy in state_out:
            copy.wait_send()

    @pl.when(late)
    def _():
        put_second[1].start()
        put_first[1].wait()
        put_second[1].wait()
        for copy in (ap_out, aq_out, c_out, rows_out):
            copy.wait_send()

    for copy in (put_out, put_zg, put_hg, put_sg, put_params):
        copy.wait()
    for copy in b_after + b_onward + c_ahead + c_after + c_onward + norm_out:
        copy.wait_send()


def place_results(*refs):
    results, outputs, held, (get_sem, put_sem) = refs[:7], refs[7:17], refs[17:24], refs[24:]
    out_o, hg_o, zg_o, sg_o, bg_o, cg_o, decay_o, bias_o, skip_o, gain_o = outputs
    gets = [pltpu.make_async_copy(src, dst, get_sem.at[k]) for k, (src, dst) in enumerate(zip(results, held))]
    for copy in gets:
        copy.start()
    puts = []
    rows = held[6]
    for k, ref in enumerate((out_o, hg_o, zg_o, sg_o, bg_o, cg_o, gain_o)):
        gets[k].wait()
        copy = pltpu.make_async_copy(rows.at[0] if ref is gain_o else held[k], ref, put_sem.at[k])
        copy.start()
        puts.append(copy)
    for k, ref in enumerate((decay_o, bias_o, skip_o)):
        ref[...] = rows[1 + k, 0:H]
    for copy in puts:
        copy.wait()


def shards(*args):
    def f32(*shape):
        return jax.ShapeDtypeStruct(shape, F32)

    def vm(*shape):
        return pltpu.VMEM(shape, F32)

    def vb(*shape):
        return pltpu.VMEM(shape, BF)

    in_hbm = pl.BlockSpec(memory_space=pltpu.HBM)
    in_vmem = pl.BlockSpec(memory_space=pltpu.VMEM)
    scalars = pltpu.SMEM((H,), F32)
    wide, narrow = vm(T, D), vb(T, D)
    square, thin = vm(T, T), vb(T, T)
    scratch = [wide] * 3 + [vm(H, T), vm(1, D)] + [scalars] * 3 + [square] * 3
    scratch += [wide] * 6
    scratch += [narrow] * 2 + [vb(Q, D)] * 2 + [narrow] * 10
    scratch += [thin] * 14 + [narrow] * 2 + [thin] * 2 + [narrow] * 2
    scratch += [vm(4, W, D)] * 2 + [narrow] * 2 + [wide] * 4 + [vm(8, T)] * 2
    scratch += [wide] * 4 + [thin] * 2 + [vm(4, 8, T), vm(T, 128), vm(T, 128)]
    scratch += [square] * 4 + [wide] + [narrow] * 2
    scratch += [wide] * 2 + [square] * 2 + [vm(3 * W, T)] * 2 + [vm(32, D)] + [wide] * 3 + [vm(H, T)]
    scratch += [
        pltpu.SemaphoreType.DMA((19,)),
        pltpu.SemaphoreType.DMA((31,)),
        pltpu.SemaphoreType.DMA((31,)),
    ]
    results = pl.pallas_call(
        body,
        out_shape=[f32(T, D), f32(T, D), f32(T, D), f32(H, T), f32(W, T), f32(W, T), f32(8, D)],
        in_specs=[in_hbm] * 10,
        out_specs=[in_hbm] * 7,
        scratch_shapes=scratch,
        compiler_params=pltpu.CompilerParams(
            collective_id=0, has_side_effects=True, vmem_limit_bytes=64 * 1024 * 1024
        ),
        name="layer",
    )(*args)
    return pl.pallas_call(
        place_results,
        out_shape=[
            f32(T, D), f32(T, D), f32(T, D), f32(H, T), f32(W, T), f32(W, T),
            f32(H), f32(H), f32(H), f32(D),
        ],
        in_specs=[in_hbm] * 7,
        out_specs=[in_hbm] * 6 + [in_vmem] * 3 + [in_hbm],
        scratch_shapes=[
            vm(T, D), vm(T, D), vm(T, D), vm(H, T), vm(W, T), vm(W, T), vm(8, D),
            pltpu.SemaphoreType.DMA((7,)), pltpu.SemaphoreType.DMA((7,)),
        ],
        compiler_params=pltpu.CompilerParams(vmem_limit_bytes=64 * 1024 * 1024),
        name="place_results",
    )(*results)


def solution(mesh):
    rows, cols = P("ctx", "dp"), P("dp", "ctx")
    heads = P("dp")
    return jax.shard_map(
        shards,
        mesh=mesh,
        in_specs=(rows, rows, cols, cols, cols, heads, heads, heads, heads, rows),
        out_specs=(rows, rows, rows, cols, cols, cols, heads, heads, heads, heads),
        check_vma=False,
    )
```

```python
import jax
import jax.numpy as jnp
from jax import lax
from jax.experimental import pallas as pl
from jax.experimental.pallas import tpu as pltpu
from jax.sharding import PartitionSpec as P

MESH = pl.DeviceIdType.MESH
F32 = jnp.float32
BF = jnp.bfloat16
T = 256
Q = 128
N = 256
D = 512
H = 8
W = 64
ROWS = 16
TILES = T // ROWS
GROUP_WIDTH = 2048
EPSILON = 1e-05

NN = (((1,), (0,)), ((), ()))
NT = (((1,), (1,)), ((), ()))


def halves(v):
    hi = v.astype(BF)
    return hi, (v - hi.astype(F32)).astype(BF)


def dot(a, b, dims=NN):
    return lax.dot_general(a, b, dims, preferred_element_type=F32)


def dot3(a, b, dims=NN):
    return dot(a[0], b[0], dims) + (dot(a[0], b[1], dims) + dot(a[1], b[0], dims))


def thirds(v):
    hi = v.astype(BF).astype(F32)
    mid = (v - hi).astype(BF).astype(F32)
    return jnp.concatenate([hi, mid, v - hi - mid, jnp.zeros_like(v)], axis=0)


def sum_thirds(v):
    return v[0:8] + (v[8:16] + v[16:24])


def lanes(v):
    return (v[:, 0:128] + v[:, 128:256]) + (v[:, 256:384] + v[:, 384:512])


def fold(v):
    return v[0:8] + v[8:16]


def tiles(step, count=TILES, init=None):
    def run(i, carry):
        return step(pl.ds(pl.multiple_of(i * ROWS, ROWS), ROWS), carry)

    return lax.fori_loop(0, count, run, 0 if init is None else init)


def iota(shape, dim):
    return lax.broadcasted_iota(jnp.int32, shape, dim)


def body(
    x_in, z_in, raw_in, b_in, c_in, decay_in, bias_in, skip_in, gain_in, og_in,
    outv, hgv, zgv, sgv, bgv, cgv, params,
    xv, zv, ogv, rawv, gainv, decay_s, bias_s, skip_s, bv, cv, c1v,
    a1, a2, a5, gate, dgate, ogg,
    vh, vl, kh, kl, wh, wl, ph, pld, qh, ql, eh, el, uh, ul,
    bh, bl, ch, cl, cth, ctl, bth, btl, c1h, c1l, gh, gl, gth, gtl, oh, ol, th, tl, fh, fl,
    state, other, sh, sl, ap, ap_in, aq, aq_in, rows, rows_in,
    yi, yv, gated, carry_v, sumh, suml, norm, cols, cols1, d1, d2, k1, k2, dy, yqh, yql,
    dv, dx, first, second, recv_a, recv_b, small,
    local_sem, send_sem, recv_sem,
):
    dp = lax.axis_index("dp")
    ctx = lax.axis_index("ctx")
    place = lax.rem(dp, 4)
    base = dp - place
    right = base + lax.rem(place + 1, 4)
    left = base + lax.rem(place + 3, 4)
    across = base + lax.rem(place + 2, 4)
    early = ctx == 0
    late = ctx == 1

    used = []

    def local(src, dst):
        copy = pltpu.make_async_copy(src, dst, local_sem.at[len(used)])
        used.append(copy)
        return copy

    sent = []

    def remote(src, dst, device):
        k = len(sent)
        sent.append(k)
        return pltpu.make_async_remote_copy(
            src_ref=src, dst_ref=dst, send_sem=send_sem.at[k], recv_sem=recv_sem.at[k],
            device_id=device, device_id_type=MESH,
        )

    to_right, to_left, to_across, to_core = (right, ctx), (left, ctx), (across, ctx), (dp, 1 - ctx)

    barrier = pltpu.get_barrier_semaphore()
    for device in (to_right, to_left, to_across, to_core):
        pl.semaphore_signal(barrier, inc=1, device_id=device, device_id_type=MESH)

    get_heads = [
        local(ref, row)
        for ref, row in ((decay_in, decay_s), (bias_in, bias_s), (skip_in, skip_s))
    ]
    get_raw = local(raw_in, rawv)
    get_gain = local(gain_in, gainv.at[0])
    get_x = local(x_in, xv)
    get_z = local(z_in, zv)
    get_og = local(og_in, ogv)
    get_b = local(b_in, bv.at[pl.ds(0, W)])
    get_c = local(c_in, cv.at[pl.ds(0, W)])
    for copy in used:
        copy.start()
    def per_head(ref, width):
        row = iota((H, width), 0)
        value = jnp.full((H, width), ref[0], F32)
        for h in range(1, H):
            value = jnp.where(row == h, ref[h], value)
        return value

    get_raw.wait()
    for copy in get_heads:
        copy.wait()
    speed = jnp.exp(per_head(decay_s, T))
    pre = rawv[...] + per_head(bias_s, T)
    step = jnp.maximum(pre, 0.0) + jnp.log1p(jnp.exp(-jnp.abs(pre)))
    rate = -speed * step
    src, dst = iota((T, T), 0), iota((T, T), 1)
    upto = jnp.where((src <= dst) & (src // Q == dst // Q), 1.0, 0.0).astype(BF)
    run = sum_thirds(dot(thirds(rate).astype(BF), upto))

    pl.semaphore_wait(barrier, 4)

    half = W // 2

    def gather(mine, group):
        ahead = [
            remote(mine.at[pl.ds(0, half)], group.at[pl.ds(W, half)], to_right),
            remote(mine.at[pl.ds(half, half)], group.at[pl.ds(2 * W + half, half)], to_left),
        ]
        after = [
            remote(mine.at[pl.ds(half, half)], group.at[pl.ds(W + half, half)], to_right),
            remote(mine.at[pl.ds(0, half)], group.at[pl.ds(2 * W, half)], to_left),
        ]
        onward = [
            remote(group.at[pl.ds(W, half)], group.at[pl.ds(3 * W, half)], to_right),
            remote(group.at[pl.ds(2 * W + half, half)], group.at[pl.ds(3 * W + half, half)], to_left),
        ]
        return ahead, after, onward

    b_ahead, b_after, b_onward = gather(b_in, bv)
    c_ahead, c_after, c_onward = gather(c_in, cv)
    for copy in b_ahead + c_ahead:
        copy.start()

    total0 = run[:, Q - 1:Q]
    total1 = run[:, T - 1:T]
    position = iota((H, T), 1)
    block1 = position >= Q
    centre = 0.5 * jnp.where(block1, total1, total0)
    scale1 = jnp.exp(run - centre)
    scale2 = step * jnp.exp(centre - run)
    since_start = jnp.where(block1, run + total0, run)
    to_end = jnp.where(block1, total1 - run, total0 - run + total1)
    scale5 = jnp.where(early, step, 1.0) * jnp.exp(jnp.where(early, to_end, since_start))
    stacked = jnp.concatenate(
        [thirds(scale1), thirds(scale2), thirds(scale5), jnp.zeros((32, T), F32)], axis=0
    ).T.astype(BF)
    row, col = iota((128, D), 0), iota((128, D), 1)
    same = (row % 8 == col // W) & (row % 32 < 24)
    for k, ref in enumerate((a1, a2, a5)):
        spread = jnp.where(same & (row // 32 == k), 1.0, 0.0).astype(BF)
        ref[...] = dot(stacked, spread)
    for copy in b_after + c_after:
        copy.start()

    own = iota((H, D), 0) == iota((H, D), 1) // W
    kappa = jnp.sum(
        jnp.where(own, jnp.exp(0.5 * (total0 + total1)), 0.0), axis=0, keepdims=True
    )
    skip_row = jnp.sum(jnp.where(own, per_head(skip_s, D), 0.0), axis=0, keepdims=True)

    for ahead, onward in ((b_ahead, b_onward), (c_ahead, c_onward)):
        for came, goes in zip(ahead, onward):
            came.wait_recv()
            goes.start()

    get_gain.wait()
    get_x.wait()
    get_z.wait()
    get_og.wait()

    def prepare(r, carry):
        z = zv[r]
        sig = 1.0 / (1.0 + jnp.exp(-z))
        g = z * sig
        gate[r] = g
        dgate[r] = sig * (1.0 + z * (1.0 - sig))
        scaled = ogv[r] * gainv[...]
        ogg[r] = scaled
        x = xv[r]
        p = scaled * g
        vh[r], vl[r] = halves(a2[r] * x)
        ph[r], pld[r] = halves(a1[r] * p)
        w = a5[r] * jnp.where(early, x, p)
        ap[r] = w
        wh[r], wl[r] = halves(w)
        return carry

    tiles(prepare)

    ap_out = remote(ap, ap_in, to_core)

    @pl.when(late)
    def _():
        ap_out.start()

    def prepare0(r, carry):
        kh[r], kl[r] = halves((a2[r] * xv[r]) * kappa)
        return carry

    tiles(prepare0, TILES // 2)

    state_out = [remote(state.at[k], other.at[k], to_core) for k in range(4)]

    def end_state(k):
        part = slice(k * W, (k + 1) * W)
        state[k] = dot3((bh[part], bl[part]), (wh[...], wl[...]))
        state_out[k].start()

    get_b.wait()
    bh[0:W], bl[0:W] = halves(bv[0:W])

    @pl.when(early)
    def _():
        end_state(0)

    def score_grad(out, far, near):
        out[0:Q, 0:Q] = dot3((vh[0:Q], vl[0:Q]), (far[0:Q], near[0:Q]), NT)
        out[0:Q, Q:T] = dot3((kh[...], kl[...]), (far[Q:T], near[Q:T]), NT)
        out[Q:T, Q:T] = dot3((vh[Q:T], vl[Q:T]), (far[Q:T], near[Q:T]), NT)
        out[Q:T, 0:Q] = jnp.zeros((Q, Q), F32)

    score_grad(d1, ph, pld)
    for copy in b_after:
        copy.wait_recv()
    bh[W:3 * W], bl[W:3 * W] = halves(bv[W:3 * W])

    @pl.when(early)
    def _():
        end_state(1)
        end_state(2)

    for copy in b_onward:
        copy.wait_recv()
    bh[3 * W:N], bl[3 * W:N] = halves(bv[3 * W:N])

    @pl.when(early)
    def _():
        end_state(3)

    get_c.wait()
    for copy in c_after:
        copy.wait_recv()
    cth[:, 0:128], ctl[:, 0:128] = halves(cv[0:128].T)
    for copy in c_onward:
        copy.wait_recv()
    cth[:, 128:256], ctl[:, 128:256] = halves(cv[128:256].T)
    c_out = remote(cv, c1v, to_core)

    @pl.when(late)
    def _():
        c_out.start()

    low = src >= dst
    high = src <= dst
    g0 = dot3((cth[0:Q], ctl[0:Q]), (bh[:, 0:Q], bl[:, 0:Q]))
    g1 = dot3((cth[Q:T], ctl[Q:T]), (bh[...], bl[...]))
    gh[0:Q, 0:Q], gl[0:Q, 0:Q] = halves(jnp.where(low[0:Q, 0:Q], g0, 0.0))
    gh[Q:T], gl[Q:T] = halves(jnp.where(low[Q:T], g1, 0.0))
    for k in range(2):
        part = pl.ds(k * 256, 256)
        yi[0:Q, part] = dot3((gh[0:Q, 0:Q], gl[0:Q, 0:Q]), (vh[0:Q, part], vl[0:Q, part]))
        yi[Q:T, part] = dot3(
            (gh[Q:T], gl[Q:T]),
            (
                jnp.concatenate([kh[:, part], vh[Q:T, part]], axis=0),
                jnp.concatenate([kl[:, part], vl[Q:T, part]], axis=0),
            ),
        )

    def mix(r, y):
        yv[r] = y
        mixed = y + skip_row * xv[r]
        g = mixed * gate[r]
        gated[r] = g
        sumh[r, 0:128], suml[r, 0:128] = halves(lanes(g * g))
        sumh[r, 128:256], suml[r, 128:256] = halves(lanes(g * ogg[r]))
        q = g * gate[r]
        qh[r], ql[r] = halves(a1[r] * q)
        return q

    aq_out = remote(aq, aq_in, to_core)

    @pl.when(early)
    def _():
        def go(r, carry):
            mix(r, a1[r] * yi[r])
            return carry

        tiles(go)

    @pl.when(late)
    def _():
        for k in range(4):
            state_out[k].wait_recv()
            sh[k * W:(k + 1) * W], sl[k * W:(k + 1) * W] = halves(other[k])
        for k in range(2):
            part = pl.ds(k * 256, 256)
            carry_v[:, part] = dot3((cth[...], ctl[...]), (sh[:, part], sl[:, part]))

        def go(r, carry):
            w = a5[r] * mix(r, a1[r] * yi[r] + a5[r] * carry_v[r])
            aq[r] = w
            eh[r], el[r] = halves(w)
            return carry

        tiles(go)
        aq_out.start()

    pick = jnp.where(iota((H, 256), 0) == iota((H, 256), 1) // 128, 1.0, 0.0).astype(BF)
    norm[0] = dot(pick, sumh[...], NT) + dot(pick, suml[...], NT)
    norm_out = [
        remote(norm.at[0], norm.at[1 + k], device)
        for k, device in enumerate((to_across, to_right, to_left))
    ]
    for copy in norm_out:
        copy.start()

    score_grad(d2, qh, ql)
    ch[...], cl[...] = halves(cv[...])

    @pl.when(early)
    def _():
        ap_out.wait_recv()
        fh[...], fl[...] = halves(ap_in[...])
        k1[...] = dot3((wh[...], wl[...]), (fh[...], fl[...]), NT)
        bth[...], btl[...] = halves(bv[...].T)
        c_out.wait_recv()
        c1h[...], c1l[...] = halves(c1v[...])

    @pl.when(late)
    def _():
        k1[...] = dot3((sh[...], sl[...]), (wh[...], wl[...]), NT)
        k2[...] = dot3((sh[...], sl[...]), (eh[...], el[...]), NT)

    for copy in norm_out:
        copy.wait_recv()
    sums = (norm[0] + norm[1]) + (norm[2] + norm[3])
    inverse = lax.rsqrt(sums[0:1] * (1.0 / GROUP_WIDTH) + EPSILON)
    slope = inverse * inverse * inverse * sums[1:2] * (1.0 / GROUP_WIDTH)
    rows[...] = jnp.where(iota((8, T), 0) == 0, inverse, slope)
    rows_out = remote(rows, rows_in, to_core)

    @pl.when(late)
    def _():
        rows_out.start()

    full = jnp.where(high, inverse * d1[...] - slope * d2[...], 0.0)
    th[...], tl[...] = halves(full)

    def c_part():
        return dot3((bh[...], bl[...]), (th[...], tl[...]))

    def b_part():
        return dot3((ch[...], cl[...]), (th[...], tl[...]), NT)

    def scatter(parts, landing):
        far = [
            remote(parts.at[pl.ds(3 * W, half)], landing.at[pl.ds(0, half)], to_right),
            remote(parts.at[pl.ds(3 * W + half, half)], landing.at[pl.ds(half, half)], to_left),
        ]
        near = [
            remote(parts.at[pl.ds(2 * W + half, half)], landing.at[pl.ds(W + half, half)], to_right),
            remote(parts.at[pl.ds(W, half)], landing.at[pl.ds(2 * W, half)], to_left),
        ]
        total = [
            remote(parts.at[pl.ds(2 * W, half)], landing.at[pl.ds(W, half)], to_right),
            remote(parts.at[pl.ds(W + half, half)], landing.at[pl.ds(2 * W + half, half)], to_left),
        ]
        return far, near, total

    def relay(parts, landing, far, total):
        far[0].wait_recv()
        parts[2 * W:2 * W + half] += landing[0:half]
        total[0].start()
        far[1].wait_recv()
        parts[W + half:2 * W] += landing[half:W]
        total[1].start()

    first_far, first_near, first_total = scatter(first, recv_a)
    second_far, second_near, second_total = scatter(second, recv_b)

    def begin(copies):
        for copy in copies:
            copy.start()

    @pl.when(early)
    def _():
        first[...] = c_part()
        begin(first_far)
        second[...] = b_part()
        aq_out.wait_recv()
        oh[...], ol[...] = halves(aq_in[...])
        k2[...] = dot3((wh[...], wl[...]), (oh[...], ol[...]), NT)
        rows_out.wait_recv()
        gth[...], gtl[...] = halves(rows_in[0:1] * k1[...] - rows_in[1:2] * k2[...])
        second[...] += dot3((c1h[...], c1l[...]), (gth[...], gtl[...]), NT)
        begin(second_far)

    @pl.when(late)
    def _():
        first[...] = b_part()
        begin(first_far)
        second[...] = c_part() + (inverse * k1[...] - slope * k2[...])
        begin(second_far)

    begin(first_near)

    lead = iota((128, T), 0)
    cols[...] = jnp.where(lead == 0, inverse, jnp.where(lead == 1, slope, 0.0)).T

    def finish(r, carry):
        gain_sum, skip_sum = carry
        inv = cols[r, 0:1]
        k = cols[r, 1:2]
        g = gated[r]
        x = xv[r]
        y = yv[r]
        normed = g * inv
        outv[r] = normed * gainv[...]
        grad = ogg[r] * inv - g * k
        zgv[r] = grad * (y + skip_row * x) * dgate[r]
        d = grad * gate[r]
        dy[r] = d
        uh[r], ul[r] = halves(a1[r] * d)
        yqh[r], yql[r] = halves(d * y)
        return gain_sum + fold(ogv[r] * normed), skip_sum + fold(d * x)

    zero = jnp.zeros((8, D), F32)
    gain_sum, skip_sum = tiles(finish, init=(zero, zero))

    begin(second_near)

    def turned(top, bottom):
        return (gh[top, bottom].astype(F32).T.astype(BF), gl[top, bottom].astype(F32).T.astype(BF))

    lo, hi = slice(0, Q), slice(Q, T)
    g00, g10, g11 = turned(lo, lo), turned(hi, lo), turned(hi, hi)
    for k in range(2):
        part = pl.ds(k * 256, 256)
        dv[0:Q, part] = dot3(g00, (uh[0:Q, part], ul[0:Q, part])) + kappa[
            :, k * 256:(k + 1) * 256
        ] * dot3(g10, (uh[Q:T, part], ul[Q:T, part]))
        dv[Q:T, part] = dot3(g11, (uh[Q:T, part], ul[Q:T, part]))

    relay(first, recv_a, first_far, first_total)
    relay(second, recv_b, second_far, second_total)
    small[0:16] = jnp.zeros((16, D), F32)

    def x_grad(r, f):
        hgv[r] = f + skip_row * dy[r]
        uh[r], ul[r] = halves(f * xv[r])

    @pl.when(early)
    def _():
        cols1[...] = jnp.where(lead == 0, rows_in[0:1], jnp.where(lead == 1, rows_in[1:2], 0.0)).T

        def later(r, carry):
            eh[r], el[r] = halves(cols1[r, 0:1] * ap_in[r] - cols1[r, 1:2] * aq_in[r])
            return carry

        tiles(later)
        cross = halves(dot3((bth[...], btl[...]), (c1h[...], c1l[...])))
        for k in range(2):
            part = pl.ds(k * 256, 256)
            dx[:, part] = dot3(cross, (eh[:, part], el[:, part]))

        def go(r, carry):
            tail = a5[r] * dx[r]
            x_grad(r, a2[r] * dv[r] + tail)
            return carry + fold(tail * xv[r])

        small[8:16] = tiles(go, init=zero)

    @pl.when(late)
    def _():
        def go(r, carry):
            x_grad(r, a2[r] * dv[r])
            return carry

        tiles(go)


    heads = jnp.where(own, 1.0, 0.0).astype(BF)
    y_sum = dot(heads, yqh[...], NT) + dot(heads, yql[...], NT)
    x_sum = dot(heads, uh[...], NT) + dot(heads, ul[...], NT)
    from_end = jnp.sum(
        jnp.where(own, jnp.sum(small[8:16], axis=0, keepdims=True), 0.0), axis=1, keepdims=True
    )
    onward = jnp.where(low, 1.0, 0.0).astype(BF)
    rate_grad = sum_thirds(dot(thirds(y_sum - x_sum).astype(BF), onward)) + from_end
    step_grad = (x_sum / step - speed * rate_grad) * (1.0 / (1.0 + jnp.exp(-pre)))
    sgv[...] = step_grad

    def as_row(column):
        hit = iota((H, D), 0) == iota((H, D), 1)
        return jnp.sum(jnp.where(hit, column, 0.0), axis=0, keepdims=True)

    skip_column = jnp.sum(
        jnp.where(own, jnp.sum(skip_sum, axis=0, keepdims=True), 0.0), axis=1, keepdims=True
    )
    small[0:1] = jnp.sum(gain_sum, axis=0, keepdims=True)
    small[1:2] = as_row(jnp.sum(rate_grad * rate, axis=1, keepdims=True))
    small[2:3] = as_row(jnp.sum(step_grad, axis=1, keepdims=True))
    small[3:4] = as_row(skip_column)
    small_out = remote(small.at[pl.ds(0, 8)], small.at[pl.ds(16, 8)], to_core)
    small_out.start()

    for copy in small_out, *first_near, *first_total:
        copy.wait_recv()
    params[...] = small[0:8] + small[16:24]
    first_sum = first[0:W] + (recv_a[W:2 * W] + recv_a[2 * W:3 * W])
    for copy in second_near + second_total:
        copy.wait_recv()
    second_sum = second[0:W] + (recv_b[W:2 * W] + recv_b[2 * W:3 * W])

    @pl.when(early)
    def _():
        cgv[...] = first_sum
        bgv[...] = second_sum
        for copy in state_out:
            copy.wait_send()

    @pl.when(late)
    def _():
        bgv[...] = first_sum
        cgv[...] = second_sum
        for copy in (ap_out, aq_out, c_out, rows_out):
            copy.wait_send()

    for copy in b_ahead + b_after + b_onward + c_ahead + c_after + c_onward + norm_out:
        copy.wait_send()
    for copy in first_far + first_near + first_total + second_far + second_near + second_total:
        copy.wait_send()
    small_out.wait_send()


def place_results(*refs):
    results, outputs, sem = refs[:7], refs[7:17], refs[17]
    out_o, hg_o, zg_o, sg_o, bg_o, cg_o, decay_o, bias_o, skip_o, gain_o = outputs
    rows = results[6]
    copies = [
        pltpu.make_async_copy(rows.at[0] if ref is gain_o else results[k], ref, sem.at[k])
        for k, ref in enumerate((out_o, hg_o, zg_o, sg_o, bg_o, cg_o, gain_o))
    ]
    for copy in copies:
        copy.start()
    for k, ref in enumerate((decay_o, bias_o, skip_o)):
        ref[...] = rows[1 + k, 0:H]
    for copy in copies:
        copy.wait()


def shards(*args):
    def f32(*shape):
        return jax.ShapeDtypeStruct(shape, F32)

    def vm(*shape):
        return pltpu.VMEM(shape, F32)

    def vb(*shape):
        return pltpu.VMEM(shape, BF)

    in_hbm = pl.BlockSpec(memory_space=pltpu.HBM)
    in_vmem = pl.BlockSpec(memory_space=pltpu.VMEM)
    scalars = pltpu.SMEM((H,), F32)
    wide, narrow = vm(T, D), vb(T, D)
    square, thin = vm(T, T), vb(T, T)
    scratch = [wide] * 3 + [vm(H, T), vm(1, D)] + [scalars] * 3 + [square] * 3
    scratch += [wide] * 6
    scratch += [narrow] * 2 + [vb(Q, D)] * 2 + [narrow] * 10
    scratch += [thin] * 14 + [narrow] * 2 + [thin] * 2 + [narrow] * 2
    scratch += [vm(4, W, D)] * 2 + [narrow] * 2 + [wide] * 4 + [vm(8, T)] * 2
    scratch += [wide] * 4 + [thin] * 2 + [vm(4, 8, T), vm(T, 128), vm(T, 128)]
    scratch += [square] * 4 + [wide] + [narrow] * 2
    scratch += [wide] * 2 + [square] * 2 + [vm(3 * W, T)] * 2 + [vm(32, D)]
    scratch += [
        pltpu.SemaphoreType.DMA((10,)),
        pltpu.SemaphoreType.DMA((37,)),
        pltpu.SemaphoreType.DMA((37,)),
    ]
    args = [pltpu.with_memory_space_constraint(array, pltpu.HBM) for array in args]
    results = pl.pallas_call(
        body,
        out_shape=[f32(T, D), f32(T, D), f32(T, D), f32(H, T), f32(W, T), f32(W, T), f32(8, D)],
        in_specs=[in_hbm] * 10,
        out_specs=[in_vmem] * 7,
        scratch_shapes=scratch,
        compiler_params=pltpu.CompilerParams(
            collective_id=0, has_side_effects=True, vmem_limit_bytes=40 * 1024 * 1024
        ),
        name="layer",
    )(*args)
    return pl.pallas_call(
        place_results,
        out_shape=[
            f32(T, D), f32(T, D), f32(T, D), f32(H, T), f32(W, T), f32(W, T),
            f32(H), f32(H), f32(H), f32(D),
        ],
        in_specs=[in_vmem] * 7,
        out_specs=[in_hbm] * 6 + [in_vmem] * 3 + [in_hbm],
        scratch_shapes=[pltpu.SemaphoreType.DMA((7,))],
        compiler_params=pltpu.CompilerParams(vmem_limit_bytes=16 * 1024 * 1024),
        name="place_results",
    )(*results)


def solution(mesh):
    rows, cols = P("ctx", "dp"), P("dp", "ctx")
    heads = P("dp")
    return jax.shard_map(
        shards,
        mesh=mesh,
        in_specs=(rows, rows, cols, cols, cols, heads, heads, heads, heads, rows),
        out_specs=(rows, rows, rows, cols, cols, cols, heads, heads, heads, heads),
        check_vma=False,
    )
```

```python
import jax
import jax.numpy as jnp
from jax import lax
from jax.experimental import pallas as pl
from jax.experimental.pallas import tpu as pltpu
from jax.sharding import PartitionSpec as P

MESH = pl.DeviceIdType.MESH
F32 = jnp.float32
BF = jnp.bfloat16
T = 256
Q = 128
N = 256
D = 512
H = 8
W = 64
ROWS = 16
TILES = T // ROWS
GROUP_WIDTH = 2048
EPSILON = 1e-05

NN = (((1,), (0,)), ((), ()))
NT = (((1,), (1,)), ((), ()))


def halves(v):
    hi = v.astype(BF)
    return hi, (v - hi.astype(F32)).astype(BF)


def dot(a, b, dims=NN):
    return lax.dot_general(a, b, dims, preferred_element_type=F32)


def dot3(a, b, dims=NN):
    return dot(a[0], b[0], dims) + (dot(a[0], b[1], dims) + dot(a[1], b[0], dims))


def thirds(v):
    hi = v.astype(BF).astype(F32)
    mid = (v - hi).astype(BF).astype(F32)
    return jnp.concatenate([hi, mid, v - hi - mid, jnp.zeros_like(v)], axis=0)


def sum_thirds(v):
    return v[0:8] + (v[8:16] + v[16:24])


def lanes(v):
    return (v[:, 0:128] + v[:, 128:256]) + (v[:, 256:384] + v[:, 384:512])


def fold(v):
    return v[0:8] + v[8:16]


def tiles(step, count=TILES, init=None, first=0):
    def run(i, carry):
        return step(pl.ds(pl.multiple_of(first + i * ROWS, ROWS), ROWS), carry)

    return lax.fori_loop(0, count, run, 0 if init is None else init)


def iota(shape, dim):
    return lax.broadcasted_iota(jnp.int32, shape, dim)


def body(
    x_in, z_in, raw_in, b_in, c_in, decay_in, bias_in, skip_in, gain_in, og_in,
    outv, hgv, zgv, sgv, bgv, cgv, params,
    xv, zv, ogv, rawv, gainv, decay_s, bias_s, skip_s, bv, cv, c1v,
    a1, a2, a5, gate, dgate, ogg,
    vh, vl, kh, kl, wh, wl, ph, pld, qh, ql, eh, el, uh, ul,
    bh, bl, ch, cl, cth, ctl, bth, btl, c1h, c1l, gh, gl, gth, gtl, oh, ol, th, tl, fh, fl,
    state, other, sh, sl, ap, ap_in, aq, aq_in, rows, rows_in,
    yi, yv, gated, carry_v, sumh, suml, norm, cols, cols1, d1, d2, k1, k2, dy, yqh, yql,
    dv, dx, b_part, c_part, recv_b, recv_c, small,
    local_sem, send_sem, recv_sem,
):
    dp = lax.axis_index("dp")
    ctx = lax.axis_index("ctx")
    place = lax.rem(dp, 4)
    base = dp - place
    right = base + lax.rem(place + 1, 4)
    left = base + lax.rem(place + 3, 4)
    across = base + lax.rem(place + 2, 4)
    early = ctx == 0
    late = ctx == 1

    used = []

    def local(src, dst):
        copy = pltpu.make_async_copy(src, dst, local_sem.at[len(used)])
        used.append(copy)
        return copy

    sent = []

    def remote(src, dst, device):
        k = len(sent)
        sent.append(k)
        return pltpu.make_async_remote_copy(
            src_ref=src, dst_ref=dst, send_sem=send_sem.at[k], recv_sem=recv_sem.at[k],
            device_id=device, device_id_type=MESH,
        )

    to_right, to_left, to_across, to_core = (right, ctx), (left, ctx), (across, ctx), (dp, 1 - ctx)

    barrier = pltpu.get_barrier_semaphore()
    for device in (to_right, to_left, to_across, to_core):
        pl.semaphore_signal(barrier, inc=1, device_id=device, device_id_type=MESH)

    get_heads = [
        local(ref, row)
        for ref, row in ((decay_in, decay_s), (bias_in, bias_s), (skip_in, skip_s))
    ]
    get_raw = local(raw_in, rawv)
    get_gain = local(gain_in, gainv.at[0])
    get_x = local(x_in, xv)
    get_z = local(z_in, zv)
    get_og = local(og_in, ogv)
    get_b = local(b_in, bv.at[pl.ds(0, W)])
    get_c = local(c_in, cv.at[pl.ds(0, W)])
    for copy in used:
        copy.start()
    def per_head(ref, width):
        row = iota((H, width), 0)
        value = jnp.full((H, width), ref[0], F32)
        for h in range(1, H):
            value = jnp.where(row == h, ref[h], value)
        return value

    get_raw.wait()
    for copy in get_heads:
        copy.wait()
    speed = jnp.exp(per_head(decay_s, T))
    pre = rawv[...] + per_head(bias_s, T)
    step = jnp.maximum(pre, 0.0) + jnp.log1p(jnp.exp(-jnp.abs(pre)))
    rate = -speed * step
    src, dst = iota((T, T), 0), iota((T, T), 1)
    upto = jnp.where((src <= dst) & (src // Q == dst // Q), 1.0, 0.0).astype(BF)
    run = sum_thirds(dot(thirds(rate).astype(BF), upto))

    pl.semaphore_wait(barrier, 4)

    lo, hi = slice(0, Q), slice(Q, T)

    def gather(mine, group, j):
        part = pl.ds(j * Q, Q)
        return [
            remote(mine.at[:, part], group.at[pl.ds(k * W, W), part], device)
            for k, device in ((3, to_across), (1, to_right), (2, to_left))
        ]

    def begin(copies):
        for copy in copies:
            copy.start()

    def arrive(copies):
        for copy in copies:
            copy.wait_recv()

    b_copies = [gather(b_in, bv, j) for j in range(2)]
    c_copies = [gather(c_in, cv, j) for j in range(2)]
    begin(b_copies[0] + c_copies[0])

    total0 = run[:, Q - 1:Q]
    total1 = run[:, T - 1:T]
    position = iota((H, T), 1)
    block1 = position >= Q
    centre = 0.5 * jnp.where(block1, total1, total0)
    scale1 = jnp.exp(run - centre)
    scale2 = step * jnp.exp(centre - run)
    since_start = jnp.where(block1, run + total0, run)
    to_end = jnp.where(block1, total1 - run, total0 - run + total1)
    scale5 = jnp.where(early, step, 1.0) * jnp.exp(jnp.where(early, to_end, since_start))
    stacked = jnp.concatenate(
        [thirds(scale1), thirds(scale2), thirds(scale5), jnp.zeros((32, T), F32)], axis=0
    ).T.astype(BF)
    row, col = iota((128, D), 0), iota((128, D), 1)
    same = (row % 8 == col // W) & (row % 32 < 24)
    for k, ref in enumerate((a1, a2, a5)):
        spread = jnp.where(same & (row // 32 == k), 1.0, 0.0).astype(BF)
        ref[...] = dot(stacked, spread)
    begin(b_copies[1] + c_copies[1])

    own = iota((H, D), 0) == iota((H, D), 1) // W
    kappa = jnp.sum(
        jnp.where(own, jnp.exp(0.5 * (total0 + total1)), 0.0), axis=0, keepdims=True
    )
    skip_row = jnp.sum(jnp.where(own, per_head(skip_s, D), 0.0), axis=0, keepdims=True)

    get_gain.wait()
    get_x.wait()
    get_z.wait()
    get_og.wait()

    def prepare(r, carry):
        z = zv[r]
        sig = 1.0 / (1.0 + jnp.exp(-z))
        g = z * sig
        gate[r] = g
        dgate[r] = sig * (1.0 + z * (1.0 - sig))
        scaled = ogv[r] * gainv[...]
        ogg[r] = scaled
        x = xv[r]
        p = scaled * g
        vh[r], vl[r] = halves(a2[r] * x)
        ph[r], pld[r] = halves(a1[r] * p)
        w = a5[r] * jnp.where(early, x, p)
        ap[r] = w
        wh[r], wl[r] = halves(w)
        return carry

    tiles(prepare)

    ap_out = remote(ap, ap_in, to_core)

    @pl.when(late)
    def _():
        ap_out.start()

    def prepare0(r, carry):
        kh[r], kl[r] = halves((a2[r] * xv[r]) * kappa)
        return carry

    tiles(prepare0, TILES // 2)

    def score_grad(out, far, near):
        out[0:Q, 0:Q] = dot3((vh[0:Q], vl[0:Q]), (far[0:Q], near[0:Q]), NT)
        out[0:Q, Q:T] = dot3((kh[...], kl[...]), (far[Q:T], near[Q:T]), NT)
        out[Q:T, Q:T] = dot3((vh[Q:T], vl[Q:T]), (far[Q:T], near[Q:T]), NT)

    score_grad(d1, ph, pld)

    low = src >= dst
    high = src <= dst
    get_b.wait()
    get_c.wait()
    arrive(b_copies[0])
    bh[:, lo], bl[:, lo] = halves(bv[:, lo])
    arrive(c_copies[0])
    cth[lo], ctl[lo] = halves(cv[:, lo].T)
    g0 = dot3((cth[lo], ctl[lo]), (bh[:, lo], bl[:, lo]))
    gh[lo, lo], gl[lo, lo] = halves(jnp.where(low[lo, lo], g0, 0.0))
    for k in range(2):
        part = pl.ds(k * 256, 256)
        yi[lo, part] = dot3((gh[lo, lo], gl[lo, lo]), (vh[lo, part], vl[lo, part]))

    def mix(r, y):
        yv[r] = y
        mixed = y + skip_row * xv[r]
        g = mixed * gate[r]
        gated[r] = g
        sumh[r, 0:128], suml[r, 0:128] = halves(lanes(g * g))
        sumh[r, 128:256], suml[r, 128:256] = halves(lanes(g * ogg[r]))
        q = g * gate[r]
        qh[r], ql[r] = halves(a1[r] * q)
        return q

    pick = jnp.where(iota((H, 256), 0) == iota((H, 256), 1) // 128, 1.0, 0.0).astype(BF)
    norm_out = [
        [
            remote(norm.at[j, 0], norm.at[j, 1 + k], device)
            for k, device in enumerate((to_across, to_right, to_left))
        ]
        for j in range(2)
    ]

    def send_sums(j, block):
        norm[j, 0] = dot(pick, sumh[block], NT) + dot(pick, suml[block], NT)
        begin(norm_out[j])

    def mix_early(j, block):
        def go(r, carry):
            mix(r, a1[r] * yi[r])
            return carry

        tiles(go, TILES // 2, first=j * Q)
        send_sums(j, block)

    @pl.when(early)
    def _():
        mix_early(0, lo)

    state_out = [remote(state.at[k], other.at[k], to_core) for k in range(4)]
    arrive(b_copies[1])
    bh[:, hi], bl[:, hi] = halves(bv[:, hi])

    @pl.when(early)
    def _():
        for k in range(4):
            part = slice(k * W, (k + 1) * W)
            state[k] = dot3((bh[part], bl[part]), (wh[...], wl[...]))
            state_out[k].start()

    arrive(c_copies[1])
    cth[hi], ctl[hi] = halves(cv[:, hi].T)
    c_out = remote(cv, c1v, to_core)

    @pl.when(late)
    def _():
        c_out.start()

    g1 = dot3((cth[hi], ctl[hi]), (bh[...], bl[...]))
    gh[hi], gl[hi] = halves(jnp.where(low[hi], g1, 0.0))
    for k in range(2):
        part = pl.ds(k * 256, 256)
        yi[hi, part] = dot3(
            (gh[hi], gl[hi]),
            (
                jnp.concatenate([kh[:, part], vh[hi, part]], axis=0),
                jnp.concatenate([kl[:, part], vl[hi, part]], axis=0),
            ),
        )

    aq_out = remote(aq, aq_in, to_core)

    @pl.when(early)
    def _():
        mix_early(1, hi)

    @pl.when(late)
    def _():
        arrive(state_out)
        for k in range(4):
            sh[k * W:(k + 1) * W], sl[k * W:(k + 1) * W] = halves(other[k])
        for k in range(2):
            part = pl.ds(k * 256, 256)
            carry_v[:, part] = dot3((cth[...], ctl[...]), (sh[:, part], sl[:, part]))

        def go(r, carry):
            w = a5[r] * mix(r, a1[r] * yi[r] + a5[r] * carry_v[r])
            aq[r] = w
            eh[r], el[r] = halves(w)
            return carry

        tiles(go, TILES // 2)
        send_sums(0, lo)
        tiles(go, TILES // 2, first=Q)
        send_sums(1, hi)
        aq_out.start()

    score_grad(d2, qh, ql)
    ch[...], cl[...] = halves(cv[...])

    @pl.when(early)
    def _():
        ap_out.wait_recv()
        fh[...], fl[...] = halves(ap_in[...])
        k1[...] = dot3((wh[...], wl[...]), (fh[...], fl[...]), NT)
        bth[...], btl[...] = halves(bv[...].T)
        c_out.wait_recv()
        c1h[...], c1l[...] = halves(c1v[...])

    @pl.when(late)
    def _():
        k1[...] = dot3((sh[...], sl[...]), (wh[...], wl[...]), NT)
        k2[...] = dot3((sh[...], sl[...]), (eh[...], el[...]), NT)

    def factors(j, block):
        arrive(norm_out[j])
        sums = (norm[j, 0] + norm[j, 1]) + (norm[j, 2] + norm[j, 3])
        inv = lax.rsqrt(sums[0:1] * (1.0 / GROUP_WIDTH) + EPSILON)
        slope = inv * inv * inv * sums[1:2] * (1.0 / GROUP_WIDTH)
        rows[:, block] = jnp.where(iota((8, Q), 0) == 0, inv, slope)
        return inv, slope

    def scatter(parts, landing, block):
        return [
            remote(parts.at[pl.ds(k * W, W), block], landing.at[pl.ds(j * W, W), block], device)
            for j, (k, device) in enumerate(((3, to_across), (2, to_right), (1, to_left)))
        ]

    c_sums = [scatter(c_part, recv_c, pl.ds(j * Q, Q)) for j in range(2)]
    b_sums = scatter(b_part, recv_b, pl.ds(0, T))

    def c_grad(j, block, until):
        inv, slope = factors(j, block)
        full = jnp.where(high[until, block], inv * d1[until, block] - slope * d2[until, block], 0.0)
        th[until, block], tl[until, block] = halves(full)
        grad = dot3((bh[:, until], bl[:, until]), (th[until, block], tl[until, block]))

        @pl.when(early)
        def _():
            c_part[:, block] = grad

        @pl.when(late)
        def _():
            c_part[:, block] = grad + (inv * k1[:, block] - slope * k2[:, block])

        begin(c_sums[j])

    c_grad(0, lo, lo)
    c_grad(1, hi, slice(0, T))
    th[hi, lo] = jnp.zeros((Q, Q), BF)
    tl[hi, lo] = jnp.zeros((Q, Q), BF)
    rows_out = remote(rows, rows_in, to_core)
    b_grad = dot3((ch[...], cl[...]), (th[...], tl[...]), NT)

    @pl.when(late)
    def _():
        rows_out.start()
        b_part[...] = b_grad
        begin(b_sums)

    @pl.when(early)
    def _():
        aq_out.wait_recv()
        oh[...], ol[...] = halves(aq_in[...])
        k2[...] = dot3((wh[...], wl[...]), (oh[...], ol[...]), NT)
        rows_out.wait_recv()
        gth[...], gtl[...] = halves(rows_in[0:1] * k1[...] - rows_in[1:2] * k2[...])
        b_part[...] = b_grad + dot3((c1h[...], c1l[...]), (gth[...], gtl[...]), NT)
        begin(b_sums)

    lead = iota((128, T), 0)
    cols[...] = jnp.where(lead == 0, rows[0:1], jnp.where(lead == 1, rows[1:2], 0.0)).T

    def finish(r, carry):
        gain_sum, skip_sum = carry
        inv = cols[r, 0:1]
        k = cols[r, 1:2]
        g = gated[r]
        x = xv[r]
        y = yv[r]
        normed = g * inv
        outv[r] = normed * gainv[...]
        grad = ogg[r] * inv - g * k
        zgv[r] = grad * (y + skip_row * x) * dgate[r]
        d = grad * gate[r]
        dy[r] = d
        uh[r], ul[r] = halves(a1[r] * d)
        yqh[r], yql[r] = halves(d * y)
        return gain_sum + fold(ogv[r] * normed), skip_sum + fold(d * x)

    zero = jnp.zeros((8, D), F32)
    gain_sum, skip_sum = tiles(finish, init=(zero, zero))

    def turned(top, bottom):
        return (gh[top, bottom].astype(F32).T.astype(BF), gl[top, bottom].astype(F32).T.astype(BF))

    g00, g10, g11 = turned(lo, lo), turned(hi, lo), turned(hi, hi)
    for k in range(2):
        part = pl.ds(k * 256, 256)
        dv[0:Q, part] = dot3(g00, (uh[0:Q, part], ul[0:Q, part])) + kappa[
            :, k * 256:(k + 1) * 256
        ] * dot3(g10, (uh[Q:T, part], ul[Q:T, part]))
        dv[Q:T, part] = dot3(g11, (uh[Q:T, part], ul[Q:T, part]))

    small[0:16] = jnp.zeros((16, D), F32)

    def x_grad(r, f):
        hgv[r] = f + skip_row * dy[r]
        uh[r], ul[r] = halves(f * xv[r])

    @pl.when(early)
    def _():
        cols1[...] = jnp.where(lead == 0, rows_in[0:1], jnp.where(lead == 1, rows_in[1:2], 0.0)).T

        def later(r, carry):
            eh[r], el[r] = halves(cols1[r, 0:1] * ap_in[r] - cols1[r, 1:2] * aq_in[r])
            return carry

        tiles(later)
        cross = halves(dot3((bth[...], btl[...]), (c1h[...], c1l[...])))
        for k in range(2):
            part = pl.ds(k * 256, 256)
            dx[:, part] = dot3(cross, (eh[:, part], el[:, part]))

        def go(r, carry):
            tail = a5[r] * dx[r]
            x_grad(r, a2[r] * dv[r] + tail)
            return carry + fold(tail * xv[r])

        small[8:16] = tiles(go, init=zero)

    @pl.when(late)
    def _():
        def go(r, carry):
            x_grad(r, a2[r] * dv[r])
            return carry

        tiles(go)


    heads = jnp.where(own, 1.0, 0.0).astype(BF)
    y_sum = dot(heads, yqh[...], NT) + dot(heads, yql[...], NT)
    x_sum = dot(heads, uh[...], NT) + dot(heads, ul[...], NT)
    from_end = jnp.sum(
        jnp.where(own, jnp.sum(small[8:16], axis=0, keepdims=True), 0.0), axis=1, keepdims=True
    )
    onward = jnp.where(low, 1.0, 0.0).astype(BF)
    rate_grad = sum_thirds(dot(thirds(y_sum - x_sum).astype(BF), onward)) + from_end
    step_grad = (x_sum / step - speed * rate_grad) * (1.0 / (1.0 + jnp.exp(-pre)))
    sgv[...] = step_grad

    def as_row(column):
        hit = iota((H, D), 0) == iota((H, D), 1)
        return jnp.sum(jnp.where(hit, column, 0.0), axis=0, keepdims=True)

    skip_column = jnp.sum(
        jnp.where(own, jnp.sum(skip_sum, axis=0, keepdims=True), 0.0), axis=1, keepdims=True
    )
    small[0:1] = jnp.sum(gain_sum, axis=0, keepdims=True)
    small[1:2] = as_row(jnp.sum(rate_grad * rate, axis=1, keepdims=True))
    small[2:3] = as_row(jnp.sum(step_grad, axis=1, keepdims=True))
    small[3:4] = as_row(skip_column)
    small_out = remote(small.at[pl.ds(0, 8)], small.at[pl.ds(16, 8)], to_core)
    small_out.start()

    arrive([small_out] + c_sums[0] + c_sums[1])
    params[...] = small[0:8] + small[16:24]
    cgv[...] = c_part[0:W] + (recv_c[0:W] + (recv_c[W:2 * W] + recv_c[2 * W:3 * W]))
    arrive(b_sums)
    bgv[...] = b_part[0:W] + (recv_b[0:W] + (recv_b[W:2 * W] + recv_b[2 * W:3 * W]))

    @pl.when(early)
    def _():
        for copy in state_out:
            copy.wait_send()

    @pl.when(late)
    def _():
        for copy in (ap_out, aq_out, c_out, rows_out):
            copy.wait_send()

    for copies in (*b_copies, *c_copies, *norm_out, *c_sums, b_sums, [small_out]):
        for copy in copies:
            copy.wait_send()


def place_results(*refs):
    results, outputs, sem = refs[:7], refs[7:17], refs[17]
    out_o, hg_o, zg_o, sg_o, bg_o, cg_o, decay_o, bias_o, skip_o, gain_o = outputs
    rows = results[6]
    copies = [
        pltpu.make_async_copy(rows.at[0] if ref is gain_o else results[k], ref, sem.at[k])
        for k, ref in enumerate((out_o, hg_o, zg_o, sg_o, bg_o, cg_o, gain_o))
    ]
    for copy in copies:
        copy.start()
    for k, ref in enumerate((decay_o, bias_o, skip_o)):
        ref[...] = rows[1 + k, 0:H]
    for copy in copies:
        copy.wait()


def shards(*args):
    def f32(*shape):
        return jax.ShapeDtypeStruct(shape, F32)

    def vm(*shape):
        return pltpu.VMEM(shape, F32)

    def vb(*shape):
        return pltpu.VMEM(shape, BF)

    in_hbm = pl.BlockSpec(memory_space=pltpu.HBM)
    in_vmem = pl.BlockSpec(memory_space=pltpu.VMEM)
    scalars = pltpu.SMEM((H,), F32)
    wide, narrow = vm(T, D), vb(T, D)
    square, thin = vm(T, T), vb(T, T)
    scratch = [wide] * 3 + [vm(H, T), vm(1, D)] + [scalars] * 3 + [square] * 3
    scratch += [wide] * 6
    scratch += [narrow] * 2 + [vb(Q, D)] * 2 + [narrow] * 10
    scratch += [thin] * 14 + [narrow] * 2 + [thin] * 2 + [narrow] * 2
    scratch += [vm(4, W, D)] * 2 + [narrow] * 2 + [wide] * 4 + [vm(8, T)] * 2
    scratch += [wide] * 4 + [thin] * 2 + [vm(2, 4, 8, Q), vm(T, 128), vm(T, 128)]
    scratch += [square] * 4 + [wide] + [narrow] * 2
    scratch += [wide] * 2 + [square] * 2 + [vm(3 * W, T)] * 2 + [vm(32, D)]
    scratch += [
        pltpu.SemaphoreType.DMA((10,)),
        pltpu.SemaphoreType.DMA((36,)),
        pltpu.SemaphoreType.DMA((36,)),
    ]
    args = [pltpu.with_memory_space_constraint(array, pltpu.HBM) for array in args]
    results = pl.pallas_call(
        body,
        out_shape=[f32(T, D), f32(T, D), f32(T, D), f32(H, T), f32(W, T), f32(W, T), f32(8, D)],
        in_specs=[in_hbm] * 10,
        out_specs=[in_vmem] * 7,
        scratch_shapes=scratch,
        compiler_params=pltpu.CompilerParams(
            collective_id=0, has_side_effects=True, vmem_limit_bytes=40 * 1024 * 1024
        ),
        name="layer",
    )(*args)
    return pl.pallas_call(
        place_results,
        out_shape=[
            f32(T, D), f32(T, D), f32(T, D), f32(H, T), f32(W, T), f32(W, T),
            f32(H), f32(H), f32(H), f32(D),
        ],
        in_specs=[in_vmem] * 7,
        out_specs=[in_hbm] * 6 + [in_vmem] * 3 + [in_hbm],
        scratch_shapes=[pltpu.SemaphoreType.DMA((7,))],
        compiler_params=pltpu.CompilerParams(vmem_limit_bytes=16 * 1024 * 1024),
        name="place_results",
    )(*results)


def solution(mesh):
    rows, cols = P("ctx", "dp"), P("dp", "ctx")
    heads = P("dp")
    return jax.shard_map(
        shards,
        mesh=mesh,
        in_specs=(rows, rows, cols, cols, cols, heads, heads, heads, heads, rows),
        out_specs=(rows, rows, rows, cols, cols, cols, heads, heads, heads, heads),
        check_vma=False,
    )
```

```python
import jax
import jax.numpy as jnp
from jax import lax
from jax.experimental import pallas as pl
from jax.experimental.pallas import tpu as pltpu
from jax.sharding import PartitionSpec as P

MESH = pl.DeviceIdType.MESH
F32 = jnp.float32
BF = jnp.bfloat16
T = 256
Q = 128
N = 256
D = 512
H = 8
W = 64
ROWS = 16
TILES = T // ROWS
GROUP_WIDTH = 2048
EPSILON = 1e-05

NN = (((1,), (0,)), ((), ()))
NT = (((1,), (1,)), ((), ()))


def halves(v):
    hi = v.astype(BF)
    return hi, (v - hi.astype(F32)).astype(BF)


def dot(a, b, dims=NN):
    return lax.dot_general(a, b, dims, preferred_element_type=F32)


def dot3(a, b, dims=NN):
    return dot(a[0], b[0], dims) + (dot(a[0], b[1], dims) + dot(a[1], b[0], dims))


def thirds(v):
    hi = v.astype(BF).astype(F32)
    mid = (v - hi).astype(BF).astype(F32)
    return jnp.concatenate([hi, mid, v - hi - mid, jnp.zeros_like(v)], axis=0)


def sum_thirds(v):
    return v[0:8] + (v[8:16] + v[16:24])


def lanes(v):
    return (v[:, 0:128] + v[:, 128:256]) + (v[:, 256:384] + v[:, 384:512])


def fold(v):
    return v[0:8] + v[8:16]


def tiles(step, count=TILES, init=None, first=0):
    def run(i, carry):
        return step(pl.ds(pl.multiple_of(first + i * ROWS, ROWS), ROWS), carry)

    return lax.fori_loop(0, count, run, 0 if init is None else init)


def iota(shape, dim):
    return lax.broadcasted_iota(jnp.int32, shape, dim)


def body(
    x_in, z_in, raw_in, b_in, c_in, decay_in, bias_in, skip_in, gain_in, og_in,
    outv, hgv, zgv, sgv, bgv, cgv, params,
    xv, zv, ogv, rawv, gainv, decay_s, bias_s, skip_s, bv, cv, c1v,
    a1, a2, a5, gate, dgate, ogg,
    vh, vl, kh, kl, wh, wl, ph, pld, qh, ql, eh, el, uh, ul,
    bh, bl, ch, cl, cth, ctl, bth, btl, c1h, c1l, gh, gl, gth, gtl, oh, ol, th, tl, fh, fl,
    state, other, sh, sl, ap, ap_in, aq, aq_in, rows, rows_in,
    yi, yv, gated, carry_v, sumh, suml, norm, cols, cols1, d1, d2, k1, k2, dy, yqh, yql,
    dv, dx, b_part, c_parts, recv_b, recv_c, small, crh, crl, turnh, turnl,
    local_sem, send_sem, recv_sem,
):
    dp = lax.axis_index("dp")
    ctx = lax.axis_index("ctx")
    place = lax.rem(dp, 4)
    base = dp - place
    right = base + lax.rem(place + 1, 4)
    left = base + lax.rem(place + 3, 4)
    across = base + lax.rem(place + 2, 4)
    early = ctx == 0
    late = ctx == 1

    used = []

    def local(src, dst):
        copy = pltpu.make_async_copy(src, dst, local_sem.at[len(used)])
        used.append(copy)
        return copy

    sent = []

    def remote(src, dst, device):
        k = len(sent)
        sent.append(k)
        return pltpu.make_async_remote_copy(
            src_ref=src, dst_ref=dst, send_sem=send_sem.at[k], recv_sem=recv_sem.at[k],
            device_id=device, device_id_type=MESH,
        )

    to_right, to_left, to_across, to_core = (right, ctx), (left, ctx), (across, ctx), (dp, 1 - ctx)

    barrier = pltpu.get_barrier_semaphore()
    for device in (to_right, to_left, to_across, to_core):
        pl.semaphore_signal(barrier, inc=1, device_id=device, device_id_type=MESH)

    get_heads = [
        local(ref, row)
        for ref, row in ((decay_in, decay_s), (bias_in, bias_s), (skip_in, skip_s))
    ]
    get_raw = local(raw_in, rawv)
    get_gain = local(gain_in, gainv.at[0])
    get_x = local(x_in, xv)
    get_z = local(z_in, zv)
    get_og = local(og_in, ogv)
    get_b = local(b_in, bv.at[pl.ds(0, W)])
    get_c = local(c_in, cv.at[pl.ds(0, W)])
    for copy in used:
        copy.start()
    def per_head(ref, width):
        row = iota((H, width), 0)
        value = jnp.full((H, width), ref[0], F32)
        for h in range(1, H):
            value = jnp.where(row == h, ref[h], value)
        return value

    get_raw.wait()
    for copy in get_heads:
        copy.wait()
    speed = jnp.exp(per_head(decay_s, T))
    pre = rawv[...] + per_head(bias_s, T)
    step = jnp.maximum(pre, 0.0) + jnp.log1p(jnp.exp(-jnp.abs(pre)))
    rate = -speed * step
    src, dst = iota((T, T), 0), iota((T, T), 1)
    upto = jnp.where((src <= dst) & (src // Q == dst // Q), 1.0, 0.0).astype(BF)
    run = sum_thirds(dot(thirds(rate).astype(BF), upto))

    pl.semaphore_wait(barrier, 4)

    lo, hi = slice(0, Q), slice(Q, T)

    def gather(mine, group, j):
        part = pl.ds(j * Q, Q)
        return [
            remote(mine.at[:, part], group.at[pl.ds(k * W, W), part], device)
            for k, device in ((3, to_across), (1, to_right), (2, to_left))
        ]

    def begin(copies):
        for copy in copies:
            copy.start()

    def arrive(copies):
        for copy in copies:
            copy.wait_recv()

    b_copies = [gather(b_in, bv, j) for j in range(2)]
    c_copies = [gather(c_in, cv, j) for j in range(2)]
    begin(b_copies[0] + c_copies[0])

    total0 = run[:, Q - 1:Q]
    total1 = run[:, T - 1:T]
    position = iota((H, T), 1)
    block1 = position >= Q
    centre = 0.5 * jnp.where(block1, total1, total0)
    scale1 = jnp.exp(run - centre)
    scale2 = step * jnp.exp(centre - run)
    since_start = jnp.where(block1, run + total0, run)
    to_end = jnp.where(block1, total1 - run, total0 - run + total1)
    scale5 = jnp.where(early, step, 1.0) * jnp.exp(jnp.where(early, to_end, since_start))
    stacked = jnp.concatenate(
        [thirds(scale1), thirds(scale2), thirds(scale5), jnp.zeros((32, T), F32)], axis=0
    ).T.astype(BF)
    row, col = iota((128, D), 0), iota((128, D), 1)
    same = (row % 8 == col // W) & (row % 32 < 24)
    for k, ref in enumerate((a1, a2, a5)):
        spread = jnp.where(same & (row // 32 == k), 1.0, 0.0).astype(BF)
        ref[...] = dot(stacked, spread)
    begin(b_copies[1] + c_copies[1])

    own = iota((H, D), 0) == iota((H, D), 1) // W
    kappa = jnp.sum(
        jnp.where(own, jnp.exp(0.5 * (total0 + total1)), 0.0), axis=0, keepdims=True
    )
    skip_row = jnp.sum(jnp.where(own, per_head(skip_s, D), 0.0), axis=0, keepdims=True)

    get_gain.wait()
    get_x.wait()
    get_z.wait()
    get_og.wait()

    def prepare(r, carry):
        z = zv[r]
        sig = 1.0 / (1.0 + jnp.exp(-z))
        g = z * sig
        gate[r] = g
        dgate[r] = sig * (1.0 + z * (1.0 - sig))
        scaled = ogv[r] * gainv[...]
        ogg[r] = scaled
        x = xv[r]
        p = scaled * g
        vh[r], vl[r] = halves(a2[r] * x)
        ph[r], pld[r] = halves(a1[r] * p)
        w = a5[r] * jnp.where(early, x, p)
        ap[r] = w
        wh[r], wl[r] = halves(w)
        return carry

    tiles(prepare)

    ap_out = remote(ap, ap_in, to_core)

    @pl.when(late)
    def _():
        ap_out.start()

    def prepare0(r, carry):
        kh[r], kl[r] = halves((a2[r] * xv[r]) * kappa)
        return carry

    tiles(prepare0, TILES // 2)

    def score_grad(out, far, near):
        out[0:Q, 0:Q] = dot3((vh[0:Q], vl[0:Q]), (far[0:Q], near[0:Q]), NT)
        out[0:Q, Q:T] = dot3((kh[...], kl[...]), (far[Q:T], near[Q:T]), NT)
        out[Q:T, Q:T] = dot3((vh[Q:T], vl[Q:T]), (far[Q:T], near[Q:T]), NT)

    score_grad(d1, ph, pld)

    low = src >= dst
    high = src <= dst
    get_b.wait()
    get_c.wait()
    arrive(b_copies[0])
    bh[:, lo], bl[:, lo] = halves(bv[:, lo])
    arrive(c_copies[0])
    cth[lo], ctl[lo] = halves(cv[:, lo].T)
    g0 = dot3((cth[lo], ctl[lo]), (bh[:, lo], bl[:, lo]))
    gh[lo, lo], gl[lo, lo] = halves(jnp.where(low[lo, lo], g0, 0.0))
    for k in range(2):
        part = pl.ds(k * 256, 256)
        yi[lo, part] = dot3((gh[lo, lo], gl[lo, lo]), (vh[lo, part], vl[lo, part]))

    def mix(r, y):
        yv[r] = y
        mixed = y + skip_row * xv[r]
        g = mixed * gate[r]
        gated[r] = g
        sumh[r, 0:128], suml[r, 0:128] = halves(lanes(g * g))
        sumh[r, 128:256], suml[r, 128:256] = halves(lanes(g * ogg[r]))
        q = g * gate[r]
        qh[r], ql[r] = halves(a1[r] * q)
        return q

    pick = jnp.where(iota((H, 256), 0) == iota((H, 256), 1) // 128, 1.0, 0.0).astype(BF)
    norm_out = [
        [
            remote(norm.at[j, 0], norm.at[j, 1 + k], device)
            for k, device in enumerate((to_across, to_right, to_left))
        ]
        for j in range(2)
    ]

    def send_sums(j, block):
        norm[j, 0] = dot(pick, sumh[block], NT) + dot(pick, suml[block], NT)
        begin(norm_out[j])

    def mix_early(j, block):
        def go(r, carry):
            mix(r, a1[r] * yi[r])
            return carry

        tiles(go, TILES // 2, first=j * Q)
        send_sums(j, block)

    @pl.when(early)
    def _():
        mix_early(0, lo)

    def scatter(parts, landing):
        return [
            remote(parts.at[pl.ds(k * W, W)], landing.at[pl.ds(j * W, W)], device)
            for j, (k, device) in enumerate(((3, to_across), (2, to_right), (1, to_left)))
        ]

    b_sums = scatter(b_part, recv_b)
    c_sums = [scatter(c_parts.at[j], recv_c.at[j]) for j in range(2)]

    def c_grad(j, grad):
        th[...], tl[...] = halves(jnp.where(high, grad[...], 0.0))
        return dot3((bh[...], bl[...]), (th[...], tl[...]))

    state_out = [remote(state.at[k], other.at[k], to_core) for k in range(4)]
    arrive(b_copies[1])
    bh[:, hi], bl[:, hi] = halves(bv[:, hi])

    @pl.when(early)
    def _():
        for k in range(4):
            part = slice(k * W, (k + 1) * W)
            state[k] = dot3((bh[part], bl[part]), (wh[...], wl[...]))
            state_out[k].start()

    c_parts[0] = c_grad(0, d1)
    arrive(c_copies[1])

    @pl.when(early)
    def _():
        begin(c_sums[0])

    cth[hi], ctl[hi] = halves(cv[:, hi].T)
    c_out = remote(cv, c1v, to_core)

    @pl.when(late)
    def _():
        c_out.start()

    g1 = dot3((cth[hi], ctl[hi]), (bh[...], bl[...]))
    gh[hi], gl[hi] = halves(jnp.where(low[hi], g1, 0.0))
    for k in range(2):
        part = pl.ds(k * 256, 256)
        yi[hi, part] = dot3(
            (gh[hi], gl[hi]),
            (
                jnp.concatenate([kh[:, part], vh[hi, part]], axis=0),
                jnp.concatenate([kl[:, part], vl[hi, part]], axis=0),
            ),
        )

    aq_out = remote(aq, aq_in, to_core)

    @pl.when(early)
    def _():
        mix_early(1, hi)

    @pl.when(late)
    def _():
        arrive(state_out)
        for k in range(4):
            sh[k * W:(k + 1) * W], sl[k * W:(k + 1) * W] = halves(other[k])
        for k in range(2):
            part = pl.ds(k * 256, 256)
            carry_v[:, part] = dot3((cth[...], ctl[...]), (sh[:, part], sl[:, part]))

        def go(r, carry):
            w = a5[r] * mix(r, a1[r] * yi[r] + a5[r] * carry_v[r])
            aq[r] = w
            eh[r], el[r] = halves(w)
            return carry

        tiles(go, TILES // 2)
        send_sums(0, lo)
        tiles(go, TILES // 2, first=Q)
        send_sums(1, hi)
        aq_out.start()
        c_parts[0] += dot3((sh[...], sl[...]), (wh[...], wl[...]), NT)
        begin(c_sums[0])

    score_grad(d2, qh, ql)
    ch[...], cl[...] = halves(cv[...])

    @pl.when(early)
    def _():
        c_parts[1] = c_grad(1, d2)
        begin(c_sums[1])
        ap_out.wait_recv()
        fh[...], fl[...] = halves(ap_in[...])
        k1[...] = dot3((wh[...], wl[...]), (fh[...], fl[...]), NT)
        bth[...], btl[...] = halves(bv[...].T)
        c_out.wait_recv()
        c1h[...], c1l[...] = halves(c1v[...])
        crh[...], crl[...] = halves(dot3((bth[...], btl[...]), (c1h[...], c1l[...])))

    @pl.when(late)
    def _():
        c_parts[1] = c_grad(1, d2) + dot3((sh[...], sl[...]), (eh[...], el[...]), NT)
        begin(c_sums[1])

    for rows_of, cols_of in ((lo, lo), (hi, lo), (hi, hi)):
        turnh[cols_of, rows_of] = gh[rows_of, cols_of].astype(F32).T.astype(BF)
        turnl[cols_of, rows_of] = gl[rows_of, cols_of].astype(F32).T.astype(BF)

    def factors(j, block):
        arrive(norm_out[j])
        sums = (norm[j, 0] + norm[j, 1]) + (norm[j, 2] + norm[j, 3])
        inv = lax.rsqrt(sums[0:1] * (1.0 / GROUP_WIDTH) + EPSILON)
        slope = inv * inv * inv * sums[1:2] * (1.0 / GROUP_WIDTH)
        rows[:, block] = jnp.where(iota((8, Q), 0) == 0, inv, slope)

    for j, block in enumerate((lo, hi)):
        factors(j, block)
    th[...], tl[...] = halves(jnp.where(high, rows[0:1] * d1[...] - rows[1:2] * d2[...], 0.0))
    rows_out = remote(rows, rows_in, to_core)
    b_grad = dot3((ch[...], cl[...]), (th[...], tl[...]), NT)

    @pl.when(late)
    def _():
        rows_out.start()
        b_part[...] = b_grad
        begin(b_sums)

    @pl.when(early)
    def _():
        aq_out.wait_recv()
        oh[...], ol[...] = halves(aq_in[...])
        k2[...] = dot3((wh[...], wl[...]), (oh[...], ol[...]), NT)
        rows_out.wait_recv()
        gth[...], gtl[...] = halves(rows_in[0:1] * k1[...] - rows_in[1:2] * k2[...])
        b_part[...] = b_grad + dot3((c1h[...], c1l[...]), (gth[...], gtl[...]), NT)
        begin(b_sums)

    lead = iota((128, T), 0)
    cols[...] = jnp.where(lead == 0, rows[0:1], jnp.where(lead == 1, rows[1:2], 0.0)).T

    def finish(r, carry):
        gain_sum, skip_sum = carry
        inv = cols[r, 0:1]
        k = cols[r, 1:2]
        g = gated[r]
        x = xv[r]
        y = yv[r]
        normed = g * inv
        outv[r] = normed * gainv[...]
        grad = ogg[r] * inv - g * k
        zgv[r] = grad * (y + skip_row * x) * dgate[r]
        d = grad * gate[r]
        dy[r] = d
        uh[r], ul[r] = halves(a1[r] * d)
        yqh[r], yql[r] = halves(d * y)
        return gain_sum + fold(ogv[r] * normed), skip_sum + fold(d * x)

    zero = jnp.zeros((8, D), F32)
    gain_sum, skip_sum = tiles(finish, init=(zero, zero))

    for k in range(2):
        part = pl.ds(k * 256, 256)
        dv[0:Q, part] = dot3((turnh[lo, lo], turnl[lo, lo]), (uh[0:Q, part], ul[0:Q, part])) + kappa[
            :, k * 256:(k + 1) * 256
        ] * dot3((turnh[lo, hi], turnl[lo, hi]), (uh[Q:T, part], ul[Q:T, part]))
        dv[Q:T, part] = dot3((turnh[hi, hi], turnl[hi, hi]), (uh[Q:T, part], ul[Q:T, part]))

    small[0:16] = jnp.zeros((16, D), F32)

    def x_grad(r, f):
        hgv[r] = f + skip_row * dy[r]
        uh[r], ul[r] = halves(f * xv[r])

    @pl.when(early)
    def _():
        cols1[...] = jnp.where(lead == 0, rows_in[0:1], jnp.where(lead == 1, rows_in[1:2], 0.0)).T

        def later(r, carry):
            eh[r], el[r] = halves(cols1[r, 0:1] * ap_in[r] - cols1[r, 1:2] * aq_in[r])
            return carry

        tiles(later)
        for k in range(2):
            part = pl.ds(k * 256, 256)
            dx[:, part] = dot3((crh[...], crl[...]), (eh[:, part], el[:, part]))

        def go(r, carry):
            tail = a5[r] * dx[r]
            x_grad(r, a2[r] * dv[r] + tail)
            return carry + fold(tail * xv[r])

        small[8:16] = tiles(go, init=zero)

    @pl.when(late)
    def _():
        def go(r, carry):
            x_grad(r, a2[r] * dv[r])
            return carry

        tiles(go)


    heads = jnp.where(own, 1.0, 0.0).astype(BF)
    y_sum = dot(heads, yqh[...], NT) + dot(heads, yql[...], NT)
    x_sum = dot(heads, uh[...], NT) + dot(heads, ul[...], NT)
    from_end = jnp.sum(
        jnp.where(own, jnp.sum(small[8:16], axis=0, keepdims=True), 0.0), axis=1, keepdims=True
    )
    onward = jnp.where(low, 1.0, 0.0).astype(BF)
    rate_grad = sum_thirds(dot(thirds(y_sum - x_sum).astype(BF), onward)) + from_end
    step_grad = (x_sum / step - speed * rate_grad) * (1.0 / (1.0 + jnp.exp(-pre)))
    sgv[...] = step_grad

    def as_row(column):
        hit = iota((H, D), 0) == iota((H, D), 1)
        return jnp.sum(jnp.where(hit, column, 0.0), axis=0, keepdims=True)

    skip_column = jnp.sum(
        jnp.where(own, jnp.sum(skip_sum, axis=0, keepdims=True), 0.0), axis=1, keepdims=True
    )
    small[0:1] = jnp.sum(gain_sum, axis=0, keepdims=True)
    small[1:2] = as_row(jnp.sum(rate_grad * rate, axis=1, keepdims=True))
    small[2:3] = as_row(jnp.sum(step_grad, axis=1, keepdims=True))
    small[3:4] = as_row(skip_column)
    small_out = remote(small.at[pl.ds(0, 8)], small.at[pl.ds(16, 8)], to_core)
    small_out.start()

    arrive([small_out] + c_sums[0] + c_sums[1])
    params[...] = small[0:8] + small[16:24]
    c_total = [
        c_parts[j, 0:W] + (recv_c[j, 0:W] + (recv_c[j, W:2 * W] + recv_c[j, 2 * W:3 * W]))
        for j in range(2)
    ]
    cgv[...] = rows[0:1] * c_total[0] - rows[1:2] * c_total[1]
    arrive(b_sums)
    bgv[...] = b_part[0:W] + (recv_b[0:W] + (recv_b[W:2 * W] + recv_b[2 * W:3 * W]))

    @pl.when(early)
    def _():
        for copy in state_out:
            copy.wait_send()

    @pl.when(late)
    def _():
        for copy in (ap_out, aq_out, c_out, rows_out):
            copy.wait_send()

    for copies in (*b_copies, *c_copies, *norm_out, *c_sums, b_sums, [small_out]):
        for copy in copies:
            copy.wait_send()


def place_results(*refs):
    results, outputs, sem = refs[:7], refs[7:17], refs[17]
    out_o, hg_o, zg_o, sg_o, bg_o, cg_o, decay_o, bias_o, skip_o, gain_o = outputs
    rows = results[6]
    copies = [
        pltpu.make_async_copy(rows.at[0] if ref is gain_o else results[k], ref, sem.at[k])
        for k, ref in enumerate((out_o, hg_o, zg_o, sg_o, bg_o, cg_o, gain_o))
    ]
    for copy in copies:
        copy.start()
    for k, ref in enumerate((decay_o, bias_o, skip_o)):
        ref[...] = rows[1 + k, 0:H]
    for copy in copies:
        copy.wait()


def shards(*args):
    def f32(*shape):
        return jax.ShapeDtypeStruct(shape, F32)

    def vm(*shape):
        return pltpu.VMEM(shape, F32)

    def vb(*shape):
        return pltpu.VMEM(shape, BF)

    in_hbm = pl.BlockSpec(memory_space=pltpu.HBM)
    in_vmem = pl.BlockSpec(memory_space=pltpu.VMEM)
    scalars = pltpu.SMEM((H,), F32)
    wide, narrow = vm(T, D), vb(T, D)
    square, thin = vm(T, T), vb(T, T)
    scratch = [wide] * 3 + [vm(H, T), vm(1, D)] + [scalars] * 3 + [square] * 3
    scratch += [wide] * 6
    scratch += [narrow] * 2 + [vb(Q, D)] * 2 + [narrow] * 10
    scratch += [thin] * 14 + [narrow] * 2 + [thin] * 2 + [narrow] * 2
    scratch += [vm(4, W, D)] * 2 + [narrow] * 2 + [wide] * 4 + [vm(8, T)] * 2
    scratch += [wide] * 4 + [thin] * 2 + [vm(2, 4, 8, Q), vm(T, 128), vm(T, 128)]
    scratch += [square] * 4 + [wide] + [narrow] * 2
    scratch += [wide] * 2 + [square, vm(2, N, T), vm(3 * W, T), vm(2, 3 * W, T), vm(32, D)] + [thin] * 4
    scratch += [
        pltpu.SemaphoreType.DMA((10,)),
        pltpu.SemaphoreType.DMA((36,)),
        pltpu.SemaphoreType.DMA((36,)),
    ]
    args = [pltpu.with_memory_space_constraint(array, pltpu.HBM) for array in args]
    results = pl.pallas_call(
        body,
        out_shape=[f32(T, D), f32(T, D), f32(T, D), f32(H, T), f32(W, T), f32(W, T), f32(8, D)],
        in_specs=[in_hbm] * 10,
        out_specs=[in_vmem] * 7,
        scratch_shapes=scratch,
        compiler_params=pltpu.CompilerParams(
            collective_id=0, has_side_effects=True, vmem_limit_bytes=40 * 1024 * 1024
        ),
        name="layer",
    )(*args)
    return pl.pallas_call(
        place_results,
        out_shape=[
            f32(T, D), f32(T, D), f32(T, D), f32(H, T), f32(W, T), f32(W, T),
            f32(H), f32(H), f32(H), f32(D),
        ],
        in_specs=[in_vmem] * 7,
        out_specs=[in_hbm] * 6 + [in_vmem] * 3 + [in_hbm],
        scratch_shapes=[pltpu.SemaphoreType.DMA((7,))],
        compiler_params=pltpu.CompilerParams(vmem_limit_bytes=16 * 1024 * 1024),
        name="place_results",
    )(*results)


def solution(mesh):
    rows, cols = P("ctx", "dp"), P("dp", "ctx")
    heads = P("dp")
    return jax.shard_map(
        shards,
        mesh=mesh,
        in_specs=(rows, rows, cols, cols, cols, heads, heads, heads, heads, rows),
        out_specs=(rows, rows, rows, cols, cols, cols, heads, heads, heads, heads),
        check_vma=False,
    )
```

```python
import jax
import jax.numpy as jnp
from jax import lax
from jax.experimental import pallas as pl
from jax.experimental.pallas import tpu as pltpu
from jax.sharding import PartitionSpec as P

MESH = pl.DeviceIdType.MESH
F32 = jnp.float32
BF = jnp.bfloat16
T = 256
Q = 128
N = 256
D = 512
H = 8
W = 64
ROWS = 16
TILES = T // ROWS
GROUP_WIDTH = 2048
EPSILON = 1e-05

NN = (((1,), (0,)), ((), ()))
NT = (((1,), (1,)), ((), ()))


def halves(v):
    hi = v.astype(BF)
    return hi, (v - hi.astype(F32)).astype(BF)


def dot(a, b, dims=NN):
    return lax.dot_general(a, b, dims, preferred_element_type=F32)


def dot3(a, b, dims=NN):
    return dot(a[0], b[0], dims) + (dot(a[0], b[1], dims) + dot(a[1], b[0], dims))


def thirds(v):
    hi = v.astype(BF).astype(F32)
    mid = (v - hi).astype(BF).astype(F32)
    return jnp.concatenate([hi, mid, v - hi - mid, jnp.zeros_like(v)], axis=0)


def sum_thirds(v):
    return v[0:8] + (v[8:16] + v[16:24])


def lanes(v):
    return (v[:, 0:128] + v[:, 128:256]) + (v[:, 256:384] + v[:, 384:512])


def fold(v):
    return v[0:8] + v[8:16]


def tiles(step, count=TILES, init=None, first=0):
    def run(i, carry):
        return step(pl.ds(pl.multiple_of(first + i * ROWS, ROWS), ROWS), carry)

    return lax.fori_loop(0, count, run, 0 if init is None else init, unroll=True)


def iota(shape, dim):
    return lax.broadcasted_iota(jnp.int32, shape, dim)


def body(
    x_in, z_in, raw_in, b_in, c_in, decay_in, bias_in, skip_in, gain_in, og_in,
    outv, hgv, zgv, sgv, bgv, cgv, params,
    xv, zv, ogv, rawv, gainv, decay_s, bias_s, skip_s, bv, cv, c1v,
    a1, a2, a5, gate, dgate, ogg,
    vh, vl, kh, kl, wh, wl, ph, pld, qh, ql, eh, el, uh, ul,
    bh, bl, ch, cl, cth, ctl, bth, btl, c1h, c1l, gh, gl, gth, gtl, oh, ol, th, tl, fh, fl,
    state, other, sh, sl, ap, ap_in, aq, aq_in, rows, rows_in,
    yi, yv, gated, carry_v, sumh, suml, norm, cols, cols1, d1, d2, k1, k2, dy, yqh, yql,
    dv, dx, b_part, c_parts, recv_b, recv_c, small, crh, crl, turnh, turnl,
    local_sem, send_sem, recv_sem,
):
    dp = lax.axis_index("dp")
    ctx = lax.axis_index("ctx")
    place = lax.rem(dp, 4)
    base = dp - place
    right = base + lax.rem(place + 1, 4)
    left = base + lax.rem(place + 3, 4)
    across = base + lax.rem(place + 2, 4)
    early = ctx == 0
    late = ctx == 1

    used = []

    def local(src, dst):
        copy = pltpu.make_async_copy(src, dst, local_sem.at[len(used)])
        used.append(copy)
        return copy

    sent = []

    def remote(src, dst, device):
        k = len(sent)
        sent.append(k)
        return pltpu.make_async_remote_copy(
            src_ref=src, dst_ref=dst, send_sem=send_sem.at[k], recv_sem=recv_sem.at[k],
            device_id=device, device_id_type=MESH,
        )

    to_right, to_left, to_across, to_core = (right, ctx), (left, ctx), (across, ctx), (dp, 1 - ctx)

    barrier = pltpu.get_barrier_semaphore()
    for device in (to_right, to_left, to_across, to_core):
        pl.semaphore_signal(barrier, inc=1, device_id=device, device_id_type=MESH)

    get_heads = [
        local(ref, row)
        for ref, row in ((decay_in, decay_s), (bias_in, bias_s), (skip_in, skip_s))
    ]
    get_raw = local(raw_in, rawv)
    get_gain = local(gain_in, gainv.at[0])
    get_x = local(x_in, xv)
    get_z = local(z_in, zv)
    get_og = local(og_in, ogv)
    get_b = local(b_in, bv.at[pl.ds(0, W)])
    get_c = local(c_in, cv.at[pl.ds(0, W)])
    for copy in used:
        copy.start()
    def per_head(ref, width):
        row = iota((H, width), 0)
        value = jnp.full((H, width), ref[0], F32)
        for h in range(1, H):
            value = jnp.where(row == h, ref[h], value)
        return value

    get_raw.wait()
    for copy in get_heads:
        copy.wait()
    speed = jnp.exp(per_head(decay_s, T))
    pre = rawv[...] + per_head(bias_s, T)
    step = jnp.maximum(pre, 0.0) + jnp.log1p(jnp.exp(-jnp.abs(pre)))
    rate = -speed * step
    src, dst = iota((T, T), 0), iota((T, T), 1)
    upto = jnp.where((src <= dst) & (src // Q == dst // Q), 1.0, 0.0).astype(BF)
    run = sum_thirds(dot(thirds(rate).astype(BF), upto))

    pl.semaphore_wait(barrier, 4)

    lo, hi = slice(0, Q), slice(Q, T)

    def gather(mine, group, j):
        part = pl.ds(j * Q, Q)
        return [
            remote(mine.at[:, part], group.at[pl.ds(k * W, W), part], device)
            for k, device in ((3, to_across), (1, to_right), (2, to_left))
        ]

    def begin(copies):
        for copy in copies:
            copy.start()

    def arrive(copies):
        for copy in copies:
            copy.wait_recv()

    b_copies = [gather(b_in, bv, j) for j in range(2)]
    c_copies = [gather(c_in, cv, j) for j in range(2)]
    begin(b_copies[0] + c_copies[0])

    total0 = run[:, Q - 1:Q]
    total1 = run[:, T - 1:T]
    position = iota((H, T), 1)
    block1 = position >= Q
    centre = 0.5 * jnp.where(block1, total1, total0)
    scale1 = jnp.exp(run - centre)
    scale2 = step * jnp.exp(centre - run)
    since_start = jnp.where(block1, run + total0, run)
    to_end = jnp.where(block1, total1 - run, total0 - run + total1)
    scale5 = jnp.where(early, step, 1.0) * jnp.exp(jnp.where(early, to_end, since_start))
    stacked = jnp.concatenate(
        [thirds(scale1), thirds(scale2), thirds(scale5), jnp.zeros((32, T), F32)], axis=0
    ).T.astype(BF)
    row, col = iota((128, D), 0), iota((128, D), 1)
    same = (row % 8 == col // W) & (row % 32 < 24)
    for k, ref in enumerate((a1, a2, a5)):
        spread = jnp.where(same & (row // 32 == k), 1.0, 0.0).astype(BF)
        ref[...] = dot(stacked, spread)
    begin(b_copies[1] + c_copies[1])

    own = iota((H, D), 0) == iota((H, D), 1) // W
    kappa = jnp.sum(
        jnp.where(own, jnp.exp(0.5 * (total0 + total1)), 0.0), axis=0, keepdims=True
    )
    skip_row = jnp.sum(jnp.where(own, per_head(skip_s, D), 0.0), axis=0, keepdims=True)

    get_gain.wait()
    get_x.wait()
    get_z.wait()
    get_og.wait()

    def prepare(r, carry):
        z = zv[r]
        sig = 1.0 / (1.0 + jnp.exp(-z))
        g = z * sig
        gate[r] = g
        dgate[r] = sig * (1.0 + z * (1.0 - sig))
        scaled = ogv[r] * gainv[...]
        ogg[r] = scaled
        x = xv[r]
        p = scaled * g
        vh[r], vl[r] = halves(a2[r] * x)
        ph[r], pld[r] = halves(a1[r] * p)
        w = a5[r] * jnp.where(early, x, p)
        ap[r] = w
        wh[r], wl[r] = halves(w)
        return carry

    tiles(prepare)

    ap_out = remote(ap, ap_in, to_core)

    @pl.when(late)
    def _():
        ap_out.start()

    def prepare0(r, carry):
        kh[r], kl[r] = halves((a2[r] * xv[r]) * kappa)
        return carry

    tiles(prepare0, TILES // 2)

    def score_grad(out, far, near):
        out[0:Q, 0:Q] = dot3((vh[0:Q], vl[0:Q]), (far[0:Q], near[0:Q]), NT)
        out[0:Q, Q:T] = dot3((kh[...], kl[...]), (far[Q:T], near[Q:T]), NT)
        out[Q:T, Q:T] = dot3((vh[Q:T], vl[Q:T]), (far[Q:T], near[Q:T]), NT)

    score_grad(d1, ph, pld)

    low = src >= dst
    high = src <= dst
    get_b.wait()
    get_c.wait()
    arrive(b_copies[0])
    bh[:, lo], bl[:, lo] = halves(bv[:, lo])
    arrive(c_copies[0])
    cth[lo], ctl[lo] = halves(cv[:, lo].T)
    g0 = dot3((cth[lo], ctl[lo]), (bh[:, lo], bl[:, lo]))
    gh[lo, lo], gl[lo, lo] = halves(jnp.where(low[lo, lo], g0, 0.0))
    for k in range(2):
        part = pl.ds(k * 256, 256)
        yi[lo, part] = dot3((gh[lo, lo], gl[lo, lo]), (vh[lo, part], vl[lo, part]))

    def mix(r, y):
        yv[r] = y
        mixed = y + skip_row * xv[r]
        g = mixed * gate[r]
        gated[r] = g
        sumh[r, 0:128], suml[r, 0:128] = halves(lanes(g * g))
        sumh[r, 128:256], suml[r, 128:256] = halves(lanes(g * ogg[r]))
        q = g * gate[r]
        qh[r], ql[r] = halves(a1[r] * q)
        return q

    pick = jnp.where(iota((H, 256), 0) == iota((H, 256), 1) // 128, 1.0, 0.0).astype(BF)
    norm_out = [
        [
            remote(norm.at[j, 0], norm.at[j, 1 + k], device)
            for k, device in enumerate((to_across, to_right, to_left))
        ]
        for j in range(2)
    ]

    def send_sums(j, block):
        norm[j, 0] = dot(pick, sumh[block], NT) + dot(pick, suml[block], NT)
        begin(norm_out[j])

    def mix_early(j, block):
        def go(r, carry):
            mix(r, a1[r] * yi[r])
            return carry

        tiles(go, TILES // 2, first=j * Q)
        send_sums(j, block)

    @pl.when(early)
    def _():
        mix_early(0, lo)

    def scatter(parts, landing):
        return [
            remote(parts.at[pl.ds(k * W, W)], landing.at[pl.ds(j * W, W)], device)
            for j, (k, device) in enumerate(((3, to_across), (2, to_right), (1, to_left)))
        ]

    b_sums = scatter(b_part, recv_b)
    c_sums = [scatter(c_parts.at[j], recv_c.at[j]) for j in range(2)]

    def c_grad(j, grad):
        th[...], tl[...] = halves(jnp.where(high, grad[...], 0.0))
        return dot3((bh[...], bl[...]), (th[...], tl[...]))

    state_out = [remote(state.at[k], other.at[k], to_core) for k in range(4)]
    arrive(b_copies[1])
    bh[:, hi], bl[:, hi] = halves(bv[:, hi])

    @pl.when(early)
    def _():
        for k in range(4):
            part = slice(k * W, (k + 1) * W)
            state[k] = dot3((bh[part], bl[part]), (wh[...], wl[...]))
            state_out[k].start()

    c_parts[0] = c_grad(0, d1)
    arrive(c_copies[1])

    @pl.when(early)
    def _():
        begin(c_sums[0])

    cth[hi], ctl[hi] = halves(cv[:, hi].T)
    c_out = remote(cv, c1v, to_core)

    @pl.when(late)
    def _():
        c_out.start()

    g1 = dot3((cth[hi], ctl[hi]), (bh[...], bl[...]))
    gh[hi], gl[hi] = halves(jnp.where(low[hi], g1, 0.0))
    for k in range(2):
        part = pl.ds(k * 256, 256)
        yi[hi, part] = dot3(
            (gh[hi], gl[hi]),
            (
                jnp.concatenate([kh[:, part], vh[hi, part]], axis=0),
                jnp.concatenate([kl[:, part], vl[hi, part]], axis=0),
            ),
        )

    aq_out = remote(aq, aq_in, to_core)

    @pl.when(early)
    def _():
        mix_early(1, hi)

    @pl.when(late)
    def _():
        arrive(state_out)
        for k in range(4):
            sh[k * W:(k + 1) * W], sl[k * W:(k + 1) * W] = halves(other[k])
        for k in range(2):
            part = pl.ds(k * 256, 256)
            carry_v[:, part] = dot3((cth[...], ctl[...]), (sh[:, part], sl[:, part]))

        def go(r, carry):
            w = a5[r] * mix(r, a1[r] * yi[r] + a5[r] * carry_v[r])
            aq[r] = w
            eh[r], el[r] = halves(w)
            return carry

        tiles(go, TILES // 2)
        send_sums(0, lo)
        tiles(go, TILES // 2, first=Q)
        send_sums(1, hi)
        aq_out.start()
        c_parts[0] += dot3((sh[...], sl[...]), (wh[...], wl[...]), NT)
        begin(c_sums[0])

    score_grad(d2, qh, ql)
    ch[...], cl[...] = halves(cv[...])

    @pl.when(early)
    def _():
        c_parts[1] = c_grad(1, d2)
        begin(c_sums[1])
        ap_out.wait_recv()
        fh[...], fl[...] = halves(ap_in[...])
        k1[...] = dot3((wh[...], wl[...]), (fh[...], fl[...]), NT)
        bth[...], btl[...] = halves(bv[...].T)
        c_out.wait_recv()
        c1h[...], c1l[...] = halves(c1v[...])
        crh[...], crl[...] = halves(dot3((bth[...], btl[...]), (c1h[...], c1l[...])))
        aq_out.wait_recv()
        oh[...], ol[...] = halves(aq_in[...])
        k2[...] = dot3((wh[...], wl[...]), (oh[...], ol[...]), NT)

    @pl.when(late)
    def _():
        c_parts[1] = c_grad(1, d2) + dot3((sh[...], sl[...]), (eh[...], el[...]), NT)
        begin(c_sums[1])

    for rows_of, cols_of in ((lo, lo), (hi, lo), (hi, hi)):
        turnh[cols_of, rows_of] = gh[rows_of, cols_of].astype(F32).T.astype(BF)
        turnl[cols_of, rows_of] = gl[rows_of, cols_of].astype(F32).T.astype(BF)

    def factors(j, block):
        arrive(norm_out[j])
        sums = (norm[j, 0] + norm[j, 1]) + (norm[j, 2] + norm[j, 3])
        inv = lax.rsqrt(sums[0:1] * (1.0 / GROUP_WIDTH) + EPSILON)
        slope = inv * inv * inv * sums[1:2] * (1.0 / GROUP_WIDTH)
        rows[:, block] = jnp.where(iota((8, Q), 0) == 0, inv, slope)

    for j, block in enumerate((lo, hi)):
        factors(j, block)
    th[...], tl[...] = halves(jnp.where(high, rows[0:1] * d1[...] - rows[1:2] * d2[...], 0.0))
    rows_out = remote(rows, rows_in, to_core)
    b_grad = dot3((ch[...], cl[...]), (th[...], tl[...]), NT)

    @pl.when(late)
    def _():
        rows_out.start()
        b_part[...] = b_grad
        begin(b_sums)

    @pl.when(early)
    def _():
        rows_out.wait_recv()
        gth[...], gtl[...] = halves(rows_in[0:1] * k1[...] - rows_in[1:2] * k2[...])
        b_part[...] = b_grad + dot3((c1h[...], c1l[...]), (gth[...], gtl[...]), NT)
        begin(b_sums)

    lead = iota((128, T), 0)
    cols[...] = jnp.where(lead == 0, rows[0:1], jnp.where(lead == 1, rows[1:2], 0.0)).T

    def finish(r, carry):
        gain_sum, skip_sum = carry
        inv = cols[r, 0:1]
        k = cols[r, 1:2]
        g = gated[r]
        x = xv[r]
        y = yv[r]
        normed = g * inv
        outv[r] = normed * gainv[...]
        grad = ogg[r] * inv - g * k
        zgv[r] = grad * (y + skip_row * x) * dgate[r]
        d = grad * gate[r]
        dy[r] = d
        uh[r], ul[r] = halves(a1[r] * d)
        yqh[r], yql[r] = halves(d * y)
        return gain_sum + fold(ogv[r] * normed), skip_sum + fold(d * x)

    zero = jnp.zeros((8, D), F32)
    gain_sum, skip_sum = tiles(finish, init=(zero, zero))

    for k in range(2):
        part = pl.ds(k * 256, 256)
        dv[0:Q, part] = dot3((turnh[lo, lo], turnl[lo, lo]), (uh[0:Q, part], ul[0:Q, part])) + kappa[
            :, k * 256:(k + 1) * 256
        ] * dot3((turnh[lo, hi], turnl[lo, hi]), (uh[Q:T, part], ul[Q:T, part]))
        dv[Q:T, part] = dot3((turnh[hi, hi], turnl[hi, hi]), (uh[Q:T, part], ul[Q:T, part]))

    small[0:16] = jnp.zeros((16, D), F32)

    def x_grad(r, f):
        hgv[r] = f + skip_row * dy[r]
        uh[r], ul[r] = halves(f * xv[r])

    @pl.when(early)
    def _():
        cols1[...] = jnp.where(lead == 0, rows_in[0:1], jnp.where(lead == 1, rows_in[1:2], 0.0)).T

        def later(r, carry):
            eh[r], el[r] = halves(cols1[r, 0:1] * ap_in[r] - cols1[r, 1:2] * aq_in[r])
            return carry

        tiles(later)
        for k in range(2):
            part = pl.ds(k * 256, 256)
            dx[:, part] = dot3((crh[...], crl[...]), (eh[:, part], el[:, part]))

        def go(r, carry):
            tail = a5[r] * dx[r]
            x_grad(r, a2[r] * dv[r] + tail)
            return carry + fold(tail * xv[r])

        small[8:16] = tiles(go, init=zero)

    @pl.when(late)
    def _():
        def go(r, carry):
            x_grad(r, a2[r] * dv[r])
            return carry

        tiles(go)


    heads = jnp.where(own, 1.0, 0.0).astype(BF)
    y_sum = dot(heads, yqh[...], NT) + dot(heads, yql[...], NT)
    x_sum = dot(heads, uh[...], NT) + dot(heads, ul[...], NT)
    from_end = jnp.sum(
        jnp.where(own, jnp.sum(small[8:16], axis=0, keepdims=True), 0.0), axis=1, keepdims=True
    )
    onward = jnp.where(low, 1.0, 0.0).astype(BF)
    rate_grad = sum_thirds(dot(thirds(y_sum - x_sum).astype(BF), onward)) + from_end
    step_grad = (x_sum / step - speed * rate_grad) * (1.0 / (1.0 + jnp.exp(-pre)))
    sgv[...] = step_grad

    def as_row(column):
        hit = iota((H, D), 0) == iota((H, D), 1)
        return jnp.sum(jnp.where(hit, column, 0.0), axis=0, keepdims=True)

    skip_column = jnp.sum(
        jnp.where(own, jnp.sum(skip_sum, axis=0, keepdims=True), 0.0), axis=1, keepdims=True
    )
    small[0:1] = jnp.sum(gain_sum, axis=0, keepdims=True)
    small[1:2] = as_row(jnp.sum(rate_grad * rate, axis=1, keepdims=True))
    small[2:3] = as_row(jnp.sum(step_grad, axis=1, keepdims=True))
    small[3:4] = as_row(skip_column)
    small_out = remote(small.at[pl.ds(0, 8)], small.at[pl.ds(16, 8)], to_core)
    small_out.start()

    arrive([small_out] + c_sums[0] + c_sums[1])
    params[...] = small[0:8] + small[16:24]
    c_total = [
        c_parts[j, 0:W] + (recv_c[j, 0:W] + (recv_c[j, W:2 * W] + recv_c[j, 2 * W:3 * W]))
        for j in range(2)
    ]
    cgv[...] = rows[0:1] * c_total[0] - rows[1:2] * c_total[1]
    arrive(b_sums)
    bgv[...] = b_part[0:W] + (recv_b[0:W] + (recv_b[W:2 * W] + recv_b[2 * W:3 * W]))

    @pl.when(early)
    def _():
        for copy in state_out:
            copy.wait_send()

    @pl.when(late)
    def _():
        for copy in (ap_out, aq_out, c_out, rows_out):
            copy.wait_send()

    for copies in (*b_copies, *c_copies, *norm_out, *c_sums, b_sums, [small_out]):
        for copy in copies:
            copy.wait_send()


def place_results(*refs):
    results, outputs, sem = refs[:7], refs[7:17], refs[17]
    out_o, hg_o, zg_o, sg_o, bg_o, cg_o, decay_o, bias_o, skip_o, gain_o = outputs
    rows = results[6]
    copies = [
        pltpu.make_async_copy(rows.at[0] if ref is gain_o else results[k], ref, sem.at[k])
        for k, ref in enumerate((out_o, hg_o, zg_o, sg_o, bg_o, cg_o, gain_o))
    ]
    for copy in copies:
        copy.start()
    for k, ref in enumerate((decay_o, bias_o, skip_o)):
        ref[...] = rows[1 + k, 0:H]
    for copy in copies:
        copy.wait()


def shards(*args):
    def f32(*shape):
        return jax.ShapeDtypeStruct(shape, F32)

    def vm(*shape):
        return pltpu.VMEM(shape, F32)

    def vb(*shape):
        return pltpu.VMEM(shape, BF)

    in_hbm = pl.BlockSpec(memory_space=pltpu.HBM)
    in_vmem = pl.BlockSpec(memory_space=pltpu.VMEM)
    scalars = pltpu.SMEM((H,), F32)
    wide, narrow = vm(T, D), vb(T, D)
    square, thin = vm(T, T), vb(T, T)
    scratch = [wide] * 3 + [vm(H, T), vm(1, D)] + [scalars] * 3 + [square] * 3
    scratch += [wide] * 6
    scratch += [narrow] * 2 + [vb(Q, D)] * 2 + [narrow] * 10
    scratch += [thin] * 14 + [narrow] * 2 + [thin] * 2 + [narrow] * 2
    scratch += [vm(4, W, D)] * 2 + [narrow] * 2 + [wide] * 4 + [vm(8, T)] * 2
    scratch += [wide] * 4 + [thin] * 2 + [vm(2, 4, 8, Q), vm(T, 128), vm(T, 128)]
    scratch += [square] * 4 + [wide] + [narrow] * 2
    scratch += [wide] * 2 + [square, vm(2, N, T), vm(3 * W, T), vm(2, 3 * W, T), vm(32, D)] + [thin] * 4
    scratch += [
        pltpu.SemaphoreType.DMA((10,)),
        pltpu.SemaphoreType.DMA((36,)),
        pltpu.SemaphoreType.DMA((36,)),
    ]
    args = [pltpu.with_memory_space_constraint(array, pltpu.HBM) for array in args]
    results = pl.pallas_call(
        body,
        out_shape=[f32(T, D), f32(T, D), f32(T, D), f32(H, T), f32(W, T), f32(W, T), f32(8, D)],
        in_specs=[in_hbm] * 10,
        out_specs=[in_vmem] * 7,
        scratch_shapes=scratch,
        compiler_params=pltpu.CompilerParams(
            collective_id=0, has_side_effects=True, vmem_limit_bytes=40 * 1024 * 1024
        ),
        name="layer",
    )(*args)
    return pl.pallas_call(
        place_results,
        out_shape=[
            f32(T, D), f32(T, D), f32(T, D), f32(H, T), f32(W, T), f32(W, T),
            f32(H), f32(H), f32(H), f32(D),
        ],
        in_specs=[in_vmem] * 7,
        out_specs=[in_hbm] * 6 + [in_vmem] * 3 + [in_hbm],
        scratch_shapes=[pltpu.SemaphoreType.DMA((7,))],
        compiler_params=pltpu.CompilerParams(vmem_limit_bytes=16 * 1024 * 1024),
        name="place_results",
    )(*results)


def solution(mesh):
    rows, cols = P("ctx", "dp"), P("dp", "ctx")
    heads = P("dp")
    return jax.shard_map(
        shards,
        mesh=mesh,
        in_specs=(rows, rows, cols, cols, cols, heads, heads, heads, heads, rows),
        out_specs=(rows, rows, rows, cols, cols, cols, heads, heads, heads, heads),
        check_vma=False,
    )
```

```python
import jax
import jax.numpy as jnp
from jax import lax
from jax.experimental import pallas as pl
from jax.experimental.pallas import tpu as pltpu
from jax.sharding import PartitionSpec as P

MESH = pl.DeviceIdType.MESH
F32 = jnp.float32
BF = jnp.bfloat16
T = 256
Q = 128
N = 256
D = 512
H = 8
W = 64
ROWS = 16
TILES = T // ROWS
GROUP_WIDTH = 2048
EPSILON = 1e-05

NN = (((1,), (0,)), ((), ()))
NT = (((1,), (1,)), ((), ()))


def halves(v):
    hi = v.astype(BF)
    return hi, (v - hi.astype(F32)).astype(BF)


def dot(a, b, dims=NN):
    return lax.dot_general(a, b, dims, preferred_element_type=F32)


def dot3(a, b, dims=NN):
    return dot(a[0], b[0], dims) + (dot(a[0], b[1], dims) + dot(a[1], b[0], dims))


def thirds(v):
    hi = v.astype(BF).astype(F32)
    mid = (v - hi).astype(BF).astype(F32)
    return jnp.concatenate([hi, mid, v - hi - mid, jnp.zeros_like(v)], axis=0)


def sum_thirds(v):
    return v[0:8] + (v[8:16] + v[16:24])


def lanes(v):
    return (v[:, 0:128] + v[:, 128:256]) + (v[:, 256:384] + v[:, 384:512])


def fold(v):
    return v[0:8] + v[8:16]


def tiles(step, count=TILES, init=None, first=0):
    def run(i, carry):
        return step(pl.ds(pl.multiple_of(first + i * ROWS, ROWS), ROWS), carry)

    return lax.fori_loop(0, count, run, 0 if init is None else init, unroll=True)


def iota(shape, dim):
    return lax.broadcasted_iota(jnp.int32, shape, dim)


def body(
    x_in, z_in, raw_in, b_in, c_in, decay_in, bias_in, skip_in, gain_in, og_in,
    outv, hgv, zgv, sgv, bgv, cgv, params,
    xv, zv, ogv, rawv, gainv, decay_s, bias_s, skip_s, bv, cv, c1v,
    a1, a2, a5, gate, dgate, ogg,
    vh, vl, kh, kl, wh, wl, ph, pld, qh, ql, eh, el, uh, ul,
    bh, bl, ch, cl, cth, ctl, bth, btl, c1h, c1l, gh, gl, gth, gtl, oh, ol, th, tl, fh, fl,
    state, other, sh, sl, ap, ap_in, aq, aq_in, rows, rows_in,
    yi, yv, gated, carry_v, sumh, suml, norm, cols, d1, d2, k1, k2, dy, yqh, yql,
    dv, dx, b_part, c_parts, recv_b, recv_c, small, crs, turnh, turnl,
    local_sem, send_sem, recv_sem,
):
    dp = lax.axis_index("dp")
    ctx = lax.axis_index("ctx")
    place = lax.rem(dp, 4)
    base = dp - place
    right = base + lax.rem(place + 1, 4)
    left = base + lax.rem(place + 3, 4)
    across = base + lax.rem(place + 2, 4)
    early = ctx == 0
    late = ctx == 1

    used = []

    def local(src, dst):
        copy = pltpu.make_async_copy(src, dst, local_sem.at[len(used)])
        used.append(copy)
        return copy

    sent = []

    def remote(src, dst, device):
        k = len(sent)
        sent.append(k)
        return pltpu.make_async_remote_copy(
            src_ref=src, dst_ref=dst, send_sem=send_sem.at[k], recv_sem=recv_sem.at[k],
            device_id=device, device_id_type=MESH,
        )

    to_right, to_left, to_across, to_core = (right, ctx), (left, ctx), (across, ctx), (dp, 1 - ctx)

    barrier = pltpu.get_barrier_semaphore()
    for device in (to_right, to_left, to_across, to_core):
        pl.semaphore_signal(barrier, inc=1, device_id=device, device_id_type=MESH)

    get_heads = [
        local(ref, row)
        for ref, row in ((decay_in, decay_s), (bias_in, bias_s), (skip_in, skip_s))
    ]
    get_raw = local(raw_in, rawv)
    get_gain = local(gain_in, gainv.at[0])
    get_x = local(x_in, xv)
    get_z = local(z_in, zv)
    get_og = local(og_in, ogv)
    get_b = local(b_in, bv.at[pl.ds(0, W)])
    get_c = local(c_in, cv.at[pl.ds(0, W)])
    for copy in used:
        copy.start()
    def per_head(ref, width):
        row = iota((H, width), 0)
        value = jnp.full((H, width), ref[0], F32)
        for h in range(1, H):
            value = jnp.where(row == h, ref[h], value)
        return value

    get_raw.wait()
    for copy in get_heads:
        copy.wait()
    speed = jnp.exp(per_head(decay_s, T))
    pre = rawv[...] + per_head(bias_s, T)
    step = jnp.maximum(pre, 0.0) + jnp.log1p(jnp.exp(-jnp.abs(pre)))
    rate = -speed * step
    src, dst = iota((T, T), 0), iota((T, T), 1)
    upto = jnp.where((src <= dst) & (src // Q == dst // Q), 1.0, 0.0).astype(BF)
    run = sum_thirds(dot(thirds(rate).astype(BF), upto))

    pl.semaphore_wait(barrier, 4)

    lo, hi = slice(0, Q), slice(Q, T)

    def gather(mine, group, j):
        part = pl.ds(j * Q, Q)
        return [
            remote(mine.at[:, part], group.at[pl.ds(k * W, W), part], device)
            for k, device in ((3, to_across), (1, to_right), (2, to_left))
        ]

    def begin(copies):
        for copy in copies:
            copy.start()

    def arrive(copies):
        for copy in copies:
            copy.wait_recv()

    b_copies = [gather(b_in, bv, j) for j in range(2)]
    c_copies = [gather(c_in, cv, j) for j in range(2)]
    begin(b_copies[0] + b_copies[1])

    total0 = run[:, Q - 1:Q]
    total1 = run[:, T - 1:T]
    position = iota((H, T), 1)
    block1 = position >= Q
    centre = 0.5 * jnp.where(block1, total1, total0)
    scale1 = jnp.exp(run - centre)
    scale2 = step * jnp.exp(centre - run)
    since_start = jnp.where(block1, run + total0, run)
    to_end = jnp.where(block1, total1 - run, total0 - run + total1)
    scale5 = jnp.where(early, step, 1.0) * jnp.exp(jnp.where(early, to_end, since_start))
    stacked = jnp.concatenate(
        [thirds(scale1), thirds(scale2), thirds(scale5), jnp.zeros((32, T), F32)], axis=0
    ).T.astype(BF)
    row, col = iota((128, D), 0), iota((128, D), 1)
    same = (row % 8 == col // W) & (row % 32 < 24)
    for k, ref in enumerate((a1, a2, a5)):
        spread = jnp.where(same & (row // 32 == k), 1.0, 0.0).astype(BF)
        ref[...] = dot(stacked, spread)
    begin(c_copies[0] + c_copies[1])

    own = iota((H, D), 0) == iota((H, D), 1) // W
    kappa = jnp.sum(
        jnp.where(own, jnp.exp(0.5 * (total0 + total1)), 0.0), axis=0, keepdims=True
    )
    skip_row = jnp.sum(jnp.where(own, per_head(skip_s, D), 0.0), axis=0, keepdims=True)

    get_gain.wait()
    get_x.wait()
    get_z.wait()
    get_og.wait()

    def prepare(r, carry):
        z = zv[r]
        sig = 1.0 / (1.0 + jnp.exp(-z))
        g = z * sig
        gate[r] = g
        dgate[r] = sig * (1.0 + z * (1.0 - sig))
        scaled = ogv[r] * gainv[...]
        ogg[r] = scaled
        x = xv[r]
        p = scaled * g
        vh[r], vl[r] = halves(a2[r] * x)
        ph[r], pld[r] = halves(a1[r] * p)
        w = a5[r] * jnp.where(early, x, p)
        ap[r] = w
        wh[r], wl[r] = halves(w)
        return carry

    tiles(prepare)

    ap_out = remote(ap, ap_in, to_core)

    @pl.when(late)
    def _():
        ap_out.start()

    def prepare0(r, carry):
        kh[r], kl[r] = halves((a2[r] * xv[r]) * kappa)
        return carry

    tiles(prepare0, TILES // 2)

    def score_grad(out, far, near):
        out[0:Q, 0:Q] = dot3((vh[0:Q], vl[0:Q]), (far[0:Q], near[0:Q]), NT)
        out[0:Q, Q:T] = dot3((kh[...], kl[...]), (far[Q:T], near[Q:T]), NT)
        out[Q:T, Q:T] = dot3((vh[Q:T], vl[Q:T]), (far[Q:T], near[Q:T]), NT)

    score_grad(d1, ph, pld)

    low = src >= dst
    high = src <= dst
    get_b.wait()
    get_c.wait()
    arrive(b_copies[0] + b_copies[1])
    bh[...], bl[...] = halves(bv[...])

    state_out = [remote(state.at[k], other.at[k], to_core) for k in range(4)]

    @pl.when(early)
    def _():
        for k in range(4):
            part = slice(k * W, (k + 1) * W)
            state[k] = dot3((bh[part], bl[part]), (wh[...], wl[...]))
            state_out[k].start()

    arrive(c_copies[0])
    cth[lo], ctl[lo] = halves(cv[:, lo].T)
    g0 = dot3((cth[lo], ctl[lo]), (bh[:, lo], bl[:, lo]))
    gh[lo, lo], gl[lo, lo] = halves(jnp.where(low[lo, lo], g0, 0.0))
    for k in range(2):
        part = pl.ds(k * 256, 256)
        yi[lo, part] = dot3((gh[lo, lo], gl[lo, lo]), (vh[lo, part], vl[lo, part]))

    def mix(r, y):
        yv[r] = y
        mixed = y + skip_row * xv[r]
        g = mixed * gate[r]
        gated[r] = g
        sumh[r, 0:128], suml[r, 0:128] = halves(lanes(g * g))
        sumh[r, 128:256], suml[r, 128:256] = halves(lanes(g * ogg[r]))
        q = g * gate[r]
        qh[r], ql[r] = halves(a1[r] * q)
        return q

    pick = jnp.where(iota((H, 256), 0) == iota((H, 256), 1) // 128, 1.0, 0.0).astype(BF)
    norm_out = [
        [
            remote(norm.at[j, 0], norm.at[j, 1 + k], device)
            for k, device in enumerate((to_across, to_right, to_left))
        ]
        for j in range(2)
    ]

    def send_sums(j, block):
        norm[j, 0] = dot(pick, sumh[block], NT) + dot(pick, suml[block], NT)
        begin(norm_out[j])

    def mix_early(j, block):
        def go(r, carry):
            mix(r, a1[r] * yi[r])
            return carry

        tiles(go, TILES // 2, first=j * Q)
        send_sums(j, block)

    @pl.when(early)
    def _():
        mix_early(0, lo)

    def scatter(parts, landing):
        return [
            remote(parts.at[pl.ds(k * W, W)], landing.at[pl.ds(j * W, W)], device)
            for j, (k, device) in enumerate(((3, to_across), (2, to_right), (1, to_left)))
        ]

    b_sums = scatter(b_part, recv_b)
    c_sums = [scatter(c_parts.at[j], recv_c.at[j]) for j in range(2)]

    def c_grad(j, grad):
        th[...], tl[...] = halves(jnp.where(high, grad[...], 0.0))
        return dot3((bh[...], bl[...]), (th[...], tl[...]))

    c_parts[0] = c_grad(0, d1)
    arrive(c_copies[1])

    @pl.when(early)
    def _():
        begin(c_sums[0])

    cth[hi], ctl[hi] = halves(cv[:, hi].T)
    c_out = remote(cv, c1v, to_core)

    @pl.when(late)
    def _():
        c_out.start()

    g1 = dot3((cth[hi], ctl[hi]), (bh[...], bl[...]))
    gh[hi], gl[hi] = halves(jnp.where(low[hi], g1, 0.0))
    for k in range(2):
        part = pl.ds(k * 256, 256)
        yi[hi, part] = dot3(
            (gh[hi], gl[hi]),
            (
                jnp.concatenate([kh[:, part], vh[hi, part]], axis=0),
                jnp.concatenate([kl[:, part], vl[hi, part]], axis=0),
            ),
        )

    aq_out = remote(aq, aq_in, to_core)

    @pl.when(early)
    def _():
        mix_early(1, hi)

    @pl.when(late)
    def _():
        arrive(state_out)
        for k in range(4):
            sh[k * W:(k + 1) * W], sl[k * W:(k + 1) * W] = halves(other[k])
        for k in range(2):
            part = pl.ds(k * 256, 256)
            carry_v[:, part] = dot3((cth[...], ctl[...]), (sh[:, part], sl[:, part]))

        def go(r, carry):
            w = a5[r] * mix(r, a1[r] * yi[r] + a5[r] * carry_v[r])
            aq[r] = w
            eh[r], el[r] = halves(w)
            return carry

        tiles(go, TILES // 2)
        send_sums(0, lo)
        tiles(go, TILES // 2, first=Q)
        send_sums(1, hi)
        aq_out.start()
        c_parts[0] += dot3((sh[...], sl[...]), (wh[...], wl[...]), NT)
        begin(c_sums[0])

    score_grad(d2, qh, ql)
    ch[...], cl[...] = halves(cv[...])

    @pl.when(early)
    def _():
        c_parts[1] = c_grad(1, d2)
        begin(c_sums[1])
        ap_out.wait_recv()
        fh[...], fl[...] = halves(ap_in[...])
        k1[...] = dot3((wh[...], wl[...]), (fh[...], fl[...]), NT)
        bth[...], btl[...] = halves(bv[...].T)
        c_out.wait_recv()
        c1h[...], c1l[...] = halves(c1v[...])
        crs[...] = dot3((bth[...], btl[...]), (c1h[...], c1l[...]))
        aq_out.wait_recv()
        oh[...], ol[...] = halves(aq_in[...])
        k2[...] = dot3((wh[...], wl[...]), (oh[...], ol[...]), NT)

    @pl.when(late)
    def _():
        c_parts[1] = c_grad(1, d2) + dot3((sh[...], sl[...]), (eh[...], el[...]), NT)
        begin(c_sums[1])

    heads = jnp.where(own, 1.0, 0.0).astype(BF)

    def weigh(r, carry):
        gy = gate[r] * yv[r]
        uh[r], ul[r] = halves(ogg[r] * gy)
        yqh[r], yql[r] = halves(gated[r] * gy)
        return carry

    tiles(weigh)
    y_sums = [
        dot(heads, high_part[...], NT) + dot(heads, low_part[...], NT)
        for high_part, low_part in ((uh, ul), (yqh, yql))
    ]
    for rows_of, cols_of in ((lo, lo), (hi, lo), (hi, hi)):
        turnh[cols_of, rows_of] = gh[rows_of, cols_of].astype(F32).T.astype(BF)
        turnl[cols_of, rows_of] = gl[rows_of, cols_of].astype(F32).T.astype(BF)

    def factors(j, block):
        arrive(norm_out[j])
        sums = (norm[j, 0] + norm[j, 1]) + (norm[j, 2] + norm[j, 3])
        inv = lax.rsqrt(sums[0:1] * (1.0 / GROUP_WIDTH) + EPSILON)
        slope = inv * inv * inv * sums[1:2] * (1.0 / GROUP_WIDTH)
        rows[:, block] = jnp.where(iota((8, Q), 0) == 0, inv, slope)

    for j, block in enumerate((lo, hi)):
        factors(j, block)
    th[...], tl[...] = halves(jnp.where(high, rows[0:1] * d1[...] - rows[1:2] * d2[...], 0.0))
    rows_out = remote(rows, rows_in, to_core)
    b_grad = dot3((ch[...], cl[...]), (th[...], tl[...]), NT)

    @pl.when(late)
    def _():
        rows_out.start()
        b_part[...] = b_grad
        begin(b_sums)

    @pl.when(early)
    def _():
        rows_out.wait_recv()
        gth[...], gtl[...] = halves(rows_in[0:1] * k1[...] - rows_in[1:2] * k2[...])
        b_part[...] = b_grad + dot3((c1h[...], c1l[...]), (gth[...], gtl[...]), NT)
        begin(b_sums)

    lead = iota((128, T), 0)
    cols[...] = jnp.where(lead == 0, rows[0:1], jnp.where(lead == 1, rows[1:2], 0.0)).T

    def finish(r, carry):
        gain_sum, skip_sum = carry
        inv = cols[r, 0:1]
        k = cols[r, 1:2]
        g = gated[r]
        x = xv[r]
        y = yv[r]
        normed = g * inv
        outv[r] = normed * gainv[...]
        grad = ogg[r] * inv - g * k
        zgv[r] = grad * (y + skip_row * x) * dgate[r]
        d = grad * gate[r]
        dy[r] = d
        uh[r], ul[r] = halves(a1[r] * d)
        return gain_sum + fold(ogv[r] * normed), skip_sum + fold(d * x)

    zero = jnp.zeros((8, D), F32)
    gain_sum, skip_sum = tiles(finish, init=(zero, zero))

    for k in range(2):
        part = pl.ds(k * 256, 256)
        dv[0:Q, part] = dot3((turnh[lo, lo], turnl[lo, lo]), (uh[0:Q, part], ul[0:Q, part])) + kappa[
            :, k * 256:(k + 1) * 256
        ] * dot3((turnh[lo, hi], turnl[lo, hi]), (uh[Q:T, part], ul[Q:T, part]))
        dv[Q:T, part] = dot3((turnh[hi, hi], turnl[hi, hi]), (uh[Q:T, part], ul[Q:T, part]))

    small[0:16] = jnp.zeros((16, D), F32)

    def x_grad(r, f):
        hgv[r] = f + skip_row * dy[r]
        uh[r], ul[r] = halves(f * xv[r])

    @pl.when(early)
    def _():
        scaled = [halves(crs[...] * rows_in[0:1]), halves(crs[...] * -rows_in[1:2])]
        cross = [jnp.concatenate([scaled[0][k], scaled[1][k]], axis=1) for k in range(2)]
        for k in range(2):
            part = pl.ds(k * 256, 256)
            dx[:, part] = dot3(
                cross,
                (
                    jnp.concatenate([fh[:, part], oh[:, part]], axis=0),
                    jnp.concatenate([fl[:, part], ol[:, part]], axis=0),
                ),
            )

        def go(r, carry):
            tail = a5[r] * dx[r]
            x_grad(r, a2[r] * dv[r] + tail)
            return carry + fold(tail * xv[r])

        small[8:16] = tiles(go, init=zero)

    @pl.when(late)
    def _():
        def go(r, carry):
            x_grad(r, a2[r] * dv[r])
            return carry

        tiles(go)


    y_sum = rows[0:1] * y_sums[0] - rows[1:2] * y_sums[1]
    x_sum = dot(heads, uh[...], NT) + dot(heads, ul[...], NT)
    from_end = jnp.sum(
        jnp.where(own, jnp.sum(small[8:16], axis=0, keepdims=True), 0.0), axis=1, keepdims=True
    )
    onward = jnp.where(low, 1.0, 0.0).astype(BF)
    rate_grad = sum_thirds(dot(thirds(y_sum - x_sum).astype(BF), onward)) + from_end
    step_grad = (x_sum / step - speed * rate_grad) * (1.0 / (1.0 + jnp.exp(-pre)))
    sgv[...] = step_grad

    def as_row(column):
        hit = iota((H, D), 0) == iota((H, D), 1)
        return jnp.sum(jnp.where(hit, column, 0.0), axis=0, keepdims=True)

    skip_column = jnp.sum(
        jnp.where(own, jnp.sum(skip_sum, axis=0, keepdims=True), 0.0), axis=1, keepdims=True
    )
    small[0:1] = jnp.sum(gain_sum, axis=0, keepdims=True)
    small[1:2] = as_row(jnp.sum(rate_grad * rate, axis=1, keepdims=True))
    small[2:3] = as_row(jnp.sum(step_grad, axis=1, keepdims=True))
    small[3:4] = as_row(skip_column)
    small_out = remote(small.at[pl.ds(0, 8)], small.at[pl.ds(16, 8)], to_core)
    small_out.start()

    arrive([small_out] + c_sums[0] + c_sums[1])
    params[...] = small[0:8] + small[16:24]
    c_total = [
        c_parts[j, 0:W] + (recv_c[j, 0:W] + (recv_c[j, W:2 * W] + recv_c[j, 2 * W:3 * W]))
        for j in range(2)
    ]
    cgv[...] = rows[0:1] * c_total[0] - rows[1:2] * c_total[1]
    arrive(b_sums)
    bgv[...] = b_part[0:W] + (recv_b[0:W] + (recv_b[W:2 * W] + recv_b[2 * W:3 * W]))

    @pl.when(early)
    def _():
        for copy in state_out:
            copy.wait_send()

    @pl.when(late)
    def _():
        for copy in (ap_out, aq_out, c_out, rows_out):
            copy.wait_send()

    for copies in (*b_copies, *c_copies, *norm_out, *c_sums, b_sums, [small_out]):
        for copy in copies:
            copy.wait_send()


def place_results(*refs):
    results, outputs, sem = refs[:7], refs[7:17], refs[17]
    out_o, hg_o, zg_o, sg_o, bg_o, cg_o, decay_o, bias_o, skip_o, gain_o = outputs
    rows = results[6]
    copies = [
        pltpu.make_async_copy(rows.at[0] if ref is gain_o else results[k], ref, sem.at[k])
        for k, ref in enumerate((out_o, hg_o, zg_o, sg_o, bg_o, cg_o, gain_o))
    ]
    for copy in copies:
        copy.start()
    for k, ref in enumerate((decay_o, bias_o, skip_o)):
        ref[...] = rows[1 + k, 0:H]
    for copy in copies:
        copy.wait()


def shards(*args):
    def f32(*shape):
        return jax.ShapeDtypeStruct(shape, F32)

    def vm(*shape):
        return pltpu.VMEM(shape, F32)

    def vb(*shape):
        return pltpu.VMEM(shape, BF)

    in_hbm = pl.BlockSpec(memory_space=pltpu.HBM)
    in_vmem = pl.BlockSpec(memory_space=pltpu.VMEM)
    scalars = pltpu.SMEM((H,), F32)
    wide, narrow = vm(T, D), vb(T, D)
    square, thin = vm(T, T), vb(T, T)
    scratch = [wide] * 3 + [vm(H, T), vm(1, D)] + [scalars] * 3 + [square] * 3
    scratch += [wide] * 6
    scratch += [narrow] * 2 + [vb(Q, D)] * 2 + [narrow] * 10
    scratch += [thin] * 14 + [narrow] * 2 + [thin] * 2 + [narrow] * 2
    scratch += [vm(4, W, D)] * 2 + [narrow] * 2 + [wide] * 4 + [vm(8, T)] * 2
    scratch += [wide] * 4 + [thin] * 2 + [vm(2, 4, 8, Q), vm(T, 128)]
    scratch += [square] * 4 + [wide] + [narrow] * 2
    scratch += [wide] * 2 + [square, vm(2, N, T), vm(3 * W, T), vm(2, 3 * W, T), vm(32, D), square] + [thin] * 2
    scratch += [
        pltpu.SemaphoreType.DMA((10,)),
        pltpu.SemaphoreType.DMA((36,)),
        pltpu.SemaphoreType.DMA((36,)),
    ]
    args = [pltpu.with_memory_space_constraint(array, pltpu.HBM) for array in args]
    results = pl.pallas_call(
        body,
        out_shape=[f32(T, D), f32(T, D), f32(T, D), f32(H, T), f32(W, T), f32(W, T), f32(8, D)],
        in_specs=[in_hbm] * 10,
        out_specs=[in_vmem] * 7,
        scratch_shapes=scratch,
        compiler_params=pltpu.CompilerParams(
            collective_id=0, has_side_effects=True, vmem_limit_bytes=40 * 1024 * 1024
        ),
        name="layer",
    )(*args)
    return pl.pallas_call(
        place_results,
        out_shape=[
            f32(T, D), f32(T, D), f32(T, D), f32(H, T), f32(W, T), f32(W, T),
            f32(H), f32(H), f32(H), f32(D),
        ],
        in_specs=[in_vmem] * 7,
        out_specs=[in_hbm] * 6 + [in_vmem] * 3 + [in_hbm],
        scratch_shapes=[pltpu.SemaphoreType.DMA((7,))],
        compiler_params=pltpu.CompilerParams(vmem_limit_bytes=16 * 1024 * 1024),
        name="place_results",
    )(*results)


def solution(mesh):
    rows, cols = P("ctx", "dp"), P("dp", "ctx")
    heads = P("dp")
    return jax.shard_map(
        shards,
        mesh=mesh,
        in_specs=(rows, rows, cols, cols, cols, heads, heads, heads, heads, rows),
        out_specs=(rows, rows, rows, cols, cols, cols, heads, heads, heads, heads),
        check_vma=False,
    )
```

```python
import jax
import jax.numpy as jnp
from jax import lax
from jax.experimental import pallas as pl
from jax.experimental.pallas import tpu as pltpu
from jax.sharding import PartitionSpec as P

MESH = pl.DeviceIdType.MESH
F32 = jnp.float32
BF = jnp.bfloat16
T = 256
Q = 128
N = 256
D = 512
H = 8
W = 64
ROWS = 16
TILES = T // ROWS
GROUP_WIDTH = 2048
EPSILON = 1e-05

NN = (((1,), (0,)), ((), ()))
NT = (((1,), (1,)), ((), ()))


def halves(v):
    hi = v.astype(BF)
    return hi, (v - hi.astype(F32)).astype(BF)


def dot(a, b, dims=NN):
    return lax.dot_general(a, b, dims, preferred_element_type=F32)


def dot3(a, b, dims=NN):
    return dot(a[0], b[0], dims) + (dot(a[0], b[1], dims) + dot(a[1], b[0], dims))


def thirds(v):
    hi = v.astype(BF).astype(F32)
    mid = (v - hi).astype(BF).astype(F32)
    return jnp.concatenate([hi, mid, v - hi - mid, jnp.zeros_like(v)], axis=0)


def sum_thirds(v):
    return v[0:8] + (v[8:16] + v[16:24])


def lanes(v):
    return (v[:, 0:128] + v[:, 128:256]) + (v[:, 256:384] + v[:, 384:512])


def fold(v):
    return v[0:8] + v[8:16]


def tiles(step, count=TILES, init=None, first=0):
    def run(i, carry):
        return step(pl.ds(pl.multiple_of(first + i * ROWS, ROWS), ROWS), carry)

    return lax.fori_loop(0, count, run, 0 if init is None else init, unroll=True)


def iota(shape, dim):
    return lax.broadcasted_iota(jnp.int32, shape, dim)


def body(
    x_in, z_in, raw_in, b_in, c_in, decay_in, bias_in, skip_in, gain_in, og_in,
    outv, hgv, zgv, sgv, bgv, cgv, params,
    xv, zv, ogv, rawv, gainv, decay_s, bias_s, skip_s, bv, cv, c1v,
    a1, a2, a5, gate, dgate, ogg,
    vh, vl, kh, kl, wh, wl, ph, pld, qh, ql, eh, el, uh, ul,
    bh, bl, ch, cl, cth, ctl, bth, btl, c1h, c1l, gh, gl, gth, gtl, oh, ol, th, tl, fh, fl,
    state, other, sh, sl, ap, ap_in, aq, aq_in, rows, rows_in,
    yi, yv, gated, carry_v, sumh, suml, norm, cols, d1, d2, k1, k2, dy, yqh, yql,
    dv, dx, b_part, c_parts, recv_b, recv_c, small, crs, turnh, turnl,
    local_sem, send_sem, recv_sem,
):
    dp = lax.axis_index("dp")
    ctx = lax.axis_index("ctx")
    place = lax.rem(dp, 4)
    base = dp - place
    right = base + lax.rem(place + 1, 4)
    left = base + lax.rem(place + 3, 4)
    across = base + lax.rem(place + 2, 4)
    early = ctx == 0
    late = ctx == 1

    used = []

    def local(src, dst):
        copy = pltpu.make_async_copy(src, dst, local_sem.at[len(used)])
        used.append(copy)
        return copy

    sent = []

    def remote(src, dst, device):
        k = len(sent)
        sent.append(k)
        return pltpu.make_async_remote_copy(
            src_ref=src, dst_ref=dst, send_sem=send_sem.at[k], recv_sem=recv_sem.at[k],
            device_id=device, device_id_type=MESH,
        )

    to_right, to_left, to_across, to_core = (right, ctx), (left, ctx), (across, ctx), (dp, 1 - ctx)

    barrier = pltpu.get_barrier_semaphore()
    for device in (to_right, to_left, to_across, to_core):
        pl.semaphore_signal(barrier, inc=1, device_id=device, device_id_type=MESH)

    get_heads = [
        local(ref, row)
        for ref, row in ((decay_in, decay_s), (bias_in, bias_s), (skip_in, skip_s))
    ]
    get_raw = local(raw_in, rawv)
    get_gain = local(gain_in, gainv.at[0])
    get_x = local(x_in, xv)
    get_z = local(z_in, zv)
    get_og = local(og_in, ogv)
    get_b = local(b_in, bv.at[pl.ds(0, W)])
    get_c = local(c_in, cv.at[pl.ds(0, W)])
    for copy in used:
        copy.start()
    def per_head(ref, width):
        row = iota((H, width), 0)
        value = jnp.full((H, width), ref[0], F32)
        for h in range(1, H):
            value = jnp.where(row == h, ref[h], value)
        return value

    get_raw.wait()
    for copy in get_heads:
        copy.wait()
    speed = jnp.exp(per_head(decay_s, T))
    pre = rawv[...] + per_head(bias_s, T)
    step = jnp.maximum(pre, 0.0) + jnp.log1p(jnp.exp(-jnp.abs(pre)))
    rate = -speed * step
    src, dst = iota((T, T), 0), iota((T, T), 1)
    upto = jnp.where((src <= dst) & (src // Q == dst // Q), 1.0, 0.0).astype(BF)
    run = sum_thirds(dot(thirds(rate).astype(BF), upto))

    pl.semaphore_wait(barrier, 4)

    lo, hi = slice(0, Q), slice(Q, T)

    def gather(mine, group, j):
        part = pl.ds(j * Q, Q)
        return [
            remote(mine.at[:, part], group.at[pl.ds(k * W, W), part], device)
            for k, device in ((3, to_across), (1, to_right), (2, to_left))
        ]

    def begin(copies):
        for copy in copies:
            copy.start()

    def arrive(copies):
        for copy in copies:
            copy.wait_recv()

    b_copies = [gather(b_in, bv, j) for j in range(2)]
    c_copies = [gather(c_in, cv, j) for j in range(2)]
    begin(b_copies[0] + b_copies[1])

    total0 = run[:, Q - 1:Q]
    total1 = run[:, T - 1:T]
    position = iota((H, T), 1)
    block1 = position >= Q
    centre = 0.5 * jnp.where(block1, total1, total0)
    scale1 = jnp.exp(run - centre)
    scale2 = step * jnp.exp(centre - run)
    since_start = jnp.where(block1, run + total0, run)
    to_end = jnp.where(block1, total1 - run, total0 - run + total1)
    scale5 = jnp.where(early, step, 1.0) * jnp.exp(jnp.where(early, to_end, since_start))
    stacked = jnp.concatenate(
        [thirds(scale1), thirds(scale2), thirds(scale5), jnp.zeros((32, T), F32)], axis=0
    ).T.astype(BF)
    row, col = iota((128, D), 0), iota((128, D), 1)
    same = (row % 8 == col // W) & (row % 32 < 24)
    for k, ref in enumerate((a1, a2, a5)):
        spread = jnp.where(same & (row // 32 == k), 1.0, 0.0).astype(BF)
        ref[...] = dot(stacked, spread)
    begin(c_copies[0] + c_copies[1])

    own = iota((H, D), 0) == iota((H, D), 1) // W
    kappa = jnp.sum(
        jnp.where(own, jnp.exp(0.5 * (total0 + total1)), 0.0), axis=0, keepdims=True
    )
    skip_row = jnp.sum(jnp.where(own, per_head(skip_s, D), 0.0), axis=0, keepdims=True)

    get_gain.wait()
    get_x.wait()
    get_z.wait()
    get_og.wait()

    def prepare(r, carry):
        z = zv[r]
        sig = 1.0 / (1.0 + jnp.exp(-z))
        g = z * sig
        gate[r] = g
        dgate[r] = sig * (1.0 + z * (1.0 - sig))
        scaled = ogv[r] * gainv[...]
        ogg[r] = scaled
        x = xv[r]
        p = scaled * g
        vh[r], vl[r] = halves(a2[r] * x)
        ph[r], pld[r] = halves(a1[r] * p)
        w = a5[r] * jnp.where(early, x, p)
        ap[r] = w
        wh[r], wl[r] = halves(w)
        return carry

    tiles(prepare)

    ap_out = remote(ap, ap_in, to_core)

    @pl.when(late)
    def _():
        ap_out.start()

    def prepare0(r, carry):
        kh[r], kl[r] = halves((a2[r] * xv[r]) * kappa)
        return carry

    tiles(prepare0, TILES // 2)

    def score_grad(out, far, near):
        out[0:Q, 0:Q] = dot3((vh[0:Q], vl[0:Q]), (far[0:Q], near[0:Q]), NT)
        out[0:Q, Q:T] = dot3((kh[...], kl[...]), (far[Q:T], near[Q:T]), NT)
        out[Q:T, Q:T] = dot3((vh[Q:T], vl[Q:T]), (far[Q:T], near[Q:T]), NT)

    score_grad(d1, ph, pld)

    low = src >= dst
    high = src <= dst
    get_b.wait()
    get_c.wait()
    arrive(b_copies[0] + b_copies[1])
    bh[...], bl[...] = halves(bv[...])

    state_out = [remote(state.at[k], other.at[k], to_core) for k in range(4)]

    @pl.when(early)
    def _():
        for k in range(4):
            part = slice(k * W, (k + 1) * W)
            state[k] = dot3((bh[part], bl[part]), (wh[...], wl[...]))
            state_out[k].start()

    arrive(c_copies[0])
    cth[lo], ctl[lo] = halves(cv[:, lo].T)
    g0 = dot3((cth[lo], ctl[lo]), (bh[:, lo], bl[:, lo]))
    gh[lo, lo], gl[lo, lo] = halves(jnp.where(low[lo, lo], g0, 0.0))
    for k in range(2):
        part = pl.ds(k * 256, 256)
        yi[lo, part] = dot3((gh[lo, lo], gl[lo, lo]), (vh[lo, part], vl[lo, part]))

    def mix(r, y):
        yv[r] = y
        mixed = y + skip_row * xv[r]
        g = mixed * gate[r]
        gated[r] = g
        sumh[r, 0:128], suml[r, 0:128] = halves(lanes(g * g))
        sumh[r, 128:256], suml[r, 128:256] = halves(lanes(g * ogg[r]))
        q = g * gate[r]
        qh[r], ql[r] = halves(a1[r] * q)
        return q

    pick = jnp.where(iota((H, 256), 0) == iota((H, 256), 1) // 128, 1.0, 0.0).astype(BF)
    norm_out = [
        [
            remote(norm.at[j, 0], norm.at[j, 1 + k], device)
            for k, device in enumerate((to_across, to_right, to_left))
        ]
        for j in range(2)
    ]

    def send_sums(j, block):
        norm[j, 0] = dot(pick, sumh[block], NT) + dot(pick, suml[block], NT)
        begin(norm_out[j])

    def mix_early(j, block):
        def go(r, carry):
            mix(r, a1[r] * yi[r])
            return carry

        tiles(go, TILES // 2, first=j * Q)
        send_sums(j, block)

    @pl.when(early)
    def _():
        mix_early(0, lo)

    def scatter(parts, landing):
        return [
            remote(parts.at[pl.ds(k * W, W)], landing.at[pl.ds(j * W, W)], device)
            for j, (k, device) in enumerate(((3, to_across), (2, to_right), (1, to_left)))
        ]

    b_sums = scatter(b_part, recv_b)
    c_sums = [scatter(c_parts.at[j], recv_c.at[j]) for j in range(2)]

    def c_grad(j, grad):
        th[...], tl[...] = halves(jnp.where(high, grad[...], 0.0))
        return dot3((bh[...], bl[...]), (th[...], tl[...]))

    c_parts[0] = c_grad(0, d1)
    arrive(c_copies[1])

    @pl.when(early)
    def _():
        begin(c_sums[0])

    cth[hi], ctl[hi] = halves(cv[:, hi].T)
    c_out = remote(cv, c1v, to_core)

    @pl.when(late)
    def _():
        c_out.start()

    g1 = dot3((cth[hi], ctl[hi]), (bh[...], bl[...]))
    gh[hi], gl[hi] = halves(jnp.where(low[hi], g1, 0.0))
    for k in range(2):
        part = pl.ds(k * 256, 256)
        yi[hi, part] = dot3(
            (gh[hi], gl[hi]),
            (
                jnp.concatenate([kh[:, part], vh[hi, part]], axis=0),
                jnp.concatenate([kl[:, part], vl[hi, part]], axis=0),
            ),
        )

    aq_out = remote(aq, aq_in, to_core)

    @pl.when(early)
    def _():
        mix_early(1, hi)

    @pl.when(late)
    def _():
        arrive(state_out)
        for k in range(4):
            sh[k * W:(k + 1) * W], sl[k * W:(k + 1) * W] = halves(other[k])
        for k in range(2):
            part = pl.ds(k * 256, 256)
            carry_v[:, part] = dot3((cth[...], ctl[...]), (sh[:, part], sl[:, part]))

        def go(r, carry):
            w = a5[r] * mix(r, a1[r] * yi[r] + a5[r] * carry_v[r])
            aq[r] = w
            eh[r], el[r] = halves(w)
            return carry

        tiles(go, TILES // 2)
        send_sums(0, lo)
        tiles(go, TILES // 2, first=Q)
        send_sums(1, hi)
        aq_out.start()
        c_parts[0] += dot3((sh[...], sl[...]), (wh[...], wl[...]), NT)
        begin(c_sums[0])

    score_grad(d2, qh, ql)

    @pl.when(early)
    def _():
        c_parts[1] = c_grad(1, d2)
        begin(c_sums[1])
        ap_out.wait_recv()
        fh[...], fl[...] = halves(ap_in[...])
        k1[...] = dot3((wh[...], wl[...]), (fh[...], fl[...]), NT)
        bth[...], btl[...] = halves(bv[...].T)
        c_out.wait_recv()
        c1h[...], c1l[...] = halves(c1v[...])
        crs[...] = dot3((bth[...], btl[...]), (c1h[...], c1l[...]))
        aq_out.wait_recv()
        oh[...], ol[...] = halves(aq_in[...])
        k2[...] = dot3((wh[...], wl[...]), (oh[...], ol[...]), NT)

    @pl.when(late)
    def _():
        c_parts[1] = c_grad(1, d2) + dot3((sh[...], sl[...]), (eh[...], el[...]), NT)
        begin(c_sums[1])

    ch[...], cl[...] = halves(cv[...])
    heads = jnp.where(own, 1.0, 0.0).astype(BF)

    def weigh(r, carry):
        gy = gate[r] * yv[r]
        uh[r], ul[r] = halves(ogg[r] * gy)
        yqh[r], yql[r] = halves(gated[r] * gy)
        return carry

    tiles(weigh)
    y_sums = [
        dot(heads, high_part[...], NT) + dot(heads, low_part[...], NT)
        for high_part, low_part in ((uh, ul), (yqh, yql))
    ]
    for rows_of, cols_of in ((lo, lo), (hi, lo), (hi, hi)):
        turnh[cols_of, rows_of] = gh[rows_of, cols_of].astype(F32).T.astype(BF)
        turnl[cols_of, rows_of] = gl[rows_of, cols_of].astype(F32).T.astype(BF)

    def factors(j, block):
        arrive(norm_out[j])
        sums = (norm[j, 0] + norm[j, 1]) + (norm[j, 2] + norm[j, 3])
        inv = lax.rsqrt(sums[0:1] * (1.0 / GROUP_WIDTH) + EPSILON)
        slope = inv * inv * inv * sums[1:2] * (1.0 / GROUP_WIDTH)
        rows[:, block] = jnp.where(iota((8, Q), 0) == 0, inv, slope)

    for j, block in enumerate((lo, hi)):
        factors(j, block)
    rows_out = remote(rows, rows_in, to_core)

    @pl.when(late)
    def _():
        rows_out.start()

    th[...], tl[...] = halves(jnp.where(high, rows[0:1] * d1[...] - rows[1:2] * d2[...], 0.0))
    b_grad = dot3((ch[...], cl[...]), (th[...], tl[...]), NT)

    @pl.when(late)
    def _():
        b_part[...] = b_grad
        begin(b_sums)

    @pl.when(early)
    def _():
        rows_out.wait_recv()
        gth[...], gtl[...] = halves(rows_in[0:1] * k1[...] - rows_in[1:2] * k2[...])
        b_part[...] = b_grad + dot3((c1h[...], c1l[...]), (gth[...], gtl[...]), NT)
        begin(b_sums)

    lead = iota((128, T), 0)
    cols[...] = jnp.where(lead == 0, rows[0:1], jnp.where(lead == 1, rows[1:2], 0.0)).T

    def finish(r, carry):
        gain_sum, skip_sum = carry
        inv = cols[r, 0:1]
        k = cols[r, 1:2]
        g = gated[r]
        x = xv[r]
        y = yv[r]
        normed = g * inv
        outv[r] = normed * gainv[...]
        grad = ogg[r] * inv - g * k
        zgv[r] = grad * (y + skip_row * x) * dgate[r]
        d = grad * gate[r]
        dy[r] = d
        uh[r], ul[r] = halves(a1[r] * d)
        return gain_sum + fold(ogv[r] * normed), skip_sum + fold(d * x)

    zero = jnp.zeros((8, D), F32)
    gain_sum, skip_sum = tiles(finish, init=(zero, zero))

    for k in range(2):
        part = pl.ds(k * 256, 256)
        dv[0:Q, part] = dot3((turnh[lo, lo], turnl[lo, lo]), (uh[0:Q, part], ul[0:Q, part])) + kappa[
            :, k * 256:(k + 1) * 256
        ] * dot3((turnh[lo, hi], turnl[lo, hi]), (uh[Q:T, part], ul[Q:T, part]))
        dv[Q:T, part] = dot3((turnh[hi, hi], turnl[hi, hi]), (uh[Q:T, part], ul[Q:T, part]))

    small[0:16] = jnp.zeros((16, D), F32)

    def x_grad(r, f):
        hgv[r] = f + skip_row * dy[r]
        uh[r], ul[r] = halves(f * xv[r])

    @pl.when(early)
    def _():
        scaled = [halves(crs[...] * rows_in[0:1]), halves(crs[...] * -rows_in[1:2])]
        cross = [jnp.concatenate([scaled[0][k], scaled[1][k]], axis=1) for k in range(2)]
        for k in range(2):
            part = pl.ds(k * 256, 256)
            dx[:, part] = dot3(
                cross,
                (
                    jnp.concatenate([fh[:, part], oh[:, part]], axis=0),
                    jnp.concatenate([fl[:, part], ol[:, part]], axis=0),
                ),
            )

        def go(r, carry):
            tail = a5[r] * dx[r]
            x_grad(r, a2[r] * dv[r] + tail)
            return carry + fold(tail * xv[r])

        small[8:16] = tiles(go, init=zero)

    @pl.when(late)
    def _():
        def go(r, carry):
            x_grad(r, a2[r] * dv[r])
            return carry

        tiles(go)


    y_sum = rows[0:1] * y_sums[0] - rows[1:2] * y_sums[1]
    x_sum = dot(heads, uh[...], NT) + dot(heads, ul[...], NT)
    from_end = jnp.sum(
        jnp.where(own, jnp.sum(small[8:16], axis=0, keepdims=True), 0.0), axis=1, keepdims=True
    )
    onward = jnp.where(low, 1.0, 0.0).astype(BF)
    rate_grad = sum_thirds(dot(thirds(y_sum - x_sum).astype(BF), onward)) + from_end
    step_grad = (x_sum / step - speed * rate_grad) * (1.0 / (1.0 + jnp.exp(-pre)))
    sgv[...] = step_grad

    def as_row(column):
        hit = iota((H, D), 0) == iota((H, D), 1)
        return jnp.sum(jnp.where(hit, column, 0.0), axis=0, keepdims=True)

    skip_column = jnp.sum(
        jnp.where(own, jnp.sum(skip_sum, axis=0, keepdims=True), 0.0), axis=1, keepdims=True
    )
    small[0:1] = jnp.sum(gain_sum, axis=0, keepdims=True)
    small[1:2] = as_row(jnp.sum(rate_grad * rate, axis=1, keepdims=True))
    small[2:3] = as_row(jnp.sum(step_grad, axis=1, keepdims=True))
    small[3:4] = as_row(skip_column)
    small_out = remote(small.at[pl.ds(0, 8)], small.at[pl.ds(16, 8)], to_core)
    small_out.start()

    arrive([small_out] + c_sums[0] + c_sums[1])
    params[...] = small[0:8] + small[16:24]
    c_total = [
        c_parts[j, 0:W] + (recv_c[j, 0:W] + (recv_c[j, W:2 * W] + recv_c[j, 2 * W:3 * W]))
        for j in range(2)
    ]
    cgv[...] = rows[0:1] * c_total[0] - rows[1:2] * c_total[1]
    arrive(b_sums)
    bgv[...] = b_part[0:W] + (recv_b[0:W] + (recv_b[W:2 * W] + recv_b[2 * W:3 * W]))

    @pl.when(early)
    def _():
        for copy in state_out:
            copy.wait_send()

    @pl.when(late)
    def _():
        for copy in (ap_out, aq_out, c_out, rows_out):
            copy.wait_send()

    for copies in (*b_copies, *c_copies, *norm_out, *c_sums, b_sums, [small_out]):
        for copy in copies:
            copy.wait_send()


def place_results(*refs):
    results, outputs, sem = refs[:7], refs[7:17], refs[17]
    out_o, hg_o, zg_o, sg_o, bg_o, cg_o, decay_o, bias_o, skip_o, gain_o = outputs
    rows = results[6]
    copies = [
        pltpu.make_async_copy(rows.at[0] if ref is gain_o else results[k], ref, sem.at[k])
        for k, ref in enumerate((out_o, hg_o, zg_o, sg_o, bg_o, cg_o, gain_o))
    ]
    for copy in copies:
        copy.start()
    for k, ref in enumerate((decay_o, bias_o, skip_o)):
        ref[...] = rows[1 + k, 0:H]
    for copy in copies:
        copy.wait()


def shards(*args):
    def f32(*shape):
        return jax.ShapeDtypeStruct(shape, F32)

    def vm(*shape):
        return pltpu.VMEM(shape, F32)

    def vb(*shape):
        return pltpu.VMEM(shape, BF)

    in_hbm = pl.BlockSpec(memory_space=pltpu.HBM)
    in_vmem = pl.BlockSpec(memory_space=pltpu.VMEM)
    scalars = pltpu.SMEM((H,), F32)
    wide, narrow = vm(T, D), vb(T, D)
    square, thin = vm(T, T), vb(T, T)
    scratch = [wide] * 3 + [vm(H, T), vm(1, D)] + [scalars] * 3 + [square] * 3
    scratch += [wide] * 6
    scratch += [narrow] * 2 + [vb(Q, D)] * 2 + [narrow] * 10
    scratch += [thin] * 14 + [narrow] * 2 + [thin] * 2 + [narrow] * 2
    scratch += [vm(4, W, D)] * 2 + [narrow] * 2 + [wide] * 4 + [vm(8, T)] * 2
    scratch += [wide] * 4 + [thin] * 2 + [vm(2, 4, 8, Q), vm(T, 128)]
    scratch += [square] * 4 + [wide] + [narrow] * 2
    scratch += [wide] * 2 + [square, vm(2, N, T), vm(3 * W, T), vm(2, 3 * W, T), vm(32, D), square] + [thin] * 2
    scratch += [
        pltpu.SemaphoreType.DMA((10,)),
        pltpu.SemaphoreType.DMA((36,)),
        pltpu.SemaphoreType.DMA((36,)),
    ]
    args = [pltpu.with_memory_space_constraint(array, pltpu.HBM) for array in args]
    results = pl.pallas_call(
        body,
        out_shape=[f32(T, D), f32(T, D), f32(T, D), f32(H, T), f32(W, T), f32(W, T), f32(8, D)],
        in_specs=[in_hbm] * 10,
        out_specs=[in_vmem] * 7,
        scratch_shapes=scratch,
        compiler_params=pltpu.CompilerParams(
            collective_id=0, has_side_effects=True, vmem_limit_bytes=40 * 1024 * 1024
        ),
        name="layer",
    )(*args)
    return pl.pallas_call(
        place_results,
        out_shape=[
            f32(T, D), f32(T, D), f32(T, D), f32(H, T), f32(W, T), f32(W, T),
            f32(H), f32(H), f32(H), f32(D),
        ],
        in_specs=[in_vmem] * 7,
        out_specs=[in_hbm] * 6 + [in_vmem] * 3 + [in_hbm],
        scratch_shapes=[pltpu.SemaphoreType.DMA((7,))],
        compiler_params=pltpu.CompilerParams(vmem_limit_bytes=16 * 1024 * 1024),
        name="place_results",
    )(*results)


def solution(mesh):
    rows, cols = P("ctx", "dp"), P("dp", "ctx")
    heads = P("dp")
    return jax.shard_map(
        shards,
        mesh=mesh,
        in_specs=(rows, rows, cols, cols, cols, heads, heads, heads, heads, rows),
        out_specs=(rows, rows, rows, cols, cols, cols, heads, heads, heads, heads),
        check_vma=False,
    )
```
